32 devices in a mesh: dp: 16 (over z, x, core), pair: 2 (over y).
Axes of the slice: x: 2, y: 2, z: 4, core: 2. Of those that a mesh axis runs over, the one named last changes fastest.
Arguments:
- tokens: bfloat16 [3072, 1792], P('dp'), may hold values from -6 to 6
- grad_out: bfloat16 [3072, 1792], P('dp'), may hold values from -6 to 6
- gate_probs: bfloat16 [3072, 2], P('dp'), may hold values from 0.049804688 to 1
- expert_ids: int32 [3072, 2], P('dp'), may hold values from 0 to 8, as said below
- route_slots: int32 [3072, 2], P('dp'), may hold values from 0 to 191, as said below
- hot_flags: int32 [9], replicated, may hold values from 0 to 1, as said below
- owner_slot: int32 [9], replicated, may hold values from 0 to 7, as said below
- cold_gate: bfloat16 [16, 640, 1792], P('dp', 'pair'), may hold values from -0.125 to 0.125
- cold_up: bfloat16 [16, 640, 1792], P('dp', 'pair'), may hold values from -0.125 to 0.125
- cold_down: bfloat16 [16, 640, 1792], P('dp', 'pair'), may hold values from -0.15625 to 0.15625
- hot_gate: bfloat16 [1280, 1792], P(('dp', 'pair')), may hold values from -0.125 to 0.125
- hot_up: bfloat16 [1280, 1792], P(('dp', 'pair')), may hold values from -0.125 to 0.125
- hot_down: bfloat16 [1280, 1792], P(('dp', 'pair')), may hold values from -0.15625 to 0.15625
Outputs:
- grad_tokens: bfloat16 [3072, 1792], P(('dp', 'pair'))
- grad_probs: float32 [3072, 2], P(('dp', 'pair'))
- grad_cold_gate: bfloat16 [16, 640, 1792], P('dp', 'pair')
- grad_cold_up: bfloat16 [16, 640, 1792], P('dp', 'pair')
- grad_cold_down: bfloat16 [16, 640, 1792], P('dp', 'pair')
- grad_hot_gate: bfloat16 [1280, 1792], P(('dp', 'pair'))
- grad_hot_up: bfloat16 [1280, 1792], P(('dp', 'pair'))
- grad_hot_down: bfloat16 [1280, 1792], P(('dp', 'pair'))
The draws below stay inside these ranges and needn't reach their ends.
Inputs may be any that keep to these rules, and one draw needn't show every extreme that they name: `expert_ids`: each token names 2 different experts; on every device at least 48 tokens name the hot expert, on some device all of them do, and some cold expert is named by 4 or more tokens. `route_slots`: on one device the routes to one expert carry the slots 0, 1, 2 and so on, each once. `hot_flags`: exactly one entry is 1. `owner_slot`: the cold experts hold the slots 0 to 7, each once; the hot expert's entry is 0.
All inputs are finite; a program needn't handle non-finite values.
Results may differ from the reference program's by a relative error of at most 0.0049.
Values may be sent and summed in bfloat16 or wider, within the bound.
No kernel may reach another device: no remote copies, remote signals or barrier semaphores. Data moves between devices by JAX's collectives and lax.ppermute only.
A program may use at most 192 MiB of HBM per device.

```python
import jax
import jax.numpy as jnp
from jax import lax

D = 1792
FF = 1280
TOP = 2
TOK_DEV = 192
CAP = 4
HCAP = 48
COLD = 8
EXPERTS = 9
TOKENS = 3072
N_DP = 16


def shuffle_rows(key, length):
    return jax.random.permutation(key, length).astype(jnp.int32)


def rank_block(block_ids, block_prio):
    same = block_ids[:, None] == block_ids[None, :]
    earlier = block_prio[None, :] < block_prio[:, None]
    return jnp.sum(same & earlier, axis=1).astype(jnp.int32)


def routing(key):
    base = jax.random.fold_in(key, 4242)
    keys = jax.random.split(base, 7)
    order = jax.random.permutation(keys[0], EXPERTS).astype(jnp.int32)
    hot_id = order[0]
    busy_id = order[1]
    places = jnp.arange(EXPERTS, dtype=jnp.int32)
    ranks = jnp.zeros((EXPERTS,), jnp.int32).at[order].set(places)
    flags = (ranks == 0).astype(jnp.int32)
    cold_perm = jax.random.permutation(keys[1], COLD).astype(jnp.int32)
    owner = jnp.where(ranks == 0, 0, cold_perm[jnp.maximum(ranks - 1, 0)]).astype(jnp.int32)
    popular = jnp.where(ranks == 0, 0, 64 + 56 // jnp.maximum(ranks, 1)).astype(jnp.int32)
    device_keys = jax.random.split(keys[2], N_DP)
    position = jax.vmap(shuffle_rows, in_axes=(0, None))(device_keys, TOK_DEV).reshape(TOKENS)
    token_device = (jnp.arange(TOKENS, dtype=jnp.int32) // TOK_DEV).astype(jnp.int32)
    extra = jax.random.randint(keys[3], (TOKENS,), 0, 4) == 0
    hot_token = (position < HCAP) | extra | (token_device == 0)
    busy_token = position >= TOK_DEV - CAP
    raw_scores = jax.random.randint(keys[4], (TOKENS, EXPERTS), 0, 1024)
    scores = raw_scores * popular[None, :] * EXPERTS + places[None, :]
    scores = jnp.where(ranks[None, :] == 0, -1, scores)
    scores = jnp.where(busy_token[:, None] & (places[None, :] == busy_id), 1 << 30, scores)
    best = lax.top_k(scores, 2)[1].astype(jnp.int32)
    first = jnp.where(hot_token, hot_id, best[:, 0])
    second = jnp.where(hot_token, best[:, 0], best[:, 1])
    swapped = jax.random.randint(keys[5], (TOKENS,), 0, 2) == 1
    ids = jnp.stack([jnp.where(swapped, second, first), jnp.where(swapped, first, second)], axis=1).astype(jnp.int32)
    prio_keys = jax.random.split(keys[6], N_DP)
    priority = jax.vmap(shuffle_rows, in_axes=(0, None))(prio_keys, TOK_DEV * TOP)
    slots = jax.vmap(rank_block)(ids.reshape(N_DP, TOK_DEV * TOP), priority).reshape(TOKENS, TOP)
    return (ids, slots, flags, owner)


def draw_expert_ids(key, part):
    return routing(key)[0]


def draw_route_slots(key, part):
    return routing(key)[1]


def draw_hot_flags(key, part):
    return routing(key)[2]


def draw_owner_slot(key, part):
    return routing(key)[3]


def block_scale(own_key, extent, shards, low, top_value):
    level, own = 1.0, jax.random.fold_in(own_key, 6)
    for dim, parts in shards:
        draws = jnp.exp(jax.random.uniform(jax.random.fold_in(own, dim), (parts,), jnp.float32, low / len(shards), top_value / len(shards)))
        level = level * jnp.repeat(draws, extent[dim] // parts).reshape([-1 if axis == dim else 1 for axis in range(len(extent))])
    return level


def noise(rng, dims, width, bound, cuts=(), held_as=jnp.bfloat16):
    drawn = width * jax.random.normal(rng, dims, jnp.float32)
    if cuts:
        drawn = drawn * block_scale(rng, dims, cuts, -0.22, 0.18)
    return jnp.clip(drawn, -bound, bound).astype(held_as)


def setup_inputs(seed: int = 0) -> dict:
    splits = jax.random.split(jax.random.key(seed), 14)
    tokens = noise(splits[0], (TOKENS, D), 1.0, 6.0, ((0, 16),))
    grad_out = noise(splits[1], (TOKENS, D), 1.0, 6.0, ((0, 16),))
    gate_probs = jnp.clip(0.049804688 + 0.9501953 * jax.random.uniform(splits[2], (TOKENS, TOP), jnp.float32) ** block_scale(splits[2], (TOKENS, TOP), ((0, 16),), -0.2, 0.2), 0.049804688, 1.0).astype(jnp.bfloat16)
    expert_ids = draw_expert_ids(jax.random.fold_in(splits[13], 71), 0)
    route_slots = draw_route_slots(jax.random.fold_in(splits[13], 71), 0)
    hot_flags = draw_hot_flags(jax.random.fold_in(splits[13], 71), 0)
    owner_slot = draw_owner_slot(jax.random.fold_in(splits[13], 71), 0)
    cold_gate = noise(splits[7], (2 * COLD, FF // 2, D), D ** -0.5, 0.125, ((0, 16), (1, 2)))
    cold_up = noise(splits[8], (2 * COLD, FF // 2, D), D ** -0.5, 0.125, ((0, 16), (1, 2)))
    cold_down = noise(splits[9], (2 * COLD, FF // 2, D), FF ** -0.5, 0.15625, ((0, 16), (1, 2)))
    hot_gate = noise(splits[10], (FF, D), D ** -0.5, 0.125, ((0, 32),))
    hot_up = noise(splits[11], (FF, D), D ** -0.5, 0.125, ((0, 32),))
    hot_down = noise(splits[12], (FF, D), FF ** -0.5, 0.15625, ((0, 32),))
    return {"tokens": tokens, "grad_out": grad_out, "gate_probs": gate_probs, "expert_ids": expert_ids, "route_slots": route_slots, "hot_flags": hot_flags, "owner_slot": owner_slot, "cold_gate": cold_gate, "cold_up": cold_up, "cold_down": cold_down, "hot_gate": hot_gate, "hot_up": hot_up, "hot_down": hot_down}


def expert_back(rows_in, rows_grad, rows_gate, w_gate, w_up, w_down):
    pre_gate = jnp.dot(rows_in, w_gate.T, preferred_element_type=jnp.float32)
    pre_up = jnp.dot(rows_in, w_up.T, preferred_element_type=jnp.float32)
    back_proj = jnp.dot(rows_grad, w_down.T, preferred_element_type=jnp.float32)
    sigmoid_gate = 1.0 / (1.0 + jnp.exp(-pre_gate))
    activation = pre_gate * sigmoid_gate
    hidden = activation * pre_up
    prob_grad = jnp.sum(hidden * back_proj, axis=1)
    gate_scale = rows_gate.astype(jnp.float32)[:, None]
    hidden_grad = gate_scale * back_proj
    gate_grad = (hidden_grad * pre_up * sigmoid_gate * (1.0 + pre_gate * (1.0 - sigmoid_gate))).astype(jnp.bfloat16)
    up_grad = (hidden_grad * activation).astype(jnp.bfloat16)
    weighted = (gate_scale * hidden).astype(jnp.bfloat16)
    input_grad = jnp.dot(gate_grad, w_gate, preferred_element_type=jnp.float32) + jnp.dot(up_grad, w_up, preferred_element_type=jnp.float32)
    return gate_grad, up_grad, weighted, input_grad, prob_grad


def pick_rows(route_table, tokens, grad_out, flat_gate):
    token_index = (route_table // TOP).astype(jnp.int32)
    rows_in = jnp.take(tokens, token_index, axis=0, mode="fill", fill_value=0)
    rows_grad = jnp.take(grad_out, token_index, axis=0, mode="fill", fill_value=0)
    rows_gate = jnp.take(flat_gate, route_table, axis=0, mode="fill", fill_value=0)
    return token_index, rows_in, rows_grad, rows_gate


def weight_grads(gate_grad, up_grad, weighted, rows_in, rows_grad):
    grad_gate = jnp.dot(gate_grad.T, rows_in, preferred_element_type=jnp.float32).astype(jnp.bfloat16)
    grad_up = jnp.dot(up_grad.T, rows_in, preferred_element_type=jnp.float32).astype(jnp.bfloat16)
    grad_down = jnp.dot(weighted.T, rows_grad, preferred_element_type=jnp.float32).astype(jnp.bfloat16)
    return grad_gate, grad_up, grad_down


def reference(tokens, grad_out, gate_probs, expert_ids, route_slots, hot_flags, owner_slot, cold_gate, cold_up, cold_down, hot_gate, hot_up, hot_down):
    route_count = TOKENS * TOP
    flat_ids = expert_ids.reshape(-1)
    flat_slots = route_slots.reshape(-1)
    flat_gate = gate_probs.reshape(-1)
    routes = jnp.arange(route_count, dtype=jnp.int32)
    device = (routes // (TOK_DEV * TOP)).astype(jnp.int32)
    is_hot = hot_flags[flat_ids]
    owners = owner_slot[flat_ids]
    live_cold = (is_hot == 0) & (flat_slots < CAP)
    live_hot = (is_hot == 1) & (flat_slots < HCAP)
    cold_pos = jnp.where(live_cold, (owners * N_DP + device) * CAP + flat_slots, COLD * N_DP * CAP).astype(jnp.int32)
    cold_table = jnp.full((COLD * N_DP * CAP,), route_count, jnp.int32).at[cold_pos].set(routes, mode="drop")
    cold_table = cold_table.reshape(COLD, N_DP * CAP)
    hot_pos = jnp.where(live_hot, device * HCAP + flat_slots, N_DP * HCAP).astype(jnp.int32)
    hot_table = jnp.full((N_DP * HCAP,), route_count, jnp.int32).at[hot_pos].set(routes, mode="drop")

    def one_slot(slot_index):
        route_table = cold_table[slot_index]
        token_index, rows_in, rows_grad, rows_gate = pick_rows(route_table, tokens, grad_out, flat_gate)
        start_row = (2 * slot_index).astype(jnp.int32)
        w_gate = lax.dynamic_slice_in_dim(cold_gate, start_row, 2, 0).reshape(FF, D)
        w_up = lax.dynamic_slice_in_dim(cold_up, start_row, 2, 0).reshape(FF, D)
        w_down = lax.dynamic_slice_in_dim(cold_down, start_row, 2, 0).reshape(FF, D)
        gate_grad, up_grad, weighted, input_grad, prob_grad = expert_back(rows_in, rows_grad, rows_gate, w_gate, w_up, w_down)
        grad_gate, grad_up, grad_down = weight_grads(gate_grad, up_grad, weighted, rows_in, rows_grad)
        return input_grad, prob_grad, grad_gate.reshape(2, FF // 2, D), grad_up.reshape(2, FF // 2, D), grad_down.reshape(2, FF // 2, D)

    cold_dx, cold_dp, cold_gg, cold_gu, cold_gd = lax.map(one_slot, jnp.arange(COLD, dtype=jnp.int32))

    hot_tokens, hot_in, hot_grad, hot_rows_gate = pick_rows(hot_table, tokens, grad_out, flat_gate)
    gate_grad, up_grad, weighted, hot_dx, hot_dp = expert_back(hot_in, hot_grad, hot_rows_gate, hot_gate, hot_up, hot_down)
    grad_hot_gate, grad_hot_up, grad_hot_down = weight_grads(gate_grad, up_grad, weighted, hot_in, hot_grad)

    flat_cold = cold_table.reshape(-1)
    cold_tokens = (flat_cold // TOP).astype(jnp.int32)
    input_total = jnp.zeros((TOKENS, D), jnp.float32)
    input_total = input_total.at[cold_tokens].add(cold_dx.reshape(-1, D), mode="drop")
    input_total = input_total.at[hot_tokens].add(hot_dx, mode="drop")
    route_grad = jnp.zeros((route_count,), jnp.float32)
    route_grad = route_grad.at[flat_cold].add(cold_dp.reshape(-1), mode="drop")
    route_grad = route_grad.at[hot_table].add(hot_dp, mode="drop")
    return (input_total.astype(jnp.bfloat16), route_grad.reshape(TOKENS, TOP),
            cold_gg.reshape(2 * COLD, FF // 2, D), cold_gu.reshape(2 * COLD, FF // 2, D), cold_gd.reshape(2 * COLD, FF // 2, D),
            grad_hot_gate, grad_hot_up, grad_hot_down)
```

```python
import functools

import jax
import jax.numpy as jnp
from jax import lax
from jax.experimental import pallas as pl
from jax.experimental.pallas import tpu as pltpu
from jax.sharding import PartitionSpec as P

TOP = 2
CAP = 4
HCAP = 48
HALF = HCAP // 2
TAIL = 128
CHUNK_BLOCK = 8
COLD_BLOCK = 128
BF = jnp.bfloat16
F32 = jnp.float32
VMEM_LIMIT = 56 * 1024 * 1024

NT = (((1,), (1,)), ((), ()))
TN = (((0,), (0,)), ((), ()))


def dot(a, b, dims=(((1,), (0,)), ((), ()))):
    return lax.dot_general(a, b, dims, preferred_element_type=F32)


def iota(shape, dim):
    return lax.broadcasted_iota(jnp.int32, shape, dim)


def positions(ids, slots, flags_ref, owner_ref, base):
    hot = jnp.zeros_like(ids)
    own = jnp.zeros_like(ids)
    for e in range(flags_ref.shape[0]):
        named = ids == e
        hot = jnp.where(named, flags_ref[e], hot)
        own = jnp.where(named, owner_ref[e], own)
    cold_pos = jnp.where(slots < CAP, own * CAP + slots, -1)
    hot_pos = jnp.where(slots < HCAP, base + slots, -1)
    return jnp.where(hot == 1, hot_pos, cold_pos)


def tail_lanes(first, second=None):
    lane = iota((first.shape[0], TAIL), 1)
    out = jnp.where(lane == 0, first, 0.0)
    if second is not None:
        out = jnp.where(lane == 1, second, out)
    return out


def split_tail(value):
    high = value.astype(BF).astype(F32)
    return tail_lanes(high, value - high)


def each_block(total, size, body):
    if total == size:
        body(0)
    else:

        def step(block, carry):
            body(pl.multiple_of(block * size, size))
            return carry

        lax.fori_loop(0, total // size, step, 0)


def add_to(ref, value, single):
    if single:
        ref[...] = value.astype(ref.dtype)
    else:
        ref[...] += value


def dispatch_kernel(
    base, tok_ref, grad_ref, prob_ref, ids_ref, slot_ref, flags_ref, owner_ref, hot_ref, cold_ref
):
    pair = lax.axis_index("pair")
    pos = positions(ids_ref[...], slot_ref[...], flags_ref, owner_ref, base)
    prob = prob_ref[...].astype(F32)
    width = tok_ref.shape[1]

    def fill(out_ref, start, target, is_grad):
        at = pl.ds(start, target.shape[0])
        first = pos[0:1, :] == target
        second = pos[1:2, :] == target
        chosen = jnp.where(first | second, 1.0, 0.0)
        rows = dot(jnp.where(is_grad, 0.0, chosen).astype(BF), tok_ref[...]) + dot(
            jnp.where(is_grad, chosen, 0.0).astype(BF), grad_ref[...]
        )
        out_ref[at, :width] = rows.astype(BF)
        weight = jnp.where(first, prob[0:1, :], 0.0) + jnp.where(second, prob[1:2, :], 0.0)
        weight = jnp.sum(jnp.where(is_grad, 0.0, weight), axis=1, keepdims=True)
        out_ref[at, width:] = tail_lanes(weight).astype(BF)

    tokens = tok_ref.shape[0]
    row = iota((HCAP, tokens), 0)
    fill(hot_ref, 0, base + HALF * pair + jnp.where(row >= HALF, row - HALF, row), row >= HALF)

    def cold_block(start):
        row = start + iota((COLD_BLOCK, tokens), 0)
        fill(cold_ref, start, (row >> 4) * CAP + (row & 3), (row & 4) != 0)

    each_block(cold_ref.shape[0], COLD_BLOCK, cold_block)


def swiglu_back(pre_gate, pre_up, back, prob):
    sig = 1.0 / (1.0 + jnp.exp(-pre_gate))
    act = pre_gate * sig
    hidden = act * pre_up
    scaled = prob * back
    gate_grad = scaled * pre_up * sig * (1.0 + pre_gate * (1.0 - sig))
    return gate_grad, scaled * act, prob * hidden, hidden * back


def hot_kernel(chunk_count, *refs):
    chunks = refs[:chunk_count]
    weights = refs[chunk_count : chunk_count + 4]
    own_ref, sent_1, sent_2, sent_3, dx_ref, rows_ref, tail_ref, sum_ref = refs[chunk_count + 4 :]
    me = lax.axis_index("dp")
    z_count = chunk_count // 2
    z, core = me // 4, me % 2
    width = rows_ref.shape[1]
    for k in range(z_count):
        for flip in range(2):
            chunk = chunks[flip * z_count + k]
            place = 2 * ((z + z_count - k) % z_count) + (core ^ flip)
            start = pl.multiple_of(place * HCAP, 16)
            rows_ref[pl.ds(start, HCAP), :] = chunk[:, :width]
            tail_ref[pl.ds(start, HCAP), :] = chunk[:, width:]
    units = weights[0].shape[0] // 3
    outs = (own_ref, sent_1, sent_2, sent_3)
    block_chunks = min(CHUNK_BLOCK, chunk_count)
    block_rows = block_chunks * HCAP
    single = block_chunks == chunk_count
    if not single:
        sum_ref[...] = jnp.zeros_like(sum_ref)

    def block(start):
        at = pl.ds(start, block_rows)
        prob = tail_ref[at, :].astype(F32).reshape(block_chunks, HCAP, TAIL)[:, :HALF, 0:1]
        none = jnp.zeros((block_chunks, HALF, units), F32)
        grad_prob = jnp.zeros((block_chunks, HALF, 1), F32)
        x_sides = []
        for j, w_ref in enumerate(weights):
            pre = dot(rows_ref[at, :], w_ref[...], NT).reshape(block_chunks, HCAP, 3 * units)
            gate_grad, up_grad, weighted, prob_term = swiglu_back(
                pre[:, :HALF, :units],
                pre[:, :HALF, units : 2 * units],
                pre[:, HALF:, 2 * units :],
                prob,
            )
            grad_prob = grad_prob + jnp.sum(prob_term, axis=2, keepdims=True)
            x_side = jnp.concatenate([gate_grad, up_grad, none], axis=2)
            g_side = jnp.concatenate([none, none, weighted], axis=2)
            both = jnp.concatenate([x_side, g_side], axis=1).reshape(block_rows, 3 * units)
            term = dot(both.astype(BF), rows_ref[at, :], TN)
            add_to(outs[j] if single else sum_ref.at[j], term, single)
            x_sides.append(x_side.reshape(block_chunks * HALF, 3 * units).astype(BF))
        total = dot(x_sides[0], weights[0][...])
        for x_side, w_ref in zip(x_sides[1:], weights[1:]):
            total = total + dot(x_side, w_ref[...])
        half_at = pl.ds(start // 2 if single else pl.multiple_of(start // 2, 16), block_rows // 2)
        dx_ref[half_at, :width] = total.astype(BF)
        dx_ref[half_at, width:] = split_tail(grad_prob.reshape(block_rows // 2, 1)).astype(BF)

    each_block(chunk_count * HCAP, block_rows, block)
    if not single:
        for j, out_ref in enumerate(outs):
            out_ref[...] = sum_ref[j].astype(out_ref.dtype)


def cold_kernel(got_ref, gate_ref, up_ref, down_ref, dx_ref, out_gate, out_up, out_down, sum_ref):
    total, width = got_ref.shape[0], gate_ref.shape[2]
    rows = min(total, COLD_BLOCK)
    single = rows == total
    outs = (out_gate, out_up, out_down)
    if not single:
        sum_ref[...] = jnp.zeros_like(sum_ref)

    def block(start):
        at = pl.ds(start, rows)
        data = got_ref[at, :width]
        prob = got_ref[at, width:].astype(F32)[:, 0:1]
        pre_gate = dot(data, gate_ref[0], NT)
        pre_up = dot(data, up_ref[0], NT)
        back = pltpu.roll(dot(data, down_ref[0], NT), rows - CAP, 0)
        gate_grad, up_grad, weighted, prob_term = swiglu_back(pre_gate, pre_up, back, prob)
        x_row = (iota(pre_gate.shape, 0) & 4) == 0
        gate_grad = jnp.where(x_row, gate_grad, 0.0).astype(BF)
        up_grad = jnp.where(x_row, up_grad, 0.0).astype(BF)
        weighted = pltpu.roll(jnp.where(x_row, weighted, 0.0), CAP, 0).astype(BF)
        prob_term = jnp.where(x_row, prob_term, 0.0)
        for j, side in enumerate((gate_grad, up_grad, weighted)):
            add_to(outs[j].at[0] if single else sum_ref.at[j], dot(side, data, TN), single)
        pick_shape = (rows // 2, rows)
        row, col = iota(pick_shape, 0), iota(pick_shape, 1)
        pick = jnp.where(col == (row >> 2) * 8 + (row & 3), 1.0, 0.0).astype(BF)
        gate_rows = dot(pick, gate_grad).astype(BF)
        up_rows = dot(pick, up_grad).astype(BF)
        half_at = pl.ds(start // 2 if single else pl.multiple_of(start // 2, 16), rows // 2)
        dx_ref[half_at, :width] = (dot(gate_rows, gate_ref[0]) + dot(up_rows, up_ref[0])).astype(BF)
        tail = split_tail(jnp.sum(prob_term, axis=1, keepdims=True)).astype(BF)
        dx_ref[half_at, width:] = dot(pick, tail).astype(BF)

    each_block(total, rows, block)
    if not single:
        for j, out_ref in enumerate(outs):
            out_ref[0] = sum_ref[j].astype(BF)


def combine_kernel(chunk_count, hot_ref, cold_ref, own_ref, send_ref):
    lanes = hot_ref.shape[1]
    width = lanes - TAIL
    hot = jnp.sum(hot_ref[...].astype(F32).reshape(chunk_count, HALF, lanes), axis=0)
    shape = (cold_ref.shape[0] // 2, cold_ref.shape[0])
    row, col = iota(shape, 0), iota(shape, 1)
    pick = jnp.where(((row >> 2) == (col >> 3)) & ((row & 3) == (col & 3)), 1.0, 0.0).astype(BF)
    rows = jnp.concatenate([hot, dot(pick, cold_ref[...])], axis=0)
    prob = rows[:, width : width + 1] + rows[:, width + 1 : width + 2]
    own_ref[:, :width] = rows[:, :width]
    own_ref[:, width:] = tail_lanes(prob)
    send_ref[:, :width] = rows[:, :width].astype(BF)
    send_ref[:, width:] = split_tail(prob).astype(BF)


def finish_kernel(base, own_ref, got_ref, ids_ref, slot_ref, flags_ref, owner_ref, dx_ref, prob_ref):
    pair = lax.axis_index("pair")
    half = dx_ref.shape[0]
    width = dx_ref.shape[1]
    pos = positions(ids_ref[...], slot_ref[...], flags_ref, owner_ref, base)
    pos = jnp.where(pair == 0, pos[:, :half], pos[:, half:])
    row = iota((own_ref.shape[0], half), 0)

    def chosen(side):
        target = jnp.where(row < HALF, base + HALF * side + row, row - HALF)
        return pos[0:1, :] == target, pos[1:2, :] == target

    def onehot(sides):
        return jnp.where(sides[0] | sides[1], 1.0, 0.0).astype(BF)

    own_side, got_side = chosen(pair), chosen(1 - pair)
    own = own_ref[:, :width]
    high = own.astype(BF)
    low = (own - high.astype(F32)).astype(BF)
    own_hot, got_hot = onehot(own_side), onehot(got_side)
    total = dot(own_hot, high, TN) + dot(own_hot, low, TN) + dot(got_hot, got_ref[:, :width], TN)
    dx_ref[...] = total.astype(BF)
    own_prob = own_ref[:, width : width + 1]
    got_tail = got_ref[:, width:].astype(F32)
    got_prob = got_tail[:, 0:1] + got_tail[:, 1:2]
    for k in range(TOP):
        terms = jnp.where(own_side[k], own_prob, 0.0) + jnp.where(got_side[k], got_prob, 0.0)
        prob_ref[k : k + 1, :] = jnp.sum(terms, axis=0, keepdims=True)


def sum_kernel(own_ref, a_ref, b_ref, c_ref, gate_ref, up_ref, down_ref):
    total = own_ref[...] + a_ref[...].astype(F32) + b_ref[...].astype(F32) + c_ref[...].astype(F32)
    units = gate_ref.shape[0]
    for index, out_ref in enumerate((gate_ref, up_ref, down_ref)):
        out_ref[...] = total[index * units : (index + 1) * units].astype(BF)


def call(kernel, outs, name, flops, scratch=(), smem=()):
    def run(*args):
        space = [pltpu.SMEM if i in smem else pltpu.VMEM for i in range(len(args))]
        moved = sum(a.size * a.dtype.itemsize for a in args)
        moved += sum(o.size * o.dtype.itemsize for o in outs)
        return pl.pallas_call(
            kernel,
            out_shape=outs,
            in_specs=[pl.BlockSpec(memory_space=s) for s in space],
            out_specs=[pl.BlockSpec(memory_space=pltpu.VMEM) for _ in outs],
            scratch_shapes=list(scratch),
            compiler_params=pltpu.CompilerParams(vmem_limit_bytes=VMEM_LIMIT),
            cost_estimate=pl.CostEstimate(flops=flops, bytes_accessed=moved, transcendentals=0),
            name=name,
        )(*args)

    return run


def local(
    tokens,
    grad_out,
    gate_probs,
    expert_ids,
    route_slots,
    hot_flags,
    owner_slot,
    cold_gate,
    cold_up,
    cold_down,
    hot_gate,
    hot_up,
    hot_down,
):
    count = lax.axis_size("dp")
    z_count = count // 4
    chunk_count = 2 * z_count
    token_count, width = tokens.shape
    lanes = width + TAIL
    units = hot_gate.shape[0]
    base = (count // 2) * CAP
    shape = jax.ShapeDtypeStruct
    half = token_count // 2
    pad = -units % 8

    hot_rows = [jnp.pad(w, ((0, pad), (0, 0))) if pad else w for w in (hot_gate, hot_up, hot_down)]
    hot_own = jnp.concatenate(hot_rows, axis=0)
    units_padded = units + pad

    def swap(value, mask):
        flip_dp, flip_pair = 2 * (mask & 1), mask >> 1
        perm = [
            (2 * i + p, 2 * (i ^ flip_dp) + (p ^ flip_pair)) for i in range(count) for p in range(2)
        ]
        return lax.ppermute(value, ("dp", "pair"), perm)

    weights = [hot_own] + [swap(hot_own, mask) for mask in (1, 2, 3)]

    ids_t, slots_t, probs_t = expert_ids.T, route_slots.T, gate_probs.T
    hot_chunk, cold_send = call(
        functools.partial(dispatch_kernel, base),
        [shape((HCAP, lanes), BF), shape((count * 2 * CAP, lanes), BF)],
        "dispatch",
        4 * (HCAP + count * 2 * CAP) * token_count * width,
        smem=(5, 6),
    )(tokens, grad_out, probs_t, ids_t, slots_t, hot_flags, owner_slot)

    def along_z(value, k):
        perm = [(i, 4 * ((i // 4 + k) % z_count) + i % 4) for i in range(count)]
        return lax.ppermute(value, "dp", perm)

    def other_core(value):
        return lax.ppermute(value, "dp", [(i, i ^ 1) for i in range(count)])

    chunks = [hot_chunk] + [along_z(hot_chunk, k) for k in range(1, z_count)]
    cold_got = lax.all_to_all(
        cold_send.reshape(count, 2 * CAP, lanes), "dp", split_axis=0, concat_axis=0, tiled=True
    ).reshape(count * 2 * CAP, lanes)
    chunks = chunks + [other_core(chunk) for chunk in chunks]

    cold_units = cold_gate.shape[1]
    cold_shape = shape(cold_gate.shape, BF)
    cold_dx, grad_cold_gate, grad_cold_up, grad_cold_down = call(
        cold_kernel,
        [shape((count * CAP, lanes), BF), cold_shape, cold_shape, cold_shape],
        "cold",
        16 * count * CAP * 2 * cold_units * width,
        scratch=[pltpu.VMEM((3, cold_units, width) if count * 2 * CAP > COLD_BLOCK else (8, 128), F32)],
    )(cold_got, cold_gate, cold_up, cold_down)

    hot_rows_total = chunk_count * HCAP
    term = shape((3 * units_padded, width), BF)
    own_term, *sent_terms, hot_dx = call(
        functools.partial(hot_kernel, chunk_count),
        [shape(term.shape, F32), term, term, term, shape((chunk_count * HALF, lanes), BF)],
        "hot",
        4 * 6 * hot_rows_total * 3 * units_padded * width,
        scratch=[
            pltpu.VMEM((hot_rows_total, width), BF),
            pltpu.VMEM((hot_rows_total, TAIL), BF),
            pltpu.VMEM((4,) + term.shape if chunk_count > CHUNK_BLOCK else (8, 128), F32),
        ],
    )(*chunks, *weights)
    got_terms = [swap(value, mask) for value, mask in zip(sent_terms, (1, 2, 3))]

    groups = [
        [4 * z + 2 * x + core for z in range(z_count) for core in range(2)] for x in range(2)
    ]
    hot_back = lax.all_to_all(
        hot_dx.reshape(chunk_count, HALF, lanes),
        "dp",
        split_axis=0,
        concat_axis=0,
        tiled=True,
        axis_index_groups=groups,
    ).reshape(chunk_count * HALF, lanes)
    cold_back = lax.all_to_all(
        cold_dx.reshape(count, CAP, lanes), "dp", split_axis=0, concat_axis=0, tiled=True
    ).reshape(count * CAP, lanes)

    rows_back = HALF + base
    own_rows, send_rows = call(
        functools.partial(combine_kernel, chunk_count),
        [shape((rows_back, lanes), F32), shape((rows_back, lanes), BF)],
        "combine",
        2 * base * base * 2 * lanes,
    )(hot_back, cold_back)
    got_rows = lax.ppermute(send_rows, "pair", [(0, 1), (1, 0)])
    dx, prob_t = call(
        functools.partial(finish_kernel, base),
        [shape((half, width), BF), shape((TOP, half), F32)],
        "finish",
        6 * rows_back * half * width,
        smem=(4, 5),
    )(own_rows, got_rows, ids_t, slots_t, hot_flags, owner_slot)

    out_shape = shape((units_padded, width), BF)
    hot_grads = call(sum_kernel, [out_shape] * 3, "hot_sum", 9 * units_padded * width)(
        own_term, *got_terms
    )
    if pad:
        hot_grads = [value[:units] for value in hot_grads]
    return (dx, prob_t.T, grad_cold_gate, grad_cold_up, grad_cold_down, *hot_grads)


def solution(mesh):
    return jax.shard_map(
        local,
        mesh=mesh,
        in_specs=(
            P("dp", None),
            P("dp", None),
            P("dp", None),
            P("dp", None),
            P("dp", None),
            P(),
            P(),
            P("dp", "pair", None),
            P("dp", "pair", None),
            P("dp", "pair", None),
            P(("dp", "pair"), None),
            P(("dp", "pair"), None),
            P(("dp", "pair"), None),
        ),
        out_specs=(
            P(("dp", "pair"), None),
            P(("dp", "pair"), None),
            P("dp", "pair", None),
            P("dp", "pair", None),
            P("dp", "pair", None),
            P(("dp", "pair"), None),
            P(("dp", "pair"), None),
            P(("dp", "pair"), None),
        ),
        check_vma=False,
    )
```

```python
import functools

import jax
import jax.numpy as jnp
from jax import lax
from jax.experimental import pallas as pl
from jax.experimental.pallas import tpu as pltpu
from jax.sharding import PartitionSpec as P

TOP = 2
CAP = 4
HCAP = 48
HALF = HCAP // 2
TAIL = 128
CHUNK_BLOCK = 8
COLD_BLOCK = 64
UNIT_BLOCK = 128
COLD_LANES = 1024
BF = jnp.bfloat16
F32 = jnp.float32
VMEM_LIMIT = 56 * 1024 * 1024
VMEM_BASE = 6 * 1024 * 1024

NT = (((1,), (1,)), ((), ()))
TN = (((0,), (0,)), ((), ()))


def dot(a, b, dims=(((1,), (0,)), ((), ()))):
    return lax.dot_general(a, b, dims, preferred_element_type=F32)


def iota(shape, dim):
    return lax.broadcasted_iota(jnp.int32, shape, dim)


def positions(ids, slots, flags_ref, owner_ref, base):
    hot = jnp.zeros_like(ids)
    own = jnp.zeros_like(ids)
    for e in range(flags_ref.shape[0]):
        named = ids == e
        hot = jnp.where(named, flags_ref[e], hot)
        own = jnp.where(named, owner_ref[e], own)
    cold_pos = jnp.where(slots < CAP, own * CAP + slots, -1)
    hot_pos = jnp.where(slots < HCAP, base + slots, -1)
    return jnp.where(hot == 1, hot_pos, cold_pos)


def tail_lanes(first, second=None):
    lane = iota((first.shape[0], TAIL), 1)
    out = jnp.where(lane == 0, first, 0.0)
    if second is not None:
        out = jnp.where(lane == 1, second, out)
    return out


def split_tail(value):
    high = value.astype(BF).astype(F32)
    return tail_lanes(high, value - high)


def each_block(total, size, body):
    if total == size:
        body(0)
    else:

        def step(block, carry):
            body(pl.multiple_of(block * size, size))
            return carry

        lax.fori_loop(0, total // size, step, 0)


def add_to(ref, value, single):
    if single:
        ref[...] = value.astype(ref.dtype)
    else:
        ref[...] += value


def dispatch_kernel(
    base, tok_ref, grad_ref, prob_ref, ids_ref, slot_ref, flags_ref, owner_ref, hot_ref, cold_ref
):
    pair = lax.axis_index("pair")
    pos = positions(ids_ref[...], slot_ref[...], flags_ref, owner_ref, base)
    prob = prob_ref[...].astype(F32)
    width = tok_ref.shape[1]

    def fill(out_ref, start, target, is_grad):
        at = pl.ds(start, target.shape[0])
        first = pos[0:1, :] == target
        second = pos[1:2, :] == target
        chosen = jnp.where(first | second, 1.0, 0.0)
        rows = dot(jnp.where(is_grad, 0.0, chosen).astype(BF), tok_ref[...]) + dot(
            jnp.where(is_grad, chosen, 0.0).astype(BF), grad_ref[...]
        )
        out_ref[at, :width] = rows.astype(BF)
        weight = jnp.where(first, prob[0:1, :], 0.0) + jnp.where(second, prob[1:2, :], 0.0)
        weight = jnp.sum(jnp.where(is_grad, 0.0, weight), axis=1, keepdims=True)
        out_ref[at, width:] = tail_lanes(weight).astype(BF)

    tokens = tok_ref.shape[0]
    row = iota((HCAP, tokens), 0)
    fill(hot_ref, 0, base + HALF * pair + jnp.where(row >= HALF, row - HALF, row), row >= HALF)

    def cold_block(start):
        row = start + iota((COLD_BLOCK, tokens), 0)
        fill(cold_ref, start, (row >> 3) * CAP + (row & 3), (row & 4) != 0)

    each_block(cold_ref.shape[0], COLD_BLOCK, cold_block)


def swiglu_back(pre_gate, pre_up, back, prob):
    sig = 1.0 / (1.0 + jnp.exp(-pre_gate))
    act = pre_gate * sig
    hidden = act * pre_up
    scaled = prob * back
    gate_grad = scaled * pre_up * sig * (1.0 + pre_gate * (1.0 - sig))
    return gate_grad, scaled * act, prob * hidden, hidden * back


def write_rows(out_ref, rows, prob):
    width = rows.shape[1]
    out_ref[:, :width] = rows.astype(out_ref.dtype)
    tail = tail_lanes(prob) if out_ref.dtype == F32 else split_tail(prob).astype(BF)
    out_ref[:, width:] = tail


def read_rows(value):
    value = value.astype(F32)
    width = value.shape[1] - TAIL
    return value[:, :width], value[:, width : width + 1] + value[:, width + 1 : width + 2]


def hot_kernel(chunk_count, units, *refs):
    chunks = refs[:chunk_count]
    weights = refs[chunk_count : chunk_count + 4]
    own_ref, send_ref, side_ref, rows_ref, tail_ref, wide_ref = refs[chunk_count + 4 :]
    width = rows_ref.shape[1]
    for k, chunk in enumerate(chunks):
        rows_ref[k * HCAP : (k + 1) * HCAP, :] = chunk[:, :width]
        tail_ref[k * HCAP : (k + 1) * HCAP, :] = chunk[:, width:]
    used = 3 * units
    for j, w_ref in enumerate(weights):
        start = j * UNIT_BLOCK
        clear = used // 16 * 16
        if clear < UNIT_BLOCK:
            wide_ref[start + clear : start + UNIT_BLOCK, :] = jnp.zeros((UNIT_BLOCK - clear, width), BF)
        wide_ref[start : start + used, :] = w_ref[...]
    columns = 4 * UNIT_BLOCK
    block_chunks = min(CHUNK_BLOCK, chunk_count)
    block_rows = block_chunks * HCAP
    half_rows = block_rows // 2

    def block(start):
        at = pl.ds(start, block_rows)
        prob = tail_ref[at, :].astype(F32).reshape(block_chunks, HCAP, TAIL)[:, :HALF, 0:1]
        prob = prob.reshape(half_rows, 1)
        pre = dot(rows_ref[at, :], wide_ref[...], NT).reshape(block_chunks, HCAP, columns)
        pre_x = pre[:, :HALF].reshape(half_rows, columns)
        pre_g = pre[:, HALF:].reshape(half_rows, columns)
        first = (iota(pre_x.shape, 1) & (UNIT_BLOCK - 1)) < units
        gate_grad, up_grad, weighted, prob_term = swiglu_back(
            pre_x,
            pltpu.roll(pre_x, columns - units, 1),
            pltpu.roll(pre_g, columns - 2 * units, 1),
            prob,
        )
        gate_grad, up_grad, weighted, prob_term = (
            jnp.where(first, value, 0.0) for value in (gate_grad, up_grad, weighted, prob_term)
        )
        grad_prob = jnp.sum(prob_term, axis=1, keepdims=True)
        x_side = gate_grad + pltpu.roll(up_grad, units, 1)
        g_side = pltpu.roll(weighted, 2 * units, 1)
        both = jnp.concatenate(
            [x_side.reshape(block_chunks, HALF, columns), g_side.reshape(block_chunks, HALF, columns)],
            axis=1,
        )
        side_ref[at, :] = both.reshape(block_rows, columns).astype(BF)
        return dot(x_side.astype(BF), wide_ref[...]), grad_prob

    if block_chunks == chunk_count:
        dx, grad_prob = block(0)
        write_rows(own_ref, dx[: half_rows // 2], grad_prob[: half_rows // 2])
        write_rows(send_ref, dx[half_rows // 2 :], grad_prob[half_rows // 2 :])
    else:
        for out_ref, offset in ((own_ref, 0), (send_ref, chunk_count * HCAP // 2)):

            def step(index, carry, out_ref=out_ref, offset=offset):
                dx, grad_prob = block(pl.multiple_of(offset + index * block_rows, 16))
                at = pl.ds(pl.multiple_of(index * half_rows, 16), half_rows)
                write_rows(out_ref.at[at], dx, grad_prob)
                return carry

            lax.fori_loop(0, chunk_count // block_chunks // 2, step, 0)


def terms_kernel(side_ref, rows_ref, own_ref, sent_1, sent_2, sent_3, sum_ref):
    used = own_ref.shape[0]
    total = side_ref.shape[0]
    block_rows = min(CHUNK_BLOCK * HCAP, total)
    outs = (own_ref, sent_1, sent_2, sent_3)

    def term(start, j):
        at = pl.ds(start, block_rows)
        columns = slice(j * UNIT_BLOCK, (j + 1) * UNIT_BLOCK)
        return dot(side_ref[at, columns], rows_ref[at, :], TN)[:used]

    if block_rows == total:
        for j, out_ref in enumerate(outs):
            out_ref[...] = term(0, j).astype(out_ref.dtype)
    else:
        sum_ref[...] = jnp.zeros_like(sum_ref)

        def step(index, carry):
            for j in range(4):
                sum_ref[j] += term(pl.multiple_of(index * block_rows, 16), j)
            return carry

        lax.fori_loop(0, total // block_rows, step, 0)
        for j, out_ref in enumerate(outs):
            out_ref[...] = sum_ref[j].astype(out_ref.dtype)


def cold_kernel(
    mine_ref, other_ref, gate_ref, up_ref, down_ref, dx_ref, out_gate, out_up, out_down, sum_ref
):
    total, width = mine_ref.shape[0], gate_ref.shape[2]
    core = lax.axis_index("dp") & 1
    side = COLD_BLOCK
    rows = 2 * side
    single = side == total
    outs = (out_gate, out_up, out_down)
    if not single:
        sum_ref[...] = jnp.zeros_like(sum_ref)

    def block(start):
        at = pl.ds(start, side)
        both = jnp.concatenate([mine_ref[at, :], other_ref[at, :]], axis=0)
        data = both[:, :width]
        prob = both[:, width:].astype(F32)[:, 0:1]
        pre_gate = dot(data, gate_ref[0], NT)
        pre_up = dot(data, up_ref[0], NT)
        back = pltpu.roll(dot(data, down_ref[0], NT), rows - CAP, 0)
        gate_grad, up_grad, weighted, prob_term = swiglu_back(pre_gate, pre_up, back, prob)
        x_row = (iota(pre_gate.shape, 0) & 4) == 0
        gate_grad = jnp.where(x_row, gate_grad, 0.0).astype(BF)
        up_grad = jnp.where(x_row, up_grad, 0.0).astype(BF)
        weighted = pltpu.roll(jnp.where(x_row, weighted, 0.0), CAP, 0).astype(BF)
        prob_term = jnp.where(x_row, prob_term, 0.0)
        shape = (rows, rows)
        row, col = iota(shape, 0), iota(shape, 1)
        source = (((row >> 3) & 1) ^ core) * side + (row >> 4) * 8 + (row & 3)
        found = jnp.where(col == source, 1.0, 0.0)
        low = jnp.where((row & 4) == 0, found, 0.0).astype(BF)
        high = jnp.where((row & 4) == 0, 0.0, found).astype(BF)
        dx = (dot(gate_grad, gate_ref[0]) + dot(up_grad, up_ref[0])).astype(BF)
        tail = split_tail(jnp.sum(prob_term, axis=1, keepdims=True)).astype(BF)
        out_at = pl.ds(2 * start if single else pl.multiple_of(2 * start, 16), rows)
        rest = width - COLD_LANES
        both_low = dot(low, dx[:, :COLD_LANES])
        dx_ref[out_at, :rest] = (both_low[:, :rest] + dot(high, dx[:, COLD_LANES:])).astype(BF)
        dx_ref[out_at, rest : rest + TAIL] = (
            both_low[:, rest : rest + TAIL] + dot(high, tail)
        ).astype(BF)
        dx_ref[out_at, rest + TAIL :] = both_low[:, rest + TAIL :].astype(BF)
        for j, grad in enumerate((gate_grad, up_grad, weighted)):
            add_to(outs[j].at[0] if single else sum_ref.at[j], dot(grad, data, TN), single)

    each_block(total, side, block)
    if not single:
        for j, out_ref in enumerate(outs):
            out_ref[0] = sum_ref[j].astype(BF)


def add_kernel(own_ref, got_ref, *outs):
    for k, out_ref in enumerate(outs):
        at = slice(k * HALF, (k + 1) * HALF)
        rows, prob = read_rows(own_ref[at, :])
        got_rows, got_prob = read_rows(got_ref[...].astype(F32)[at])
        write_rows(out_ref, rows + got_rows, prob + got_prob)


def combine_kernel(*refs):
    *hot_refs, cold_ref, own_ref, send_ref = refs
    hot, hot_prob = read_rows(hot_refs[0][...])
    for ref in hot_refs[1:]:
        rows, prob = read_rows(ref[...])
        hot, hot_prob = hot + rows, hot_prob + prob
    total = cold_ref.shape[0]
    shape = (total // 4, total)
    row, col = iota(shape, 0), iota(shape, 1)
    found = jnp.where(((row >> 2) == (col >> 4)) & ((row & 3) == (col & 3)), 1.0, 0.0)
    low = dot(jnp.where((col & 4) == 0, found, 0.0).astype(BF), cold_ref[...])
    high = dot(jnp.where((col & 4) == 0, 0.0, found).astype(BF), cold_ref[...])
    rest = hot.shape[1] - COLD_LANES
    cold_prob = high[:, rest : rest + 1] + high[:, rest + 1 : rest + 2]
    cold = jnp.concatenate([low, high[:, :rest]], axis=1)
    rows = jnp.concatenate([hot, cold], axis=0)
    prob = jnp.concatenate([hot_prob, cold_prob], axis=0)
    write_rows(own_ref, rows, prob)
    write_rows(send_ref, rows, prob)


def finish_kernel(base, own_ref, got_ref, ids_ref, slot_ref, flags_ref, owner_ref, dx_ref, prob_ref):
    pair = lax.axis_index("pair")
    half = dx_ref.shape[0]
    width = dx_ref.shape[1]
    pos = positions(ids_ref[...], slot_ref[...], flags_ref, owner_ref, base)
    pos = jnp.where(pair == 0, pos[:, :half], pos[:, half:])
    row = iota((own_ref.shape[0], half), 0)

    def chosen(side):
        target = jnp.where(row < HALF, base + HALF * side + row, row - HALF)
        return pos[0:1, :] == target, pos[1:2, :] == target

    def onehot(sides):
        return jnp.where(sides[0] | sides[1], 1.0, 0.0).astype(BF)

    own_side, got_side = chosen(pair), chosen(1 - pair)
    own = own_ref[:, :width]
    high = own.astype(BF)
    low = (own - high.astype(F32)).astype(BF)
    own_hot, got_hot = onehot(own_side), onehot(got_side)
    total = dot(own_hot, high, TN) + dot(own_hot, low, TN) + dot(got_hot, got_ref[:, :width], TN)
    dx_ref[...] = total.astype(BF)
    own_prob = own_ref[:, width : width + 1]
    got_tail = got_ref[:, width:].astype(F32)
    got_prob = got_tail[:, 0:1] + got_tail[:, 1:2]
    for k in range(TOP):
        terms = jnp.where(own_side[k], own_prob, 0.0) + jnp.where(got_side[k], got_prob, 0.0)
        prob_ref[k : k + 1, :] = jnp.sum(terms, axis=0, keepdims=True)


def sum_kernel(own_ref, a_ref, b_ref, c_ref, gate_ref, up_ref, down_ref):
    total = own_ref[...] + a_ref[...].astype(F32) + b_ref[...].astype(F32) + c_ref[...].astype(F32)
    units = gate_ref.shape[0]
    for index, out_ref in enumerate((gate_ref, up_ref, down_ref)):
        out_ref[...] = total[index * units : (index + 1) * units].astype(BF)


def call(kernel, outs, name, flops, scratch=(), smem=()):
    def run(*args):
        space = [pltpu.SMEM if i in smem else pltpu.VMEM for i in range(len(args))]
        moved = sum(a.size * a.dtype.itemsize for a in args)
        moved += sum(o.size * o.dtype.itemsize for o in outs)
        return pl.pallas_call(
            kernel,
            out_shape=outs,
            in_specs=[pl.BlockSpec(memory_space=s) for s in space],
            out_specs=[pl.BlockSpec(memory_space=pltpu.VMEM) for _ in outs],
            scratch_shapes=[pltpu.VMEM(*each) for each in scratch],
            compiler_params=pltpu.CompilerParams(
                vmem_limit_bytes=min(VMEM_LIMIT, VMEM_BASE + 3 * moved)
            ),
            cost_estimate=pl.CostEstimate(flops=flops, bytes_accessed=moved, transcendentals=0),
            name=name,
        )(*args)

    return run


def local(
    tokens,
    grad_out,
    gate_probs,
    expert_ids,
    route_slots,
    hot_flags,
    owner_slot,
    cold_gate,
    cold_up,
    cold_down,
    hot_gate,
    hot_up,
    hot_down,
):
    count = lax.axis_size("dp")
    z_count = count // 4
    chunk_count = 2 * z_count
    token_count, width = tokens.shape
    lanes = width + TAIL
    units = hot_gate.shape[0]
    base = (count // 2) * CAP
    shape = jax.ShapeDtypeStruct
    half = token_count // 2
    pad = -units % 8

    hot_rows = [jnp.pad(w, ((0, pad), (0, 0))) if pad else w for w in (hot_gate, hot_up, hot_down)]
    hot_own = jnp.concatenate(hot_rows, axis=0)
    units_padded = units + pad

    def swap(value, mask):
        flip_dp, flip_pair = 2 * (mask & 1), mask >> 1
        perm = [
            (2 * i + p, 2 * (i ^ flip_dp) + (p ^ flip_pair)) for i in range(count) for p in range(2)
        ]
        return lax.ppermute(value, ("dp", "pair"), perm)

    by_pair = swap(hot_own, 2)
    weights = [hot_own, swap(hot_own, 1), by_pair, swap(by_pair, 1)]

    ids_t, slots_t, probs_t = expert_ids.T, route_slots.T, gate_probs.T
    chips = count // 2
    cold_rows = chips * 2 * CAP
    hot_chunk, cold_send = call(
        functools.partial(dispatch_kernel, base),
        [shape((HCAP, lanes), BF), shape((cold_rows, lanes), BF)],
        "dispatch",
        4 * (HCAP + cold_rows) * token_count * width,
        smem=(5, 6),
    )(tokens, grad_out, probs_t, ids_t, slots_t, hot_flags, owner_slot)

    def along_z(value, k):
        perm = [(i, 4 * ((i // 4 + k) % z_count) + i % 4) for i in range(count)]
        return lax.ppermute(value, "dp", perm)

    def other_core(value):
        return lax.ppermute(value, "dp", [(i, i ^ 1) for i in range(count)])

    chunks = [hot_chunk] + [along_z(hot_chunk, k) for k in range(1, z_count)]
    same_core = [[2 * chip + core for chip in range(chips)] for core in range(2)]
    cold_mine = lax.all_to_all(
        cold_send.reshape(chips, 2 * CAP, lanes),
        "dp",
        split_axis=0,
        concat_axis=0,
        tiled=True,
        axis_index_groups=same_core,
    ).reshape(cold_rows, lanes)
    cold_other = other_core(cold_mine)
    first_out, _ = lax.optimization_barrier((hot_chunk, chunks[-1]))
    chunks = chunks + [other_core(first_out)] + [other_core(chunk) for chunk in chunks[1:]]

    cold_units = cold_gate.shape[1]
    cold_shape = shape(cold_gate.shape, BF)
    cold_dx, grad_cold_gate, grad_cold_up, grad_cold_down = call(
        cold_kernel,
        [shape((count * 2 * CAP, COLD_LANES), BF), cold_shape, cold_shape, cold_shape],
        "cold",
        16 * 2 * cold_rows * cold_units * width,
        scratch=[((3, cold_units, width) if cold_rows > COLD_BLOCK else (8, 128), F32)],
    )(cold_mine, cold_other, cold_gate, cold_up, cold_down)

    used = 3 * units_padded
    all_rows = chunk_count * HCAP
    half_rows = chunk_count * HALF // 2
    dx_own, dx_send, side, rows = call(
        functools.partial(hot_kernel, chunk_count, units_padded),
        [
            shape((half_rows, lanes), F32),
            shape((half_rows, lanes), BF),
            shape((all_rows, 4 * UNIT_BLOCK), BF),
            shape((all_rows, width), BF),
        ],
        "hot",
        3 * all_rows * 4 * UNIT_BLOCK * width,
        scratch=[((all_rows, TAIL), BF), ((4 * UNIT_BLOCK, width), BF)],
    )(*chunks, *weights)
    dx_got = other_core(dx_send)
    own_term, *sent_terms = call(
        terms_kernel,
        [shape((used, width), F32)] + [shape((used, width), BF)] * 3,
        "hot_terms",
        2 * all_rows * 4 * UNIT_BLOCK * width,
        scratch=[((4, used, width) if chunk_count > CHUNK_BLOCK else (8, 128), F32)],
    )(side, rows)
    hot_parts = call(
        add_kernel,
        [shape((HALF, lanes), F32)] + [shape((HALF, lanes), BF)] * (z_count - 1),
        "add_cores",
        2 * half_rows * lanes,
    )(dx_own, dx_got)
    hot_back = [hot_parts[0]] + [along_z(hot_parts[k], -k) for k in range(1, z_count)]
    got_terms = [swap(value, mask) for value, mask in zip(sent_terms[:2], (1, 2))]
    last_term, _ = lax.optimization_barrier((sent_terms[2], hot_back[-1]))
    got_terms.append(swap(last_term, 3))
    cold_dx, _ = lax.optimization_barrier((cold_dx, hot_parts[0]))
    cold_back = lax.all_to_all(
        cold_dx.reshape(count, 2 * CAP, COLD_LANES), "dp", split_axis=0, concat_axis=0, tiled=True
    ).reshape(count * 2 * CAP, COLD_LANES)

    rows_back = HALF + base
    own_rows, send_rows = call(
        combine_kernel,
        [shape((rows_back, lanes), F32), shape((rows_back, lanes), BF)],
        "combine",
        2 * base * base * 2 * lanes,
    )(*hot_back, cold_back)
    got_rows = lax.ppermute(send_rows, "pair", [(0, 1), (1, 0)])
    dx, prob_t = call(
        functools.partial(finish_kernel, base),
        [shape((half, width), BF), shape((TOP, half), F32)],
        "finish",
        6 * rows_back * half * width,
        smem=(4, 5),
    )(own_rows, got_rows, ids_t, slots_t, hot_flags, owner_slot)

    out_shape = shape((units_padded, width), BF)
    hot_grads = call(sum_kernel, [out_shape] * 3, "hot_sum", 9 * units_padded * width)(
        own_term, *got_terms
    )
    if pad:
        hot_grads = [value[:units] for value in hot_grads]
    return (dx, prob_t.T, grad_cold_gate, grad_cold_up, grad_cold_down, *hot_grads)


def solution(mesh):
    return jax.shard_map(
        local,
        mesh=mesh,
        in_specs=(
            P("dp", None),
            P("dp", None),
            P("dp", None),
            P("dp", None),
            P("dp", None),
            P(),
            P(),
            P("dp", "pair", None),
            P("dp", "pair", None),
            P("dp", "pair", None),
            P(("dp", "pair"), None),
            P(("dp", "pair"), None),
            P(("dp", "pair"), None),
        ),
        out_specs=(
            P(("dp", "pair"), None),
            P(("dp", "pair"), None),
            P("dp", "pair", None),
            P("dp", "pair", None),
            P("dp", "pair", None),
            P(("dp", "pair"), None),
            P(("dp", "pair"), None),
            P(("dp", "pair"), None),
        ),
        check_vma=False,
    )
```

```python
import functools

import jax
import jax.numpy as jnp
from jax import lax
from jax.experimental import pallas as pl
from jax.experimental.pallas import tpu as pltpu
from jax.sharding import PartitionSpec as P

TOP = 2
CAP = 4
HCAP = 48
HALF = HCAP // 2
TAIL = 128
CHUNK_BLOCK = 8
COLD_BLOCK = 64
UNIT_BLOCK = 128
BF = jnp.bfloat16
F32 = jnp.float32
VMEM_LIMIT = 56 * 1024 * 1024
VMEM_BASE = 6 * 1024 * 1024

NT = (((1,), (1,)), ((), ()))
TN = (((0,), (0,)), ((), ()))


def dot(a, b, dims=(((1,), (0,)), ((), ()))):
    return lax.dot_general(a, b, dims, preferred_element_type=F32)


def iota(shape, dim):
    return lax.broadcasted_iota(jnp.int32, shape, dim)


def positions(ids, slots, flags_ref, owner_ref, base):
    hot = jnp.zeros_like(ids)
    own = jnp.zeros_like(ids)
    for e in range(flags_ref.shape[0]):
        named = ids == e
        hot = jnp.where(named, flags_ref[e], hot)
        own = jnp.where(named, owner_ref[e], own)
    cold_pos = jnp.where(slots < CAP, own * CAP + slots, -1)
    hot_pos = jnp.where(slots < HCAP, base + slots, -1)
    return jnp.where(hot == 1, hot_pos, cold_pos)


def tail_lanes(first, second=None):
    lane = iota((first.shape[0], TAIL), 1)
    out = jnp.where(lane == 0, first, 0.0)
    if second is not None:
        out = jnp.where(lane == 1, second, out)
    return out


def split_tail(value):
    high = value.astype(BF).astype(F32)
    return tail_lanes(high, value - high)


def each_block(total, size, body):
    if total == size:
        body(0)
    else:

        def step(block, carry):
            body(pl.multiple_of(block * size, size))
            return carry

        lax.fori_loop(0, total // size, step, 0)


def add_to(ref, value, single):
    if single:
        ref[...] = value.astype(ref.dtype)
    else:
        ref[...] += value


def gather_rows(out_ref, start, target, is_grad, pos, prob, tok_ref, grad_ref):
    width = tok_ref.shape[1]
    at = pl.ds(start, target.shape[0])
    first = pos[0:1, :] == target
    second = pos[1:2, :] == target
    chosen = jnp.where(first | second, 1.0, 0.0)
    rows = dot(jnp.where(is_grad, 0.0, chosen).astype(BF), tok_ref[...]) + dot(
        jnp.where(is_grad, chosen, 0.0).astype(BF), grad_ref[...]
    )
    out_ref[at, :width] = rows.astype(BF)
    weight = jnp.where(first, prob[0:1, :], 0.0) + jnp.where(second, prob[1:2, :], 0.0)
    weight = jnp.sum(jnp.where(is_grad, 0.0, weight), axis=1, keepdims=True)
    out_ref[at, width:] = tail_lanes(weight).astype(BF)


def hot_dispatch_kernel(base, *refs):
    tok_ref, grad_ref, prob_ref, ids_ref, slot_ref, flags_ref, owner_ref = refs[:7]
    gate_ref, up_ref, down_ref, hot_ref, weight_ref, pos_ref = refs[7:]
    pair = lax.axis_index("pair")
    pos = positions(ids_ref[...], slot_ref[...], flags_ref, owner_ref, base)
    pos_ref[...] = pos
    joined = [ref[...].astype(F32) for ref in (gate_ref, up_ref, down_ref)]
    weight_ref[...] = jnp.concatenate(joined, axis=0).astype(BF)
    row = iota((HCAP, tok_ref.shape[0]), 0)
    target = base + HALF * pair + jnp.where(row >= HALF, row - HALF, row)
    prob = prob_ref[...].astype(F32)
    gather_rows(hot_ref, 0, target, row >= HALF, pos, prob, tok_ref, grad_ref)


def cold_dispatch_kernel(tok_ref, grad_ref, prob_ref, pos_ref, cold_ref):
    pos = pos_ref[...]
    prob = prob_ref[...].astype(F32)

    def block(start):
        row = start + iota((COLD_BLOCK, tok_ref.shape[0]), 0)
        target = (row >> 3) * CAP + (row & 3)
        gather_rows(cold_ref, start, target, (row & 4) != 0, pos, prob, tok_ref, grad_ref)

    each_block(cold_ref.shape[0], COLD_BLOCK, block)


def swiglu_back(pre_gate, pre_up, back, prob):
    sig = 1.0 / (1.0 + jnp.exp(-pre_gate))
    act = pre_gate * sig
    hidden = act * pre_up
    scaled = prob * back
    gate_grad = scaled * pre_up * sig * (1.0 + pre_gate * (1.0 - sig))
    return gate_grad, scaled * act, prob * hidden, hidden * back


def write_rows(out_ref, rows, prob):
    width = rows.shape[1]
    out_ref[:, :width] = rows.astype(out_ref.dtype)
    tail = tail_lanes(prob) if out_ref.dtype == F32 else split_tail(prob).astype(BF)
    out_ref[:, width:] = tail


def read_rows(value):
    value = value.astype(F32)
    width = value.shape[1] - TAIL
    return value[:, :width], value[:, width : width + 1] + value[:, width + 1 : width + 2]


def hot_kernel(chunk_count, units, *refs):
    chunks = refs[:chunk_count]
    weights = refs[chunk_count : chunk_count + 4]
    own_ref, send_ref, *terms = refs[chunk_count + 4 : chunk_count + 10]
    rows_ref, tail_ref, wide_ref, sum_ref = refs[chunk_count + 10 :]
    width = rows_ref.shape[1]
    for k, chunk in enumerate(chunks):
        rows_ref[k * HCAP : (k + 1) * HCAP, :] = chunk[:, :width]
        tail_ref[k * HCAP : (k + 1) * HCAP, :] = chunk[:, width:]
    used = 3 * units
    for j, w_ref in enumerate(weights):
        start = j * UNIT_BLOCK
        clear = used // 16 * 16
        if clear < UNIT_BLOCK:
            wide_ref[start + clear : start + UNIT_BLOCK, :] = jnp.zeros((UNIT_BLOCK - clear, width), BF)
        wide_ref[start : start + used, :] = w_ref[...]
    columns = 4 * UNIT_BLOCK
    block_chunks = min(CHUNK_BLOCK, chunk_count)
    block_rows = block_chunks * HCAP
    half_rows = block_rows // 2
    single = block_chunks == chunk_count

    def block(start):
        at = pl.ds(start, block_rows)
        prob = tail_ref[at, :].astype(F32).reshape(block_chunks, HCAP, TAIL)[:, :HALF, 0:1]
        prob = prob.reshape(half_rows, 1)
        pre = dot(rows_ref[at, :], wide_ref[...], NT).reshape(block_chunks, HCAP, columns)
        pre_x = pre[:, :HALF].reshape(half_rows, columns)
        pre_g = pre[:, HALF:].reshape(half_rows, columns)
        first = (iota(pre_x.shape, 1) & (UNIT_BLOCK - 1)) < units
        gate_grad, up_grad, weighted, prob_term = swiglu_back(
            pre_x,
            pltpu.roll(pre_x, columns - units, 1),
            pltpu.roll(pre_g, columns - 2 * units, 1),
            prob,
        )
        gate_grad, up_grad, weighted, prob_term = (
            jnp.where(first, value, 0.0) for value in (gate_grad, up_grad, weighted, prob_term)
        )
        grad_prob = jnp.sum(prob_term, axis=1, keepdims=True)
        x_side = gate_grad + pltpu.roll(up_grad, units, 1)
        g_side = pltpu.roll(weighted, 2 * units, 1)
        both = jnp.concatenate(
            [x_side.reshape(block_chunks, HALF, columns), g_side.reshape(block_chunks, HALF, columns)],
            axis=1,
        )
        both = both.reshape(block_rows, columns).astype(BF)
        dx = dot(x_side.astype(BF), wide_ref[...])
        for j in range(4):
            term = dot(both[:, j * UNIT_BLOCK : (j + 1) * UNIT_BLOCK], rows_ref[at, :], TN)
            add_to(terms[j] if single else sum_ref.at[j], term[:used], single)
        return dx, grad_prob

    if single:
        dx, grad_prob = block(0)
        write_rows(own_ref, dx[: half_rows // 2], grad_prob[: half_rows // 2])
        write_rows(send_ref, dx[half_rows // 2 :], grad_prob[half_rows // 2 :])
    else:
        sum_ref[...] = jnp.zeros_like(sum_ref)
        for out_ref, offset in ((own_ref, 0), (send_ref, chunk_count * HCAP // 2)):

            def step(index, carry, out_ref=out_ref, offset=offset):
                dx, grad_prob = block(pl.multiple_of(offset + index * block_rows, 16))
                at = pl.ds(pl.multiple_of(index * half_rows, 16), half_rows)
                write_rows(out_ref.at[at], dx, grad_prob)
                return carry

            lax.fori_loop(0, chunk_count // block_chunks // 2, step, 0)
        for j, out_ref in enumerate(terms):
            out_ref[...] = sum_ref[j].astype(out_ref.dtype)


def cold_kernel(
    mine_ref, other_ref, gate_hbm, up_hbm, down_hbm, own_ref, send_ref, *refs
):
    outs, (w_ref, grad_ref, sum_ref, in_sem, out_sem) = refs[:3], refs[3:]
    total, width = mine_ref.shape[0], gate_hbm.shape[2]
    side = COLD_BLOCK
    rows = 2 * side
    single = side == total
    loads = [
        pltpu.make_async_copy(ref.at[0], w_ref.at[j], in_sem.at[j])
        for j, ref in enumerate((gate_hbm, up_hbm, down_hbm))
    ]
    stores = [
        pltpu.make_async_copy(grad_ref.at[j], ref.at[0], out_sem.at[j]) for j, ref in enumerate(outs)
    ]
    for load in loads:
        load.start()
    if not single:
        sum_ref[...] = jnp.zeros_like(sum_ref)
        for load in loads:
            load.wait()

    def weight(j):
        if single:
            loads[j].wait()
        return w_ref[j]

    def block(start):
        at = pl.ds(start, side)
        both = jnp.concatenate([mine_ref[at, :], other_ref[at, :]], axis=0)
        data = both[:, :width]
        prob = both[:, width:].astype(F32)[:, 0:1]
        gate = weight(0)
        pre_gate = dot(data, gate, NT)
        up = weight(1)
        pre_up = dot(data, up, NT)
        back = pltpu.roll(dot(data, weight(2), NT), rows - CAP, 0)
        gate_grad, up_grad, weighted, prob_term = swiglu_back(pre_gate, pre_up, back, prob)
        x_row = (iota(pre_gate.shape, 0) & 4) == 0
        gate_grad = jnp.where(x_row, gate_grad, 0.0).astype(BF)
        up_grad = jnp.where(x_row, up_grad, 0.0).astype(BF)
        weighted = pltpu.roll(jnp.where(x_row, weighted, 0.0), CAP, 0).astype(BF)
        prob_term = jnp.where(x_row, prob_term, 0.0)
        for j, grad in enumerate((gate_grad, up_grad, weighted)):
            term = dot(grad, data, TN)
            if single:
                grad_ref[j] = term.astype(BF)
                stores[j].start()
            else:
                sum_ref[j] += term
        shape = (side, rows)
        row, col = iota(shape, 0), iota(shape, 1)
        pick = jnp.where(col == (row >> 2) * 8 + (row & 3), 1.0, 0.0).astype(BF)
        gate_rows = dot(pick, gate_grad).astype(BF)
        up_rows = dot(pick, up_grad).astype(BF)
        dx = dot(gate_rows, gate) + dot(up_rows, up)
        tail = dot(pick, split_tail(jnp.sum(prob_term, axis=1, keepdims=True)).astype(BF))
        grad_prob = tail[:, 0:1] + tail[:, 1:2]
        half = side // 2
        out_at = pl.ds(start // 2 if single else pl.multiple_of(start // 2, 16), half)
        write_rows(own_ref.at[out_at], dx[:half], grad_prob[:half])
        write_rows(send_ref.at[out_at], dx[half:], grad_prob[half:])

    each_block(total, side, block)
    if not single:
        for j in range(3):
            grad_ref[j] = sum_ref[j].astype(BF)
            stores[j].start()
    for store in stores:
        store.wait()


def add_kernel(z_count, hot_own_ref, hot_got_ref, cold_own_ref, cold_got_ref, *refs):
    outs, (cold_ref, cold_prob_ref) = refs[:-2], refs[-2:]
    z = lax.axis_index("dp") // 4
    hot, hot_prob = read_rows(hot_own_ref[...])
    hot_got, hot_got_prob = read_rows(hot_got_ref[...])
    hot, hot_prob = hot + hot_got, hot_prob + hot_got_prob
    cold, cold_prob = read_rows(cold_own_ref[...])
    cold_got, cold_got_prob = read_rows(cold_got_ref[...])
    cold_ref[...] = cold + cold_got
    cold_prob_ref[...] = tail_lanes(cold_prob + cold_got_prob)
    for k, out_ref in enumerate(outs):
        at = slice(k * HALF, (k + 1) * HALF)
        cold_at = pl.ds(pl.multiple_of(8 * ((z + z_count - k) % z_count), 8), 8)
        rows = jnp.concatenate([hot[at], cold_ref[cold_at, :]], axis=0)
        prob = jnp.concatenate([hot_prob[at], cold_prob_ref[cold_at, :][:, 0:1]], axis=0)
        write_rows(out_ref, rows, prob)


def combine_kernel(z_count, *refs):
    *parts, own_ref, send_y_ref, send_x_ref = refs
    x = (lax.axis_index("dp") // 2) % 2
    hot, cold = 0.0, []
    for ref in parts:
        rows, prob = read_rows(ref[...])
        both = jnp.concatenate([rows, tail_lanes(prob)], axis=1)
        hot = hot + both[:HALF]
        part = both[HALF:]
        cold.append(jnp.where(x == 0, part, pltpu.roll(part, CAP, 0)))
    low = (iota(cold[0].shape, 0) & 4) == 0
    mine, other = [], []
    for even, odd in zip(cold[0::2], cold[1::2]):
        mine.append(jnp.where(low, even, pltpu.roll(odd, CAP, 0)))
        other.append(jnp.where(low, pltpu.roll(even, CAP, 0), odd))
    rows = jnp.concatenate([hot] + mine, axis=0)
    away = jnp.concatenate(other, axis=0)
    width = rows.shape[1] - TAIL
    own_ref[...] = rows
    write_rows(send_y_ref, rows[:, :width], rows[:, width : width + 1])
    write_rows(send_x_ref, away[:, :width], away[:, width : width + 1])


def finish_kernel(base, z_count, own_ref, y_ref, x_ref, xy_ref, pos_ref, dx_ref, prob_ref):
    pair = lax.axis_index("pair")
    me = lax.axis_index("dp")
    z, x = me // 4, (me // 2) % 2
    half = dx_ref.shape[0]
    pos = jnp.where(pair == 0, pos_ref[:, :half], pos_ref[:, half:])

    def cold_target(row, side):
        owner = z + (row >> 2)
        owner = jnp.where(owner >= z_count, owner - z_count, owner)
        return (2 * owner + side) * CAP + (row & 3)

    def with_hot(side):
        row = iota((own_ref.shape[0], half), 0)
        return jnp.where(row < HALF, base + HALF * side + row, cold_target(row - HALF, x))

    away = cold_target(iota((x_ref.shape[0], half), 0), 1 - x)
    total = 0.0
    grad_prob = [0.0] * TOP
    for ref, target in (
        (own_ref, with_hot(pair)),
        (y_ref, with_hot(1 - pair)),
        (x_ref, away),
        (xy_ref, away),
    ):
        routes = [pos[k : k + 1, :] == target for k in range(TOP)]
        onehot = jnp.where(routes[0] | routes[1], 1.0, 0.0).astype(BF)
        rows, prob = read_rows(ref[...])
        high = rows.astype(BF)
        total = total + dot(onehot, high, TN)
        if ref.dtype == F32:
            total = total + dot(onehot, (rows - high.astype(F32)).astype(BF), TN)
        for k in range(TOP):
            terms = jnp.sum(jnp.where(routes[k], prob, 0.0), axis=0, keepdims=True)
            grad_prob[k] = grad_prob[k] + terms
    dx_ref[...] = total.astype(BF)
    for k in range(TOP):
        prob_ref[k : k + 1, :] = grad_prob[k]


def part_kernel(own_ref, a_ref, b_ref, out_ref):
    out_ref[...] = own_ref[...] + a_ref[...].astype(F32) + b_ref[...].astype(F32)


def sum_kernel(part_ref, last_ref, gate_ref, up_ref, down_ref):
    total = part_ref[...] + last_ref[...].astype(F32)
    units = gate_ref.shape[0]
    for index, out_ref in enumerate((gate_ref, up_ref, down_ref)):
        out_ref[...] = total[index * units : (index + 1) * units].astype(BF)


def call(kernel, outs, name, flops, scratch=(), smem=(), hbm=(), out_hbm=(), limit=0):
    def run(*args):
        def space(index, far, smem=()):
            return pltpu.SMEM if index in smem else pltpu.HBM if index in far else pltpu.VMEM

        moved = sum(a.size * a.dtype.itemsize for a in args)
        moved += sum(o.size * o.dtype.itemsize for o in outs)
        return pl.pallas_call(
            kernel,
            out_shape=outs,
            in_specs=[pl.BlockSpec(memory_space=space(i, hbm, smem)) for i in range(len(args))],
            out_specs=[pl.BlockSpec(memory_space=space(i, out_hbm)) for i in range(len(outs))],
            scratch_shapes=[pltpu.VMEM(*s) if isinstance(s, tuple) else s for s in scratch],
            compiler_params=pltpu.CompilerParams(
                vmem_limit_bytes=limit or min(VMEM_LIMIT, VMEM_BASE + 3 * moved)
            ),
            cost_estimate=pl.CostEstimate(flops=flops, bytes_accessed=moved, transcendentals=0),
            name=name,
        )(*args)

    return run


def local(
    tokens,
    grad_out,
    gate_probs,
    expert_ids,
    route_slots,
    hot_flags,
    owner_slot,
    cold_gate,
    cold_up,
    cold_down,
    hot_gate,
    hot_up,
    hot_down,
):
    count = lax.axis_size("dp")
    z_count = count // 4
    chunk_count = 2 * z_count
    token_count, width = tokens.shape
    lanes = width + TAIL
    units = hot_gate.shape[0]
    base = (count // 2) * CAP
    shape = jax.ShapeDtypeStruct
    half = token_count // 2
    pad = -units % 8

    def swap(value, mask):
        flip_dp, flip_pair = 2 * (mask & 1), mask >> 1
        perm = [
            (2 * i + p, 2 * (i ^ flip_dp) + (p ^ flip_pair)) for i in range(count) for p in range(2)
        ]
        return lax.ppermute(value, ("dp", "pair"), perm)

    def along_z(value, k):
        perm = [(i, 4 * ((i // 4 + k) % z_count) + i % 4) for i in range(count)]
        return lax.ppermute(value, "dp", perm)

    def other_core(value):
        return lax.ppermute(value, "dp", [(i, i ^ 1) for i in range(count)])

    hot_weights = [jnp.pad(w, ((0, pad), (0, 0))) if pad else w for w in (hot_gate, hot_up, hot_down)]
    units_padded = units + pad
    used = 3 * units_padded
    chips = count // 2
    cold_rows = chips * 2 * CAP
    probs_t = gate_probs.T
    hot_chunk, hot_own, pos = call(
        functools.partial(hot_dispatch_kernel, base),
        [
            shape((HCAP, lanes), BF),
            shape((used, width), BF),
            shape((TOP, token_count), jnp.int32),
        ],
        "hot_dispatch",
        4 * HCAP * token_count * width,
        smem=(5, 6),
        limit=VMEM_LIMIT,
    )(tokens, grad_out, probs_t, expert_ids.T, route_slots.T, hot_flags, owner_slot, *hot_weights)
    (cold_send,) = call(
        cold_dispatch_kernel,
        [shape((cold_rows, lanes), BF)],
        "cold_dispatch",
        4 * cold_rows * token_count * width,
        limit=VMEM_LIMIT,
    )(tokens, grad_out, probs_t, pos)

    chunks = [hot_chunk] + [along_z(hot_chunk, k) for k in range(1, z_count)]
    by_pair = swap(hot_own, 2)
    by_x = swap(hot_own, 1)
    first_out, by_pair_out, _ = lax.optimization_barrier((hot_chunk, by_pair, chunks[1]))
    weights = [hot_own, by_x, by_pair, swap(by_pair_out, 1)]

    same_core = [[2 * chip + core for chip in range(chips)] for core in range(2)]
    cold_mine = lax.all_to_all(
        cold_send.reshape(chips, 2 * CAP, lanes),
        "dp",
        split_axis=0,
        concat_axis=0,
        tiled=True,
        axis_index_groups=same_core,
    ).reshape(cold_rows, lanes)
    cold_other = other_core(cold_mine)
    chunks = chunks + [other_core(first_out)] + [other_core(chunk) for chunk in chunks[1:]]

    cold_units = cold_gate.shape[1]
    cold_shape = shape(cold_gate.shape, BF)
    cold_own, cold_out, grad_cold_gate, grad_cold_up, grad_cold_down = call(
        cold_kernel,
        [shape((cold_rows // 2, lanes), F32), shape((cold_rows // 2, lanes), BF)] + [cold_shape] * 3,
        "cold",
        14 * 2 * cold_rows * cold_units * width,
        scratch=[
            ((3, cold_units, width), BF),
            ((3, cold_units, width), BF),
            ((3, cold_units, width) if cold_rows > COLD_BLOCK else (8, 128), F32),
            pltpu.SemaphoreType.DMA((3,)),
            pltpu.SemaphoreType.DMA((3,)),
        ],
        hbm=(2, 3, 4),
        out_hbm=(2, 3, 4),
    )(cold_mine, cold_other, cold_gate, cold_up, cold_down)

    all_rows = chunk_count * HCAP
    half_rows = chunk_count * HALF // 2
    term = shape((used, width), BF)
    hot_dx, hot_dx_out, own_term, *sent_terms = call(
        functools.partial(hot_kernel, chunk_count, units_padded),
        [
            shape((half_rows, lanes), F32),
            shape((half_rows, lanes), BF),
            shape(term.shape, F32),
            term,
            term,
            term,
        ],
        "hot",
        5 * all_rows * 4 * UNIT_BLOCK * width,
        scratch=[
            ((all_rows, width), BF),
            ((all_rows, TAIL), BF),
            ((4 * UNIT_BLOCK, width), BF),
            ((4, used, width) if chunk_count > CHUNK_BLOCK else (8, 128), F32),
        ],
    )(*chunks, *weights)

    hot_got, cold_got = other_core(hot_dx_out), other_core(cold_out)
    message = HALF + 2 * CAP
    parts = call(
        functools.partial(add_kernel, z_count),
        [shape((message, lanes), F32)] + [shape((message, lanes), BF)] * (z_count - 1),
        "add_cores",
        2 * half_rows * lanes,
        scratch=[((cold_rows // 2, width), F32), ((cold_rows // 2, TAIL), F32)],
    )(hot_dx, hot_got, cold_own, cold_got)
    parts = [parts[0]] + [along_z(parts[k], -k) for k in range(1, z_count)]

    got_x, got_y = swap(sent_terms[0], 1), swap(sent_terms[1], 2)
    last_term, _ = lax.optimization_barrier((sent_terms[2], parts[-1]))
    got_xy = swap(last_term, 3)
    (part_term,) = call(part_kernel, [shape(term.shape, F32)], "hot_part", 2 * used * width)(
        own_term, got_x, got_y
    )
    own_part, part_term = lax.optimization_barrier((parts[0], part_term))

    cold_back = z_count * CAP
    own_rows, send_y, send_x = call(
        functools.partial(combine_kernel, z_count),
        [
            shape((HALF + cold_back, lanes), F32),
            shape((HALF + cold_back, lanes), BF),
            shape((cold_back, lanes), BF),
        ],
        "combine",
        z_count * message * lanes,
    )(own_part, *parts[1:])
    rows_y, rows_x, rows_xy = swap(send_y, 2), swap(send_x, 1), swap(send_x, 3)
    dx, prob_t = call(
        functools.partial(finish_kernel, base, z_count),
        [shape((half, width), BF), shape((TOP, half), F32)],
        "finish",
        6 * (HALF + 2 * cold_back) * half * width,
    )(own_rows, rows_y, rows_x, rows_xy, pos)

    out_shape = shape((units_padded, width), BF)
    hot_grads = call(sum_kernel, [out_shape] * 3, "hot_sum", 4 * used * width)(part_term, got_xy)
    if pad:
        hot_grads = [value[:units] for value in hot_grads]
    return (dx, prob_t.T, grad_cold_gate, grad_cold_up, grad_cold_down, *hot_grads)


def solution(mesh):
    return jax.shard_map(
        local,
        mesh=mesh,
        in_specs=(
            P("dp", None),
            P("dp", None),
            P("dp", None),
            P("dp", None),
            P("dp", None),
            P(),
            P(),
            P("dp", "pair", None),
            P("dp", "pair", None),
            P("dp", "pair", None),
            P(("dp", "pair"), None),
            P(("dp", "pair"), None),
            P(("dp", "pair"), None),
        ),
        out_specs=(
            P(("dp", "pair"), None),
            P(("dp", "pair"), None),
            P("dp", "pair", None),
            P("dp", "pair", None),
            P("dp", "pair", None),
            P(("dp", "pair"), None),
            P(("dp", "pair"), None),
            P(("dp", "pair"), None),
        ),
        check_vma=False,
    )
```

```python
import functools

import jax
import jax.numpy as jnp
from jax import lax
from jax.experimental import pallas as pl
from jax.experimental.pallas import tpu as pltpu
from jax.sharding import PartitionSpec as P

TOP = 2
CAP = 4
HCAP = 48
HALF = HCAP // 2
TAIL = 128
CHUNK_BLOCK = 8
COLD_BLOCK = 64
UNIT_BLOCK = 128
BF = jnp.bfloat16
F32 = jnp.float32
VMEM_LIMIT = 56 * 1024 * 1024
VMEM_BASE = 6 * 1024 * 1024

NT = (((1,), (1,)), ((), ()))
TN = (((0,), (0,)), ((), ()))


def dot(a, b, dims=(((1,), (0,)), ((), ()))):
    return lax.dot_general(a, b, dims, preferred_element_type=F32)


def iota(shape, dim):
    return lax.broadcasted_iota(jnp.int32, shape, dim)


def positions(ids, slots, flags_ref, owner_ref, base):
    hot = jnp.zeros_like(ids)
    own = jnp.zeros_like(ids)
    for e in range(flags_ref.shape[0]):
        named = ids == e
        hot = jnp.where(named, flags_ref[e], hot)
        own = jnp.where(named, owner_ref[e], own)
    cold_pos = jnp.where(slots < CAP, own * CAP + slots, -1)
    hot_pos = jnp.where(slots < HCAP, base + slots, -1)
    return jnp.where(hot == 1, hot_pos, cold_pos)


def tail_lanes(first, second=None):
    lane = iota((first.shape[0], TAIL), 1)
    out = jnp.where(lane == 0, first, 0.0)
    if second is not None:
        out = jnp.where(lane == 1, second, out)
    return out


def split_tail(value):
    high = value.astype(BF).astype(F32)
    return tail_lanes(high, value - high)


def each_block(total, size, body):
    if total == size:
        body(0)
    else:

        def step(block, carry):
            body(pl.multiple_of(block * size, size))
            return carry

        lax.fori_loop(0, total // size, step, 0)


def add_to(ref, value, single):
    if single:
        ref[...] = value.astype(ref.dtype)
    else:
        ref[...] += value


def gather_rows(out_ref, start, target, is_grad, pos, prob, tok_ref, grad_ref):
    width = tok_ref.shape[1]
    at = pl.ds(start, target.shape[0])
    first = pos[0:1, :] == target
    second = pos[1:2, :] == target
    chosen = jnp.where(first | second, 1.0, 0.0)
    rows = dot(jnp.where(is_grad, 0.0, chosen).astype(BF), tok_ref[...]) + dot(
        jnp.where(is_grad, chosen, 0.0).astype(BF), grad_ref[...]
    )
    out_ref[at, :width] = rows.astype(BF)
    weight = jnp.where(first, prob[0:1, :], 0.0) + jnp.where(second, prob[1:2, :], 0.0)
    weight = jnp.sum(jnp.where(is_grad, 0.0, weight), axis=1, keepdims=True)
    out_ref[at, width:] = tail_lanes(weight).astype(BF)


def hot_dispatch_kernel(base, *refs):
    tok_ref, grad_ref, prob_ref, ids_ref, slot_ref, flags_ref, owner_ref = refs[:7]
    hot_ref, pos_ref = refs[7:]
    pair = lax.axis_index("pair")
    pos = positions(ids_ref[...], slot_ref[...], flags_ref, owner_ref, base)
    pos_ref[...] = pos
    row = iota((HCAP, tok_ref.shape[0]), 0)
    target = base + HALF * pair + jnp.where(row >= HALF, row - HALF, row)
    prob = prob_ref[...].astype(F32)
    gather_rows(hot_ref, 0, target, row >= HALF, pos, prob, tok_ref, grad_ref)


def cold_dispatch_kernel(
    tok_ref, grad_ref, prob_ref, pos_ref, gate_ref, up_ref, down_ref, cold_ref, weight_ref
):
    joined = [ref[...].astype(F32) for ref in (gate_ref, up_ref, down_ref)]
    weight_ref[...] = jnp.concatenate(joined, axis=0).astype(BF)
    pos = pos_ref[...]
    prob = prob_ref[...].astype(F32)

    def block(start):
        row = start + iota((COLD_BLOCK, tok_ref.shape[0]), 0)
        target = (row >> 3) * CAP + (row & 3)
        gather_rows(cold_ref, start, target, (row & 4) != 0, pos, prob, tok_ref, grad_ref)

    each_block(cold_ref.shape[0], COLD_BLOCK, block)


def swiglu_back(pre_gate, pre_up, back, prob):
    sig = 1.0 / (1.0 + jnp.exp(-pre_gate))
    act = pre_gate * sig
    hidden = act * pre_up
    scaled = prob * back
    gate_grad = scaled * pre_up * sig * (1.0 + pre_gate * (1.0 - sig))
    return gate_grad, scaled * act, prob * hidden, hidden * back


def write_rows(out_ref, rows, prob):
    width = rows.shape[1]
    out_ref[:, :width] = rows.astype(out_ref.dtype)
    tail = tail_lanes(prob) if out_ref.dtype == F32 else split_tail(prob).astype(BF)
    out_ref[:, width:] = tail


def read_rows(value):
    value = value.astype(F32)
    width = value.shape[1] - TAIL
    return value[:, :width], value[:, width : width + 1] + value[:, width + 1 : width + 2]


def hot_kernel(chunk_count, units, *refs):
    chunks = refs[:chunk_count]
    weights = refs[chunk_count : chunk_count + 4]
    own_ref, send_ref, *terms = refs[chunk_count + 4 : chunk_count + 10]
    rows_ref, tail_ref, wide_ref, sum_ref = refs[chunk_count + 10 :]
    width = rows_ref.shape[1]
    for k, chunk in enumerate(chunks):
        rows_ref[k * HCAP : (k + 1) * HCAP, :] = chunk[:, :width]
        tail_ref[k * HCAP : (k + 1) * HCAP, :] = chunk[:, width:]
    used = 3 * units
    for j, w_ref in enumerate(weights):
        start = j * UNIT_BLOCK
        clear = used // 16 * 16
        if clear < UNIT_BLOCK:
            wide_ref[start + clear : start + UNIT_BLOCK, :] = jnp.zeros((UNIT_BLOCK - clear, width), BF)
        wide_ref[start : start + used, :] = w_ref[...]
    columns = 4 * UNIT_BLOCK
    block_chunks = min(CHUNK_BLOCK, chunk_count)
    block_rows = block_chunks * HCAP
    half_rows = block_rows // 2
    single = block_chunks == chunk_count

    def block(start):
        at = pl.ds(start, block_rows)
        prob = tail_ref[at, :].astype(F32).reshape(block_chunks, HCAP, TAIL)[:, :HALF, 0:1]
        prob = prob.reshape(half_rows, 1)
        pre = dot(rows_ref[at, :], wide_ref[...], NT).reshape(block_chunks, HCAP, columns)
        pre_x = pre[:, :HALF].reshape(half_rows, columns)
        pre_g = pre[:, HALF:].reshape(half_rows, columns)
        first = (iota(pre_x.shape, 1) & (UNIT_BLOCK - 1)) < units
        gate_grad, up_grad, weighted, prob_term = swiglu_back(
            pre_x,
            pltpu.roll(pre_x, columns - units, 1),
            pltpu.roll(pre_g, columns - 2 * units, 1),
            prob,
        )
        gate_grad, up_grad, weighted, prob_term = (
            jnp.where(first, value, 0.0) for value in (gate_grad, up_grad, weighted, prob_term)
        )
        grad_prob = jnp.sum(prob_term, axis=1, keepdims=True)
        x_side = gate_grad + pltpu.roll(up_grad, units, 1)
        g_side = pltpu.roll(weighted, 2 * units, 1)
        both = jnp.concatenate(
            [x_side.reshape(block_chunks, HALF, columns), g_side.reshape(block_chunks, HALF, columns)],
            axis=1,
        )
        both = both.reshape(block_rows, columns).astype(BF)
        dx = dot(x_side.astype(BF), wide_ref[...])
        for j in range(4):
            term = dot(both[:, j * UNIT_BLOCK : (j + 1) * UNIT_BLOCK], rows_ref[at, :], TN)
            add_to(terms[j] if single else sum_ref.at[j], term[:used], single)
        return dx, grad_prob

    if single:
        dx, grad_prob = block(0)
        write_rows(own_ref, dx[: half_rows // 2], grad_prob[: half_rows // 2])
        write_rows(send_ref, dx[half_rows // 2 :], grad_prob[half_rows // 2 :])
    else:
        sum_ref[...] = jnp.zeros_like(sum_ref)
        for out_ref, offset in ((own_ref, 0), (send_ref, chunk_count * HCAP // 2)):

            def step(index, carry, out_ref=out_ref, offset=offset):
                dx, grad_prob = block(pl.multiple_of(offset + index * block_rows, 16))
                at = pl.ds(pl.multiple_of(index * half_rows, 16), half_rows)
                write_rows(out_ref.at[at], dx, grad_prob)
                return carry

            lax.fori_loop(0, chunk_count // block_chunks // 2, step, 0)
        for j, out_ref in enumerate(terms):
            out_ref[...] = sum_ref[j].astype(out_ref.dtype)


def cold_kernel(
    mine_ref, other_ref, gate_hbm, up_hbm, down_hbm, own_ref, send_ref, *refs
):
    outs, (w_ref, grad_ref, sum_ref, in_sem, out_sem) = refs[:3], refs[3:]
    total, width = mine_ref.shape[0], gate_hbm.shape[2]
    side = COLD_BLOCK
    rows = 2 * side
    single = side == total
    loads = [
        pltpu.make_async_copy(ref.at[0], w_ref.at[j], in_sem.at[j])
        for j, ref in enumerate((gate_hbm, up_hbm, down_hbm))
    ]
    stores = [
        pltpu.make_async_copy(grad_ref.at[j], ref.at[0], out_sem.at[j]) for j, ref in enumerate(outs)
    ]
    for load in loads:
        load.start()
    if not single:
        sum_ref[...] = jnp.zeros_like(sum_ref)
        for load in loads:
            load.wait()

    def weight(j):
        if single:
            loads[j].wait()
        return w_ref[j]

    def block(start):
        at = pl.ds(start, side)
        both = jnp.concatenate([mine_ref[at, :], other_ref[at, :]], axis=0)
        data = both[:, :width]
        prob = both[:, width:].astype(F32)[:, 0:1]
        gate = weight(0)
        pre_gate = dot(data, gate, NT)
        up = weight(1)
        pre_up = dot(data, up, NT)
        back = pltpu.roll(dot(data, weight(2), NT), rows - CAP, 0)
        gate_grad, up_grad, weighted, prob_term = swiglu_back(pre_gate, pre_up, back, prob)
        x_row = (iota(pre_gate.shape, 0) & 4) == 0
        gate_grad = jnp.where(x_row, gate_grad, 0.0).astype(BF)
        up_grad = jnp.where(x_row, up_grad, 0.0).astype(BF)
        weighted = pltpu.roll(jnp.where(x_row, weighted, 0.0), CAP, 0).astype(BF)
        prob_term = jnp.where(x_row, prob_term, 0.0)
        for j, grad in enumerate((gate_grad, up_grad, weighted)):
            term = dot(grad, data, TN)
            if single:
                grad_ref[j] = term.astype(BF)
                stores[j].start()
            else:
                sum_ref[j] += term
        shape = (side, rows)
        row, col = iota(shape, 0), iota(shape, 1)
        pick = jnp.where(col == (row >> 2) * 8 + (row & 3), 1.0, 0.0).astype(BF)
        gate_rows = dot(pick, gate_grad).astype(BF)
        up_rows = dot(pick, up_grad).astype(BF)
        dx = dot(gate_rows, gate) + dot(up_rows, up)
        tail = dot(pick, split_tail(jnp.sum(prob_term, axis=1, keepdims=True)).astype(BF))
        grad_prob = tail[:, 0:1] + tail[:, 1:2]
        half = side // 2
        out_at = pl.ds(start // 2 if single else pl.multiple_of(start // 2, 16), half)
        write_rows(own_ref.at[out_at], dx[:half], grad_prob[:half])
        write_rows(send_ref.at[out_at], dx[half:], grad_prob[half:])

    each_block(total, side, block)
    if not single:
        for j in range(3):
            grad_ref[j] = sum_ref[j].astype(BF)
            stores[j].start()
    for store in stores:
        store.wait()


def add_kernel(z_count, hot_own_ref, hot_got_ref, cold_own_ref, cold_got_ref, out_ref, hot_ref):
    z = lax.axis_index("dp") // 4
    width = hot_ref.shape[1] - TAIL

    def added(own_ref, got_ref):
        rows, prob = read_rows(own_ref[...])
        got_rows, got_prob = read_rows(got_ref[...])
        return jnp.concatenate([rows + got_rows, tail_lanes(prob + got_prob)], axis=1)

    hot = added(hot_own_ref, hot_got_ref)
    for k in range(z_count):
        hot_ref[pl.ds(pl.multiple_of((z ^ k) * HALF, 8), HALF), :] = hot[k * HALF : (k + 1) * HALF]
    cold = added(cold_own_ref, cold_got_ref)
    message = HALF + 2 * CAP
    parts = []
    for k in range(z_count):
        parts += [hot_ref[k * HALF : (k + 1) * HALF, :], cold[k * 2 * CAP : (k + 1) * 2 * CAP]]
    rows = jnp.concatenate(parts, axis=0)
    write_rows(out_ref, rows[:, :width], rows[:, width : width + 1])


def combine_kernel(z_count, got_ref, own_ref, send_y_ref, send_x_ref):
    x = (lax.axis_index("dp") // 2) % 2
    message = HALF + 2 * CAP
    rows, prob = read_rows(got_ref[...])
    both = jnp.concatenate([rows, tail_lanes(prob)], axis=1)
    hot, cold = 0.0, []
    for k in range(z_count):
        hot = hot + both[k * message : k * message + HALF]
        part = both[k * message + HALF : (k + 1) * message]
        cold.append(jnp.where(x == 0, part, pltpu.roll(part, CAP, 0)))
    low = (iota(cold[0].shape, 0) & 4) == 0
    mine, other = [], []
    for even, odd in zip(cold[0::2], cold[1::2]):
        mine.append(jnp.where(low, even, pltpu.roll(odd, CAP, 0)))
        other.append(jnp.where(low, pltpu.roll(even, CAP, 0), odd))
    rows = jnp.concatenate([hot] + mine, axis=0)
    away = jnp.concatenate(other, axis=0)
    width = rows.shape[1] - TAIL
    own_ref[...] = rows
    write_rows(send_y_ref, rows[:, :width], rows[:, width : width + 1])
    write_rows(send_x_ref, away[:, :width], away[:, width : width + 1])


def finish_kernel(base, own_ref, y_ref, x_ref, xy_ref, pos_ref, dx_ref, prob_ref):
    pair = lax.axis_index("pair")
    x = (lax.axis_index("dp") // 2) % 2
    half = dx_ref.shape[0]
    pos = jnp.where(pair == 0, pos_ref[:, :half], pos_ref[:, half:])

    def cold_target(row, side):
        return (2 * (row >> 2) + side) * CAP + (row & 3)

    def with_hot(side):
        row = iota((own_ref.shape[0], half), 0)
        return jnp.where(row < HALF, base + HALF * side + row, cold_target(row - HALF, x))

    away = cold_target(iota((x_ref.shape[0], half), 0), 1 - x)
    total = 0.0
    grad_prob = [0.0] * TOP
    for ref, target in (
        (own_ref, with_hot(pair)),
        (y_ref, with_hot(1 - pair)),
        (x_ref, away),
        (xy_ref, away),
    ):
        routes = [pos[k : k + 1, :] == target for k in range(TOP)]
        onehot = jnp.where(routes[0] | routes[1], 1.0, 0.0).astype(BF)
        rows, prob = read_rows(ref[...])
        high = rows.astype(BF)
        total = total + dot(onehot, high, TN)
        if ref.dtype == F32:
            total = total + dot(onehot, (rows - high.astype(F32)).astype(BF), TN)
        for k in range(TOP):
            terms = jnp.sum(jnp.where(routes[k], prob, 0.0), axis=0, keepdims=True)
            grad_prob[k] = grad_prob[k] + terms
    dx_ref[...] = total.astype(BF)
    for k in range(TOP):
        prob_ref[k : k + 1, :] = grad_prob[k]


def sum_kernel(own_ref, a_ref, b_ref, c_ref, gate_ref, up_ref, down_ref):
    total = own_ref[...] + a_ref[...].astype(F32) + b_ref[...].astype(F32) + c_ref[...].astype(F32)
    units = gate_ref.shape[0]
    for index, out_ref in enumerate((gate_ref, up_ref, down_ref)):
        out_ref[...] = total[index * units : (index + 1) * units].astype(BF)


def call(kernel, outs, name, flops, scratch=(), smem=(), hbm=(), out_hbm=(), limit=0):
    def run(*args):
        def space(index, far, smem=()):
            return pltpu.SMEM if index in smem else pltpu.HBM if index in far else pltpu.VMEM

        moved = sum(a.size * a.dtype.itemsize for a in args)
        moved += sum(o.size * o.dtype.itemsize for o in outs)
        return pl.pallas_call(
            kernel,
            out_shape=outs,
            in_specs=[pl.BlockSpec(memory_space=space(i, hbm, smem)) for i in range(len(args))],
            out_specs=[pl.BlockSpec(memory_space=space(i, out_hbm)) for i in range(len(outs))],
            scratch_shapes=[pltpu.VMEM(*s) if isinstance(s, tuple) else s for s in scratch],
            compiler_params=pltpu.CompilerParams(
                vmem_limit_bytes=limit or min(VMEM_LIMIT, VMEM_BASE + 3 * moved)
            ),
            cost_estimate=pl.CostEstimate(flops=flops, bytes_accessed=moved, transcendentals=0),
            name=name,
        )(*args)

    return run


def local(
    tokens,
    grad_out,
    gate_probs,
    expert_ids,
    route_slots,
    hot_flags,
    owner_slot,
    cold_gate,
    cold_up,
    cold_down,
    hot_gate,
    hot_up,
    hot_down,
):
    count = lax.axis_size("dp")
    z_count = count // 4
    chunk_count = 2 * z_count
    token_count, width = tokens.shape
    lanes = width + TAIL
    units = hot_gate.shape[0]
    base = (count // 2) * CAP
    shape = jax.ShapeDtypeStruct
    half = token_count // 2
    pad = -units % 8

    def swap(value, mask):
        flip_dp, flip_pair = 2 * (mask & 1), mask >> 1
        perm = [
            (2 * i + p, 2 * (i ^ flip_dp) + (p ^ flip_pair)) for i in range(count) for p in range(2)
        ]
        return lax.ppermute(value, ("dp", "pair"), perm)

    def along_z(value, k):
        perm = [(i, 4 * ((i // 4) ^ k) + i % 4) for i in range(count)]
        return lax.ppermute(value, "dp", perm)

    def other_core(value):
        return lax.ppermute(value, "dp", [(i, i ^ 1) for i in range(count)])

    hot_weights = [jnp.pad(w, ((0, pad), (0, 0))) if pad else w for w in (hot_gate, hot_up, hot_down)]
    units_padded = units + pad
    used = 3 * units_padded
    chips = count // 2
    cold_rows = chips * 2 * CAP
    probs_t = gate_probs.T
    hot_chunk, pos = call(
        functools.partial(hot_dispatch_kernel, base),
        [shape((HCAP, lanes), BF), shape((TOP, token_count), jnp.int32)],
        "hot_dispatch",
        4 * HCAP * token_count * width,
        smem=(5, 6),
        limit=VMEM_LIMIT,
    )(tokens, grad_out, probs_t, expert_ids.T, route_slots.T, hot_flags, owner_slot)
    cold_send, hot_own = call(
        cold_dispatch_kernel,
        [shape((cold_rows, lanes), BF), shape((used, width), BF)],
        "cold_dispatch",
        4 * cold_rows * token_count * width,
        limit=VMEM_LIMIT,
    )(tokens, grad_out, probs_t, pos, *hot_weights)

    chunks = [hot_chunk] + [along_z(hot_chunk, k) for k in range(1, z_count)]
    by_pair = swap(hot_own, 2)
    by_x = swap(hot_own, 1)
    first_out, by_pair_out, _ = lax.optimization_barrier((hot_chunk, by_pair, chunks[1]))
    weights = [hot_own, by_x, by_pair, swap(by_pair_out, 1)]

    same_core = [[2 * chip + core for chip in range(chips)] for core in range(2)]
    cold_mine = lax.all_to_all(
        cold_send.reshape(chips, 2 * CAP, lanes),
        "dp",
        split_axis=0,
        concat_axis=0,
        tiled=True,
        axis_index_groups=same_core,
    ).reshape(cold_rows, lanes)
    cold_mine, _ = lax.optimization_barrier((cold_mine, chunks[2]))
    cold_other = other_core(cold_mine)
    chunks = chunks + [other_core(first_out)] + [other_core(chunk) for chunk in chunks[1:]]

    cold_units = cold_gate.shape[1]
    cold_shape = shape(cold_gate.shape, BF)
    cold_own, cold_out, grad_cold_gate, grad_cold_up, grad_cold_down = call(
        cold_kernel,
        [shape((cold_rows // 2, lanes), F32), shape((cold_rows // 2, lanes), BF)] + [cold_shape] * 3,
        "cold",
        14 * 2 * cold_rows * cold_units * width,
        scratch=[
            ((3, cold_units, width), BF),
            ((3, cold_units, width), BF),
            ((3, cold_units, width) if cold_rows > COLD_BLOCK else (8, 128), F32),
            pltpu.SemaphoreType.DMA((3,)),
            pltpu.SemaphoreType.DMA((3,)),
        ],
        hbm=(2, 3, 4),
        out_hbm=(2, 3, 4),
    )(cold_mine, cold_other, cold_gate, cold_up, cold_down)

    weights[0], cold_own = lax.optimization_barrier((hot_own, cold_own))
    all_rows = chunk_count * HCAP
    half_rows = chunk_count * HALF // 2
    term = shape((used, width), BF)
    hot_dx, hot_dx_out, own_term, *sent_terms = call(
        functools.partial(hot_kernel, chunk_count, units_padded),
        [
            shape((half_rows, lanes), F32),
            shape((half_rows, lanes), BF),
            shape(term.shape, F32),
            term,
            term,
            term,
        ],
        "hot",
        5 * all_rows * 4 * UNIT_BLOCK * width,
        scratch=[
            ((all_rows, width), BF),
            ((all_rows, TAIL), BF),
            ((4 * UNIT_BLOCK, width), BF),
            ((4, used, width) if chunk_count > CHUNK_BLOCK else (8, 128), F32),
        ],
    )(*chunks, *weights)

    hot_got, cold_got = other_core(hot_dx_out), other_core(cold_out)
    message = HALF + 2 * CAP
    (parts,) = call(
        functools.partial(add_kernel, z_count),
        [shape((z_count * message, lanes), BF)],
        "add_cores",
        2 * half_rows * lanes,
        scratch=[((half_rows, lanes), F32)],
    )(hot_dx, hot_got, cold_own, cold_got)
    same_line = [[4 * z + other for z in range(z_count)] for other in range(4)]
    parts = lax.all_to_all(
        parts.reshape(z_count, message, lanes),
        "dp",
        split_axis=0,
        concat_axis=0,
        tiled=True,
        axis_index_groups=same_line,
    ).reshape(z_count * message, lanes)
    got_terms = [swap(value, mask) for value, mask in zip(sent_terms, (1, 2, 3))]

    cold_back = z_count * CAP
    own_rows, send_y, send_x = call(
        functools.partial(combine_kernel, z_count),
        [
            shape((HALF + cold_back, lanes), F32),
            shape((HALF + cold_back, lanes), BF),
            shape((cold_back, lanes), BF),
        ],
        "combine",
        z_count * message * lanes,
    )(parts)
    rows_y, rows_x, rows_xy = swap(send_y, 2), swap(send_x, 1), swap(send_x, 3)
    dx, prob_t = call(
        functools.partial(finish_kernel, base),
        [shape((half, width), BF), shape((TOP, half), F32)],
        "finish",
        6 * (HALF + 2 * cold_back) * half * width,
    )(own_rows, rows_y, rows_x, rows_xy, pos)

    out_shape = shape((units_padded, width), BF)
    hot_grads = call(sum_kernel, [out_shape] * 3, "hot_sum", 5 * used * width)(
        own_term, *got_terms
    )
    if pad:
        hot_grads = [value[:units] for value in hot_grads]
    return (dx, prob_t.T, grad_cold_gate, grad_cold_up, grad_cold_down, *hot_grads)


def solution(mesh):
    return jax.shard_map(
        local,
        mesh=mesh,
        in_specs=(
            P("dp", None),
            P("dp", None),
            P("dp", None),
            P("dp", None),
            P("dp", None),
            P(),
            P(),
            P("dp", "pair", None),
            P("dp", "pair", None),
            P("dp", "pair", None),
            P(("dp", "pair"), None),
            P(("dp", "pair"), None),
            P(("dp", "pair"), None),
        ),
        out_specs=(
            P(("dp", "pair"), None),
            P(("dp", "pair"), None),
            P("dp", "pair", None),
            P("dp", "pair", None),
            P("dp", "pair", None),
            P(("dp", "pair"), None),
            P(("dp", "pair"), None),
            P(("dp", "pair"), None),
        ),
        check_vma=False,
    )
```

```python
import functools

import jax
import jax.numpy as jnp
from jax import lax
from jax.experimental import pallas as pl
from jax.experimental.pallas import tpu as pltpu
from jax.sharding import PartitionSpec as P

TOP = 2
CAP = 4
HCAP = 48
HALF = HCAP // 2
TAIL = 128
CHUNK_BLOCK = 8
COLD_BLOCK = 64
COLD_ROWS = 128
UNIT_BLOCK = 128
BF = jnp.bfloat16
F32 = jnp.float32
VMEM_LIMIT = 56 * 1024 * 1024
VMEM_BASE = 12 * 1024 * 1024

NT = (((1,), (1,)), ((), ()))
TN = (((0,), (0,)), ((), ()))


def dot(a, b, dims=(((1,), (0,)), ((), ()))):
    return lax.dot_general(a, b, dims, preferred_element_type=F32)


def iota(shape, dim):
    return lax.broadcasted_iota(jnp.int32, shape, dim)


def positions(ids, slots, flags_ref, owner_ref, base):
    hot = jnp.zeros_like(ids)
    own = jnp.zeros_like(ids)
    for e in range(flags_ref.shape[0]):
        named = ids == e
        hot = jnp.where(named, flags_ref[e], hot)
        own = jnp.where(named, owner_ref[e], own)
    cold_pos = jnp.where(slots < CAP, own * CAP + slots, -1)
    hot_pos = jnp.where(slots < HCAP, base + slots, -1)
    return jnp.where(hot == 1, hot_pos, cold_pos)


def tail_lanes(first, second=None):
    lane = iota((first.shape[0], TAIL), 1)
    out = jnp.where(lane == 0, first, 0.0)
    if second is not None:
        out = jnp.where(lane == 1, second, out)
    return out


def split_tail(value):
    high = value.astype(BF).astype(F32)
    return tail_lanes(high, value - high)


def each_block(total, size, body):
    if total == size:
        body(0)
    else:

        def step(block, carry):
            body(pl.multiple_of(block * size, size))
            return carry

        lax.fori_loop(0, total // size, step, 0)


def add_to(ref, value, single):
    if single:
        ref[...] = value.astype(ref.dtype)
    else:
        ref[...] += value


def gather_rows(out_ref, start, target, is_grad, pos, prob, tok_ref, grad_ref):
    width = tok_ref.shape[1]
    at = pl.ds(start, target.shape[0])
    first = pos[0:1, :] == target
    second = pos[1:2, :] == target
    chosen = jnp.where(first | second, 1.0, 0.0)
    rows = dot(jnp.where(is_grad, 0.0, chosen).astype(BF), tok_ref[...]) + dot(
        jnp.where(is_grad, chosen, 0.0).astype(BF), grad_ref[...]
    )
    out_ref[at, :width] = rows.astype(BF)
    weight = jnp.where(first, prob[0:1, :], 0.0) + jnp.where(second, prob[1:2, :], 0.0)
    weight = jnp.sum(jnp.where(is_grad, 0.0, weight), axis=1, keepdims=True)
    out_ref[at, width:] = tail_lanes(weight).astype(BF)


def dispatch_kernel(base, *refs):
    tok_ref, grad_ref, prob_ref, ids_ref, slot_ref, flags_ref, owner_ref = refs[:7]
    gate_ref, up_ref, down_ref, pos_ref, weight_ref, *messages, cold_ref = refs[7:]
    pair = lax.axis_index("pair")
    me = lax.axis_index("dp")
    z, x = me // 4, (me // 2) % 2
    pos = positions(ids_ref[...], slot_ref[...], flags_ref, owner_ref, base)
    pos_ref[...] = pos
    joined = [ref[...].astype(F32) for ref in (gate_ref, up_ref, down_ref)]
    weight_ref[...] = jnp.concatenate(joined, axis=0).astype(BF)
    prob = prob_ref[...].astype(F32)

    def gather(out_ref, start, target, is_grad):
        gather_rows(out_ref, start, target, is_grad, pos, prob, tok_ref, grad_ref)

    row = iota((HCAP, tok_ref.shape[0]), 0)
    target = base + HALF * pair + jnp.where(row >= HALF, row - HALF, row)
    gather(messages[0], 0, target, row >= HALF)

    def block(start):
        row = start + iota((COLD_BLOCK, tok_ref.shape[0]), 0)
        chip = 2 * (z ^ (row >> 4)) + (x ^ ((row >> 3) & 1))
        gather(cold_ref, start, chip * CAP + (row & 3), (row & 4) != 0)

    each_block(cold_ref.shape[0], COLD_BLOCK, block)
    for k, message in enumerate(messages):
        if k:
            message[:HCAP, :] = messages[0][:HCAP, :]
        message[HCAP:, :] = cold_ref[k * 16 : (k + 1) * 16, :]


def away_kernel(*refs):
    *messages, out_ref = refs
    rows = [ref[HCAP:, :].astype(F32)[2 * CAP :] for ref in messages]
    out_ref[...] = jnp.concatenate(rows, axis=0).astype(BF)


def swiglu_back(pre_gate, pre_up, back, prob):
    sig = 1.0 / (1.0 + jnp.exp(-pre_gate))
    act = pre_gate * sig
    hidden = act * pre_up
    scaled = prob * back
    gate_grad = scaled * pre_up * sig * (1.0 + pre_gate * (1.0 - sig))
    return gate_grad, scaled * act, prob * hidden, hidden * back


def write_rows(out_ref, rows, prob):
    width = rows.shape[1]
    out_ref[:, :width] = rows.astype(out_ref.dtype)
    tail = tail_lanes(prob) if out_ref.dtype == F32 else split_tail(prob).astype(BF)
    out_ref[:, width:] = tail


def read_rows(value):
    value = value.astype(F32)
    width = value.shape[1] - TAIL
    return value[:, :width], value[:, width : width + 1] + value[:, width + 1 : width + 2]


def hot_kernel(chunk_count, units, *refs):
    chunks = refs[:chunk_count]
    weights = refs[chunk_count : chunk_count + 4]
    own_ref, send_ref, *terms = refs[chunk_count + 4 : chunk_count + 10]
    rows_ref, tail_ref, wide_ref, sum_ref = refs[chunk_count + 10 :]
    width = rows_ref.shape[1]
    for k, chunk in enumerate(chunks):
        rows_ref[k * HCAP : (k + 1) * HCAP, :] = chunk[:HCAP, :width]
        tail_ref[k * HCAP : (k + 1) * HCAP, :] = chunk[:HCAP, width:]
    used = 3 * units
    for j, w_ref in enumerate(weights):
        start = j * UNIT_BLOCK
        clear = used // 16 * 16
        if clear < UNIT_BLOCK:
            wide_ref[start + clear : start + UNIT_BLOCK, :] = jnp.zeros((UNIT_BLOCK - clear, width), BF)
        wide_ref[start : start + used, :] = w_ref[...]
    columns = 4 * UNIT_BLOCK
    block_chunks = min(CHUNK_BLOCK, chunk_count)
    block_rows = block_chunks * HCAP
    half_rows = block_rows // 2
    single = block_chunks == chunk_count

    def block(start):
        at = pl.ds(start, block_rows)
        prob = tail_ref[at, :].astype(F32).reshape(block_chunks, HCAP, TAIL)[:, :HALF, 0:1]
        prob = prob.reshape(half_rows, 1)
        pre = dot(rows_ref[at, :], wide_ref[...], NT).reshape(block_chunks, HCAP, columns)
        pre_x = pre[:, :HALF].reshape(half_rows, columns)
        pre_g = pre[:, HALF:].reshape(half_rows, columns)
        first = (iota(pre_x.shape, 1) & (UNIT_BLOCK - 1)) < units
        gate_grad, up_grad, weighted, prob_term = swiglu_back(
            pre_x,
            pltpu.roll(pre_x, columns - units, 1),
            pltpu.roll(pre_g, columns - 2 * units, 1),
            prob,
        )
        gate_grad, up_grad, weighted, prob_term = (
            jnp.where(first, value, 0.0) for value in (gate_grad, up_grad, weighted, prob_term)
        )
        grad_prob = jnp.sum(prob_term, axis=1, keepdims=True)
        x_side = gate_grad + pltpu.roll(up_grad, units, 1)
        g_side = pltpu.roll(weighted, 2 * units, 1)
        both = jnp.concatenate(
            [x_side.reshape(block_chunks, HALF, columns), g_side.reshape(block_chunks, HALF, columns)],
            axis=1,
        )
        both = both.reshape(block_rows, columns).astype(BF)
        dx = dot(x_side.astype(BF), wide_ref[...])
        for j in range(4):
            term = dot(both[:, j * UNIT_BLOCK : (j + 1) * UNIT_BLOCK], rows_ref[at, :], TN)
            add_to(terms[j] if single else sum_ref.at[j], term[:used], single)
        return dx, grad_prob

    if single:
        dx, grad_prob = block(0)
        write_rows(own_ref, dx[: half_rows // 2], grad_prob[: half_rows // 2])
        write_rows(send_ref, dx[half_rows // 2 :], grad_prob[half_rows // 2 :])
    else:
        sum_ref[...] = jnp.zeros_like(sum_ref)
        for out_ref, offset in ((own_ref, 0), (send_ref, chunk_count * HCAP // 2)):

            def step(index, carry, out_ref=out_ref, offset=offset):
                dx, grad_prob = block(pl.multiple_of(offset + index * block_rows, 16))
                at = pl.ds(pl.multiple_of(index * half_rows, 16), half_rows)
                write_rows(out_ref.at[at], dx, grad_prob)
                return carry

            lax.fori_loop(0, chunk_count // block_chunks // 2, step, 0)
        for j, out_ref in enumerate(terms):
            out_ref[...] = sum_ref[j].astype(out_ref.dtype)


def cold_kernel(message_count, *refs):
    messages = refs[:message_count]
    mine_x_ref, other_x_ref, gate_hbm, up_hbm, down_hbm = refs[message_count : message_count + 5]
    own_ref, send_ref, *outs = refs[message_count + 5 : message_count + 10]
    data_ref, dx_ref, w_ref, grad_ref, sum_ref, in_sem, out_sem = refs[message_count + 10 :]
    total, width = data_ref.shape[0], gate_hbm.shape[2]
    rows = COLD_ROWS
    single = rows == total
    loads = [
        pltpu.make_async_copy(ref.at[0], w_ref.at[j], in_sem.at[j])
        for j, ref in enumerate((gate_hbm, up_hbm, down_hbm))
    ]
    stores = [
        pltpu.make_async_copy(grad_ref.at[j], ref.at[0], out_sem.at[j]) for j, ref in enumerate(outs)
    ]
    for load in loads:
        load.start()
    quarter = total // 4
    z_count = message_count // 2
    for flip, away_ref in enumerate((mine_x_ref, other_x_ref)):
        near = [ref[HCAP:, :].astype(F32)[: 2 * CAP] for ref in messages[flip * z_count :][:z_count]]
        start = 2 * flip * quarter
        data_ref[start : start + quarter, :] = jnp.concatenate(near, axis=0).astype(BF)
        data_ref[start + quarter : start + 2 * quarter, :] = away_ref[...]
    if not single:
        sum_ref[...] = jnp.zeros_like(sum_ref)
        for load in loads:
            load.wait()

    def weight(j):
        if single:
            loads[j].wait()
        return w_ref[j]

    def block(start):
        at = pl.ds(start, rows)
        data = data_ref[at, :width]
        prob = data_ref[at, width:].astype(F32)[:, 0:1]
        gate = weight(0)
        pre_gate = dot(data, gate, NT)
        up = weight(1)
        pre_up = dot(data, up, NT)
        back = pltpu.roll(dot(data, weight(2), NT), rows - CAP, 0)
        gate_grad, up_grad, weighted, prob_term = swiglu_back(pre_gate, pre_up, back, prob)
        x_row = (iota(pre_gate.shape, 0) & 4) == 0
        gate_grad = jnp.where(x_row, gate_grad, 0.0).astype(BF)
        up_grad = jnp.where(x_row, up_grad, 0.0).astype(BF)
        weighted = pltpu.roll(jnp.where(x_row, weighted, 0.0), CAP, 0).astype(BF)
        prob_term = jnp.where(x_row, prob_term, 0.0)
        for j, grad in enumerate((gate_grad, up_grad, weighted)):
            term = dot(grad, data, TN)
            if single:
                grad_ref[j] = term.astype(BF)
                stores[j].start()
            else:
                sum_ref[j] += term
        shape = (rows // 2, rows)
        row, col = iota(shape, 0), iota(shape, 1)
        pick = jnp.where(col == (row >> 2) * 8 + (row & 3), 1.0, 0.0).astype(BF)
        gate_rows = dot(pick, gate_grad).astype(BF)
        up_rows = dot(pick, up_grad).astype(BF)
        dx = dot(gate_rows, gate) + dot(up_rows, up)
        tail = dot(pick, split_tail(jnp.sum(prob_term, axis=1, keepdims=True)).astype(BF))
        grad_prob = tail[:, 0:1] + tail[:, 1:2]
        half_at = pl.ds(start // 2 if single else pl.multiple_of(start // 2, 16), rows // 2)
        write_rows(dx_ref.at[half_at], dx, grad_prob)

    each_block(total, rows, block)
    own_ref[...] = dx_ref[: total // 4, :]
    dx_rows, dx_prob = read_rows(dx_ref[total // 4 :, :])
    write_rows(send_ref, dx_rows, dx_prob)
    if not single:
        for j in range(3):
            grad_ref[j] = sum_ref[j].astype(BF)
            stores[j].start()
    for store in stores:
        store.wait()


def add_kernel(hot_own_ref, hot_got_ref, cold_own_ref, cold_got_ref, *outs):
    def added(own_ref, got_ref):
        rows, prob = read_rows(own_ref[...])
        got_rows, got_prob = read_rows(got_ref[...])
        return jnp.concatenate([rows + got_rows, tail_lanes(prob + got_prob)], axis=1)

    hot = added(hot_own_ref, hot_got_ref)
    cold = added(cold_own_ref, cold_got_ref)
    half = cold.shape[0] // 2
    width = cold.shape[1] - TAIL
    for k, out_ref in enumerate(outs):
        at = k // 2 * 2 * CAP
        near, far = cold[at : at + 2 * CAP], cold[half + at : half + at + 2 * CAP]
        low = (iota(near.shape, 0) & 4) == 0
        if k % 2:
            part = jnp.where(low, pltpu.roll(near, CAP, 0), far)
        else:
            part = jnp.where(low, near, pltpu.roll(far, CAP, 0))
        rows = jnp.concatenate([hot[k * HALF : (k + 1) * HALF], part], axis=0)
        write_rows(out_ref, rows[:, :width], rows[:, width : width + 1])


def combine_kernel(*refs):
    *parts, own_ref, send_y_ref, send_x_ref = refs
    hot, cold = 0.0, []
    for ref in parts:
        rows, prob = read_rows(ref[...])
        both = jnp.concatenate([rows, tail_lanes(prob)], axis=1)
        hot = hot + both[:HALF]
        cold.append(both[HALF:])
    low = (iota(cold[0].shape, 0) & 4) == 0
    mine, other = [], []
    for even, odd in zip(cold[0::2], cold[1::2]):
        mine.append(jnp.where(low, even, pltpu.roll(odd, CAP, 0)))
        other.append(jnp.where(low, pltpu.roll(even, CAP, 0), odd))
    rows = jnp.concatenate([hot] + mine, axis=0)
    away = jnp.concatenate(other, axis=0)
    width = rows.shape[1] - TAIL
    own_ref[...] = rows
    write_rows(send_y_ref, rows[:, :width], rows[:, width : width + 1])
    write_rows(send_x_ref, away[:, :width], away[:, width : width + 1])


def finish_kernel(base, own_ref, y_ref, x_ref, xy_ref, pos_ref, dx_ref, prob_ref):
    pair = lax.axis_index("pair")
    me = lax.axis_index("dp")
    z, x = me // 4, (me // 2) % 2
    half = dx_ref.shape[0]
    pos = jnp.where(pair == 0, pos_ref[:, :half], pos_ref[:, half:])

    def cold_target(row, side):
        return (2 * (z ^ (row >> 2)) + side) * CAP + (row & 3)

    def with_hot(side):
        row = iota((own_ref.shape[0], half), 0)
        return jnp.where(row < HALF, base + HALF * side + row, cold_target(row - HALF, x))

    away = cold_target(iota((x_ref.shape[0], half), 0), 1 - x)
    total = 0.0
    grad_prob = [0.0] * TOP
    for ref, target in (
        (own_ref, with_hot(pair)),
        (y_ref, with_hot(1 - pair)),
        (x_ref, away),
        (xy_ref, away),
    ):
        routes = [pos[k : k + 1, :] == target for k in range(TOP)]
        onehot = jnp.where(routes[0] | routes[1], 1.0, 0.0).astype(BF)
        rows, prob = read_rows(ref[...])
        high = rows.astype(BF)
        total = total + dot(onehot, high, TN)
        if ref.dtype == F32:
            total = total + dot(onehot, (rows - high.astype(F32)).astype(BF), TN)
        for k in range(TOP):
            terms = jnp.sum(jnp.where(routes[k], prob, 0.0), axis=0, keepdims=True)
            grad_prob[k] = grad_prob[k] + terms
    dx_ref[...] = total.astype(BF)
    for k in range(TOP):
        prob_ref[k : k + 1, :] = grad_prob[k]


def sum_kernel(own_ref, a_ref, b_ref, c_ref, gate_ref, up_ref, down_ref):
    total = own_ref[...] + a_ref[...].astype(F32) + b_ref[...].astype(F32) + c_ref[...].astype(F32)
    units = gate_ref.shape[0]
    for index, out_ref in enumerate((gate_ref, up_ref, down_ref)):
        out_ref[...] = total[index * units : (index + 1) * units].astype(BF)


def call(kernel, outs, name, scratch=(), smem=(), hbm=(), out_hbm=(), limit=0):
    def run(*args):
        def space(index, far, smem=()):
            return pltpu.SMEM if index in smem else pltpu.HBM if index in far else pltpu.VMEM

        moved = sum(a.size * a.dtype.itemsize for a in args)
        moved += sum(o.size * o.dtype.itemsize for o in outs)
        return pl.pallas_call(
            kernel,
            out_shape=outs,
            in_specs=[pl.BlockSpec(memory_space=space(i, hbm, smem)) for i in range(len(args))],
            out_specs=[pl.BlockSpec(memory_space=space(i, out_hbm)) for i in range(len(outs))],
            scratch_shapes=[pltpu.VMEM(*s) if isinstance(s, tuple) else s for s in scratch],
            compiler_params=pltpu.CompilerParams(
                vmem_limit_bytes=limit or min(VMEM_LIMIT, VMEM_BASE + 3 * moved // 2)
            ),
            cost_estimate=pl.CostEstimate(flops=1024, bytes_accessed=1024, transcendentals=0),
            name=name,
        )(*args)

    return run


def local(
    tokens,
    grad_out,
    gate_probs,
    expert_ids,
    route_slots,
    hot_flags,
    owner_slot,
    cold_gate,
    cold_up,
    cold_down,
    hot_gate,
    hot_up,
    hot_down,
):
    count = lax.axis_size("dp")
    z_count = count // 4
    chunk_count = 2 * z_count
    token_count, width = tokens.shape
    lanes = width + TAIL
    units = hot_gate.shape[0]
    base = (count // 2) * CAP
    shape = jax.ShapeDtypeStruct
    half = token_count // 2
    pad = -units % 8

    def swap(value, mask):
        flip_dp, flip_pair = 2 * (mask & 1), mask >> 1
        perm = [
            (2 * i + p, 2 * (i ^ flip_dp) + (p ^ flip_pair)) for i in range(count) for p in range(2)
        ]
        return lax.ppermute(value, ("dp", "pair"), perm)

    def along_z(value, k):
        perm = [(i, 4 * ((i // 4) ^ k) + i % 4) for i in range(count)]
        return lax.ppermute(value, "dp", perm)

    def other_core(value):
        return lax.ppermute(value, "dp", [(i, i ^ 1) for i in range(count)])

    hot_weights = [jnp.pad(w, ((0, pad), (0, 0))) if pad else w for w in (hot_gate, hot_up, hot_down)]
    units_padded = units + pad
    used = 3 * units_padded
    cold_rows = z_count * 2 * 2 * CAP
    message = shape((HCAP + 4 * CAP, lanes), BF)
    pos, hot_own, *messages = call(
        functools.partial(dispatch_kernel, base),
        [shape((TOP, token_count), jnp.int32), shape((used, width), BF)] + [message] * z_count,
        "dispatch",
        scratch=[((cold_rows, lanes), BF)],
        smem=(5, 6),
        limit=VMEM_LIMIT,
    )(
        tokens,
        grad_out,
        gate_probs.T,
        expert_ids.T,
        route_slots.T,
        hot_flags,
        owner_slot,
        *hot_weights,
    )

    chunks = [messages[0]] + [along_z(messages[k], k) for k in range(1, z_count)]
    by_pair = swap(hot_own, 2)
    by_x = swap(hot_own, 1)
    first_out, by_pair_out, _ = lax.optimization_barrier((messages[0], by_pair, chunks[1]))
    weights = [hot_own, by_x, by_pair, swap(by_pair_out, 1)]
    (away,) = call(away_kernel, [shape((cold_rows // 2, lanes), BF)], "cold_away")(*chunks)
    chunks = chunks + [other_core(first_out)] + [other_core(chunk) for chunk in chunks[1:]]
    cold_mine = swap(away, 1)
    cold_other = other_core(cold_mine)

    cold_units = cold_gate.shape[1]
    cold_shape = shape(cold_gate.shape, BF)
    all_rows = chunk_count * HCAP
    half_rows = chunk_count * HALF // 2
    term = shape((used, width), BF)
    hot_dx, hot_dx_out, own_term, *sent_terms = call(
        functools.partial(hot_kernel, chunk_count, units_padded),
        [
            shape((half_rows, lanes), F32),
            shape((half_rows, lanes), BF),
            shape(term.shape, F32),
            term,
            term,
            term,
        ],
        "hot",
        scratch=[
            ((all_rows, width), BF),
            ((all_rows, TAIL), BF),
            ((4 * UNIT_BLOCK, width), BF),
            ((4, used, width) if chunk_count > CHUNK_BLOCK else (8, 128), F32),
        ],
    )(*chunks, *weights)

    cold_mine, hot_dx = lax.optimization_barrier((cold_mine, hot_dx))
    cold_own, cold_out, grad_cold_gate, grad_cold_up, grad_cold_down = call(
        functools.partial(cold_kernel, chunk_count),
        [shape((cold_rows // 2, lanes), F32), shape((cold_rows // 2, lanes), BF)] + [cold_shape] * 3,
        "cold",
        scratch=[
            ((2 * cold_rows, lanes), BF),
            ((cold_rows, lanes), F32),
            ((3, cold_units, width), BF),
            ((3, cold_units, width), BF),
            ((3, cold_units, width) if 2 * cold_rows > COLD_ROWS else (8, 128), F32),
            pltpu.SemaphoreType.DMA((3,)),
            pltpu.SemaphoreType.DMA((3,)),
        ],
        hbm=range(chunk_count + 2, chunk_count + 5),
        out_hbm=(2, 3, 4),
    )(*chunks, cold_mine, cold_other, cold_gate, cold_up, cold_down)

    hot_got, cold_got = other_core(hot_dx_out), other_core(cold_out)
    part = (HALF + 2 * CAP, lanes)
    parts = call(
        add_kernel, [shape(part, F32)] + [shape(part, BF)] * (z_count - 1), "add_cores"
    )(hot_dx, hot_got, cold_own, cold_got)
    parts = [parts[0]] + [along_z(parts[k], k) for k in range(1, z_count)]
    got_x, got_y = swap(sent_terms[0], 1), swap(sent_terms[1], 2)
    last_term, *_ = lax.optimization_barrier((sent_terms[2], *parts[1:]))
    got_terms = [got_x, got_y, swap(last_term, 3)]
    parts[0], *_ = lax.optimization_barrier((parts[0], got_x, got_y))

    cold_back = z_count * CAP
    own_rows, send_y, send_x = call(
        combine_kernel,
        [
            shape((HALF + cold_back, lanes), F32),
            shape((HALF + cold_back, lanes), BF),
            shape((cold_back, lanes), BF),
        ],
        "combine",
    )(*parts)
    rows_y, rows_x, rows_xy = swap(send_y, 2), swap(send_x, 1), swap(send_x, 3)
    dx, prob_t = call(
        functools.partial(finish_kernel, base),
        [shape((half, width), BF), shape((TOP, half), F32)],
        "finish",
    )(own_rows, rows_y, rows_x, rows_xy, pos)

    out_shape = shape((units_padded, width), BF)
    hot_grads = call(sum_kernel, [out_shape] * 3, "hot_sum")(
        own_term, *got_terms
    )
    if pad:
        hot_grads = [value[:units] for value in hot_grads]
    return (dx, prob_t.T, grad_cold_gate, grad_cold_up, grad_cold_down, *hot_grads)


def solution(mesh):
    return jax.shard_map(
        local,
        mesh=mesh,
        in_specs=(
            P("dp", None),
            P("dp", None),
            P("dp", None),
            P("dp", None),
            P("dp", None),
            P(),
            P(),
            P("dp", "pair", None),
            P("dp", "pair", None),
            P("dp", "pair", None),
            P(("dp", "pair"), None),
            P(("dp", "pair"), None),
            P(("dp", "pair"), None),
        ),
        out_specs=(
            P(("dp", "pair"), None),
            P(("dp", "pair"), None),
            P("dp", "pair", None),
            P("dp", "pair", None),
            P("dp", "pair", None),
            P(("dp", "pair"), None),
            P(("dp", "pair"), None),
            P(("dp", "pair"), None),
        ),
        check_vma=False,
    )
```

```python
import functools

import jax
import jax.numpy as jnp
from jax import lax
from jax.experimental import pallas as pl
from jax.experimental.pallas import tpu as pltpu
from jax.sharding import PartitionSpec as P

TOP = 2
CAP = 4
HCAP = 48
HALF = HCAP // 2
TAIL = 128
CHUNK_BLOCK = 8
COLD_BLOCK = 64
COLD_ROWS = 128
UNIT_BLOCK = 128
BF = jnp.bfloat16
F32 = jnp.float32
VMEM_LIMIT = 56 * 1024 * 1024
VMEM_BASE = 12 * 1024 * 1024

NT = (((1,), (1,)), ((), ()))
TN = (((0,), (0,)), ((), ()))


def dot(a, b, dims=(((1,), (0,)), ((), ()))):
    return lax.dot_general(a, b, dims, preferred_element_type=F32)


def iota(shape, dim):
    return lax.broadcasted_iota(jnp.int32, shape, dim)


def positions(ids, slots, flags_ref, owner_ref, base):
    hot = jnp.zeros_like(ids)
    own = jnp.zeros_like(ids)
    for e in range(flags_ref.shape[0]):
        named = ids == e
        hot = jnp.where(named, flags_ref[e], hot)
        own = jnp.where(named, owner_ref[e], own)
    cold_pos = jnp.where(slots < CAP, own * CAP + slots, -1)
    hot_pos = jnp.where(slots < HCAP, base + slots, -1)
    return jnp.where(hot == 1, hot_pos, cold_pos)


def tail_lanes(first, second=None):
    lane = iota((first.shape[0], TAIL), 1)
    out = jnp.where(lane == 0, first, 0.0)
    if second is not None:
        out = jnp.where(lane == 1, second, out)
    return out


def split_tail(value):
    high = value.astype(BF).astype(F32)
    return tail_lanes(high, value - high)


def each_block(total, size, body):
    if total == size:
        body(0)
    else:

        def step(block, carry):
            body(pl.multiple_of(block * size, size))
            return carry

        lax.fori_loop(0, total // size, step, 0)


def add_to(ref, value, single):
    if single:
        ref[...] = value.astype(ref.dtype)
    else:
        ref[...] += value


def gather_rows(out_ref, start, target, is_grad, pos, prob, tok_ref, grad_ref):
    width = tok_ref.shape[1]
    at = pl.ds(start, target.shape[0])
    first = pos[0:1, :] == target
    second = pos[1:2, :] == target
    chosen = jnp.where(first | second, 1.0, 0.0)
    rows = dot(jnp.where(is_grad, 0.0, chosen).astype(BF), tok_ref[...]) + dot(
        jnp.where(is_grad, chosen, 0.0).astype(BF), grad_ref[...]
    )
    out_ref[at, :width] = rows.astype(BF)
    weight = jnp.where(first, prob[0:1, :], 0.0) + jnp.where(second, prob[1:2, :], 0.0)
    weight = jnp.sum(jnp.where(is_grad, 0.0, weight), axis=1, keepdims=True)
    out_ref[at, width:] = tail_lanes(weight).astype(BF)


def dispatch_kernel(base, *refs):
    tok_ref, grad_ref, prob_ref, ids_ref, slot_ref, flags_ref, owner_ref = refs[:7]
    gate_ref, up_ref, down_ref, pos_ref, weight_ref, *messages, cold_ref = refs[7:]
    pair = lax.axis_index("pair")
    me = lax.axis_index("dp")
    z, x = me // 4, (me // 2) % 2
    pos = positions(ids_ref[...], slot_ref[...], flags_ref, owner_ref, base)
    pos_ref[...] = pos
    joined = [ref[...].astype(F32) for ref in (gate_ref, up_ref, down_ref)]
    weight_ref[...] = jnp.concatenate(joined, axis=0).astype(BF)
    prob = prob_ref[...].astype(F32)

    def gather(out_ref, start, target, is_grad):
        gather_rows(out_ref, start, target, is_grad, pos, prob, tok_ref, grad_ref)

    row = iota((HCAP, tok_ref.shape[0]), 0)
    target = base + HALF * pair + jnp.where(row >= HALF, row - HALF, row)
    gather(messages[0], 0, target, row >= HALF)

    def block(start):
        row = start + iota((COLD_BLOCK, tok_ref.shape[0]), 0)
        chip = 2 * (z ^ (row >> 4)) + (x ^ ((row >> 3) & 1))
        gather(cold_ref, start, chip * CAP + (row & 3), (row & 4) != 0)

    each_block(cold_ref.shape[0], COLD_BLOCK, block)
    for k, message in enumerate(messages):
        if k:
            message[:HCAP, :] = messages[0][:HCAP, :]
        message[HCAP:, :] = cold_ref[k * 16 : (k + 1) * 16, :]


def away_kernel(*refs):
    *messages, out_ref = refs
    rows = [ref[HCAP:, :].astype(F32)[2 * CAP :] for ref in messages]
    out_ref[...] = jnp.concatenate(rows, axis=0).astype(BF)


def swiglu_back(pre_gate, pre_up, back, prob):
    sig = 1.0 / (1.0 + jnp.exp(-pre_gate))
    act = pre_gate * sig
    hidden = act * pre_up
    scaled = prob * back
    gate_grad = scaled * pre_up * sig * (1.0 + pre_gate * (1.0 - sig))
    return gate_grad, scaled * act, prob * hidden, hidden * back


def write_rows(out_ref, rows, prob):
    width = rows.shape[1]
    out_ref[:, :width] = rows.astype(out_ref.dtype)
    tail = tail_lanes(prob) if out_ref.dtype == F32 else split_tail(prob).astype(BF)
    out_ref[:, width:] = tail


def read_rows(value):
    value = value.astype(F32)
    width = value.shape[1] - TAIL
    return value[:, :width], value[:, width : width + 1] + value[:, width + 1 : width + 2]


def hot_kernel(chunk_count, units, *refs):
    chunks = refs[:chunk_count]
    weights = refs[chunk_count : chunk_count + 4]
    own_ref, send_ref, *terms = refs[chunk_count + 4 : chunk_count + 10]
    rows_ref, tail_ref, wide_ref, sum_ref = refs[chunk_count + 10 :]
    width = rows_ref.shape[1]
    for k, chunk in enumerate(chunks):
        rows_ref[k * HCAP : (k + 1) * HCAP, :] = chunk[:HCAP, :width]
        tail_ref[k * HCAP : (k + 1) * HCAP, :] = chunk[:HCAP, width:]
    used = 3 * units
    for j, w_ref in enumerate(weights):
        start = j * UNIT_BLOCK
        clear = used // 16 * 16
        if clear < UNIT_BLOCK:
            wide_ref[start + clear : start + UNIT_BLOCK, :] = jnp.zeros((UNIT_BLOCK - clear, width), BF)
        wide_ref[start : start + used, :] = w_ref[...]
    columns = 4 * UNIT_BLOCK
    block_chunks = min(CHUNK_BLOCK, chunk_count)
    block_rows = block_chunks * HCAP
    half_rows = block_rows // 2
    single = block_chunks == chunk_count

    def block(start):
        at = pl.ds(start, block_rows)
        prob = tail_ref[at, :].astype(F32).reshape(block_chunks, HCAP, TAIL)[:, :HALF, 0:1]
        prob = prob.reshape(half_rows, 1)
        pre = dot(rows_ref[at, :], wide_ref[...], NT).reshape(block_chunks, HCAP, columns)
        pre_x = pre[:, :HALF].reshape(half_rows, columns)
        pre_g = pre[:, HALF:].reshape(half_rows, columns)
        first = (iota(pre_x.shape, 1) & (UNIT_BLOCK - 1)) < units
        gate_grad, up_grad, weighted, prob_term = swiglu_back(
            pre_x,
            pltpu.roll(pre_x, columns - units, 1),
            pltpu.roll(pre_g, columns - 2 * units, 1),
            prob,
        )
        gate_grad, up_grad, weighted, prob_term = (
            jnp.where(first, value, 0.0) for value in (gate_grad, up_grad, weighted, prob_term)
        )
        grad_prob = jnp.sum(prob_term, axis=1, keepdims=True)
        x_side = gate_grad + pltpu.roll(up_grad, units, 1)
        g_side = pltpu.roll(weighted, 2 * units, 1)
        both = jnp.concatenate(
            [x_side.reshape(block_chunks, HALF, columns), g_side.reshape(block_chunks, HALF, columns)],
            axis=1,
        )
        both = both.reshape(block_rows, columns).astype(BF)
        dx = dot(x_side.astype(BF), wide_ref[...])
        for j in range(4):
            term = dot(both[:, j * UNIT_BLOCK : (j + 1) * UNIT_BLOCK], rows_ref[at, :], TN)
            add_to(terms[j] if single else sum_ref.at[j], term[:used], single)
        return dx, grad_prob

    if single:
        dx, grad_prob = block(0)
        write_rows(own_ref, dx[: half_rows // 2], grad_prob[: half_rows // 2])
        write_rows(send_ref, dx[half_rows // 2 :], grad_prob[half_rows // 2 :])
    else:
        sum_ref[...] = jnp.zeros_like(sum_ref)
        for out_ref, offset in ((own_ref, 0), (send_ref, chunk_count * HCAP // 2)):

            def step(index, carry, out_ref=out_ref, offset=offset):
                dx, grad_prob = block(pl.multiple_of(offset + index * block_rows, 16))
                at = pl.ds(pl.multiple_of(index * half_rows, 16), half_rows)
                write_rows(out_ref.at[at], dx, grad_prob)
                return carry

            lax.fori_loop(0, chunk_count // block_chunks // 2, step, 0)
        for j, out_ref in enumerate(terms):
            out_ref[...] = sum_ref[j].astype(out_ref.dtype)


def cold_kernel(message_count, *refs):
    messages = refs[:message_count]
    mine_x_ref, other_x_ref, gate_hbm, up_hbm, down_hbm = refs[message_count : message_count + 5]
    own_ref, send_ref, *outs = refs[message_count + 5 : message_count + 10]
    data_ref, dx_ref, w_ref, grad_ref, sum_ref, in_sem, out_sem = refs[message_count + 10 :]
    total, width = data_ref.shape[0], gate_hbm.shape[2]
    rows = COLD_ROWS
    single = rows == total
    loads = [
        pltpu.make_async_copy(ref.at[0], w_ref.at[j], in_sem.at[j])
        for j, ref in enumerate((gate_hbm, up_hbm, down_hbm))
    ]
    stores = [
        pltpu.make_async_copy(grad_ref.at[j], ref.at[0], out_sem.at[j]) for j, ref in enumerate(outs)
    ]
    for load in loads:
        load.start()
    quarter = total // 4
    z_count = message_count // 2
    for flip, away_ref in enumerate((mine_x_ref, other_x_ref)):
        near = [ref[HCAP:, :].astype(F32)[: 2 * CAP] for ref in messages[flip * z_count :][:z_count]]
        start = 2 * flip * quarter
        data_ref[start : start + quarter, :] = jnp.concatenate(near, axis=0).astype(BF)
        data_ref[start + quarter : start + 2 * quarter, :] = away_ref[...]
    if not single:
        sum_ref[...] = jnp.zeros_like(sum_ref)
        for load in loads:
            load.wait()

    def weight(j):
        if single:
            loads[j].wait()
        return w_ref[j]

    def block(start):
        at = pl.ds(start, rows)
        data = data_ref[at, :width]
        prob = data_ref[at, width:].astype(F32)[:, 0:1]
        gate = weight(0)
        pre_gate = dot(data, gate, NT)
        up = weight(1)
        pre_up = dot(data, up, NT)
        back = pltpu.roll(dot(data, weight(2), NT), rows - CAP, 0)
        gate_grad, up_grad, weighted, prob_term = swiglu_back(pre_gate, pre_up, back, prob)
        x_row = (iota(pre_gate.shape, 0) & 4) == 0
        gate_grad = jnp.where(x_row, gate_grad, 0.0).astype(BF)
        up_grad = jnp.where(x_row, up_grad, 0.0).astype(BF)
        weighted = pltpu.roll(jnp.where(x_row, weighted, 0.0), CAP, 0).astype(BF)
        prob_term = jnp.where(x_row, prob_term, 0.0)
        for j, grad in enumerate((gate_grad, up_grad, weighted)):
            term = dot(grad, data, TN)
            if single:
                grad_ref[j] = term.astype(BF)
                stores[j].start()
            else:
                sum_ref[j] += term
        shape = (rows // 2, rows)
        row, col = iota(shape, 0), iota(shape, 1)
        pick = jnp.where(col == (row >> 2) * 8 + (row & 3), 1.0, 0.0).astype(BF)
        gate_rows = dot(pick, gate_grad).astype(BF)
        up_rows = dot(pick, up_grad).astype(BF)
        dx = dot(gate_rows, gate) + dot(up_rows, up)
        tail = dot(pick, split_tail(jnp.sum(prob_term, axis=1, keepdims=True)).astype(BF))
        grad_prob = tail[:, 0:1] + tail[:, 1:2]
        half_at = pl.ds(start // 2 if single else pl.multiple_of(start // 2, 16), rows // 2)
        write_rows(dx_ref.at[half_at], dx, grad_prob)

    each_block(total, rows, block)
    own_ref[...] = dx_ref[: total // 4, :]
    dx_rows, dx_prob = read_rows(dx_ref[total // 4 :, :])
    write_rows(send_ref, dx_rows, dx_prob)
    if not single:
        for j in range(3):
            grad_ref[j] = sum_ref[j].astype(BF)
            stores[j].start()
    for store in stores:
        store.wait()


def add_kernel(hot_own_ref, hot_got_ref, cold_own_ref, cold_got_ref, *outs):
    def added(own_ref, got_ref):
        rows, prob = read_rows(own_ref[...])
        got_rows, got_prob = read_rows(got_ref[...])
        return jnp.concatenate([rows + got_rows, tail_lanes(prob + got_prob)], axis=1)

    hot = added(hot_own_ref, hot_got_ref)
    cold = added(cold_own_ref, cold_got_ref)
    half = cold.shape[0] // 2
    width = cold.shape[1] - TAIL
    for k, out_ref in enumerate(outs):
        at = k // 2 * 2 * CAP
        near, far = cold[at : at + 2 * CAP], cold[half + at : half + at + 2 * CAP]
        low = (iota(near.shape, 0) & 4) == 0
        if k % 2:
            part = jnp.where(low, pltpu.roll(near, CAP, 0), far)
        else:
            part = jnp.where(low, near, pltpu.roll(far, CAP, 0))
        rows = jnp.concatenate([hot[k * HALF : (k + 1) * HALF], part], axis=0)
        write_rows(out_ref, rows[:, :width], rows[:, width : width + 1])


def combine_kernel(*refs):
    *parts, own_ref, send_y_ref, send_x_ref = refs
    hot, cold = 0.0, []
    for ref in parts:
        rows, prob = read_rows(ref[...])
        both = jnp.concatenate([rows, tail_lanes(prob)], axis=1)
        hot = hot + both[:HALF]
        cold.append(both[HALF:])
    low = (iota(cold[0].shape, 0) & 4) == 0
    mine, other = [], []
    for even, odd in zip(cold[0::2], cold[1::2]):
        mine.append(jnp.where(low, even, pltpu.roll(odd, CAP, 0)))
        other.append(jnp.where(low, pltpu.roll(even, CAP, 0), odd))
    rows = jnp.concatenate([hot] + mine, axis=0)
    away = jnp.concatenate(other, axis=0)
    width = rows.shape[1] - TAIL
    own_ref[...] = rows
    write_rows(send_y_ref, rows[:, :width], rows[:, width : width + 1])
    write_rows(send_x_ref, away[:, :width], away[:, width : width + 1])


def finish_kernel(base, own_ref, y_ref, x_ref, xy_ref, pos_ref, dx_ref, prob_ref):
    pair = lax.axis_index("pair")
    me = lax.axis_index("dp")
    z, x = me // 4, (me // 2) % 2
    half = dx_ref.shape[0]
    pos = jnp.where(pair == 0, pos_ref[:, :half], pos_ref[:, half:])

    def cold_target(row, side):
        return (2 * (z ^ (row >> 2)) + side) * CAP + (row & 3)

    def with_hot(side):
        row = iota((own_ref.shape[0], half), 0)
        return jnp.where(row < HALF, base + HALF * side + row, cold_target(row - HALF, x))

    away = cold_target(iota((x_ref.shape[0], half), 0), 1 - x)
    total = 0.0
    grad_prob = [0.0] * TOP
    for ref, target in (
        (own_ref, with_hot(pair)),
        (y_ref, with_hot(1 - pair)),
        (x_ref, away),
        (xy_ref, away),
    ):
        routes = [pos[k : k + 1, :] == target for k in range(TOP)]
        onehot = jnp.where(routes[0] | routes[1], 1.0, 0.0).astype(BF)
        rows, prob = read_rows(ref[...])
        high = rows.astype(BF)
        total = total + dot(onehot, high, TN)
        if ref.dtype == F32:
            total = total + dot(onehot, (rows - high.astype(F32)).astype(BF), TN)
        for k in range(TOP):
            terms = jnp.sum(jnp.where(routes[k], prob, 0.0), axis=0, keepdims=True)
            grad_prob[k] = grad_prob[k] + terms
    dx_ref[...] = total.astype(BF)
    for k in range(TOP):
        prob_ref[k : k + 1, :] = grad_prob[k]


def sum_kernel(own_ref, a_ref, b_ref, c_ref, gate_ref, up_ref, down_ref):
    total = own_ref[...] + a_ref[...].astype(F32) + b_ref[...].astype(F32) + c_ref[...].astype(F32)
    units = gate_ref.shape[0]
    for index, out_ref in enumerate((gate_ref, up_ref, down_ref)):
        out_ref[...] = total[index * units : (index + 1) * units].astype(BF)


def call(kernel, outs, name, scratch=(), smem=(), hbm=(), out_hbm=(), limit=0):
    def run(*args):
        def space(index, far, smem=()):
            return pltpu.SMEM if index in smem else pltpu.HBM if index in far else pltpu.VMEM

        moved = sum(a.size * a.dtype.itemsize for a in args)
        moved += sum(o.size * o.dtype.itemsize for o in outs)
        return pl.pallas_call(
            kernel,
            out_shape=outs,
            in_specs=[pl.BlockSpec(memory_space=space(i, hbm, smem)) for i in range(len(args))],
            out_specs=[pl.BlockSpec(memory_space=space(i, out_hbm)) for i in range(len(outs))],
            scratch_shapes=[pltpu.VMEM(*s) if isinstance(s, tuple) else s for s in scratch],
            compiler_params=pltpu.CompilerParams(
                vmem_limit_bytes=limit or min(VMEM_LIMIT, VMEM_BASE + 3 * moved // 2)
            ),
            cost_estimate=pl.CostEstimate(flops=1024, bytes_accessed=1024, transcendentals=0),
            name=name,
        )(*args)

    return run


def local(
    tokens,
    grad_out,
    gate_probs,
    expert_ids,
    route_slots,
    hot_flags,
    owner_slot,
    cold_gate,
    cold_up,
    cold_down,
    hot_gate,
    hot_up,
    hot_down,
):
    count = lax.axis_size("dp")
    z_count = count // 4
    chunk_count = 2 * z_count
    token_count, width = tokens.shape
    lanes = width + TAIL
    units = hot_gate.shape[0]
    base = (count // 2) * CAP
    shape = jax.ShapeDtypeStruct
    half = token_count // 2
    pad = -units % 8

    def swap(value, mask):
        flip_dp, flip_pair = 2 * (mask & 1), mask >> 1
        perm = [
            (2 * i + p, 2 * (i ^ flip_dp) + (p ^ flip_pair)) for i in range(count) for p in range(2)
        ]
        return lax.ppermute(value, ("dp", "pair"), perm)

    def along_z(value, k):
        perm = [(i, 4 * ((i // 4) ^ k) + i % 4) for i in range(count)]
        return lax.ppermute(value, "dp", perm)

    def other_core(value):
        return lax.ppermute(value, "dp", [(i, i ^ 1) for i in range(count)])

    hot_weights = [jnp.pad(w, ((0, pad), (0, 0))) if pad else w for w in (hot_gate, hot_up, hot_down)]
    units_padded = units + pad
    used = 3 * units_padded
    cold_rows = z_count * 2 * 2 * CAP
    message = shape((HCAP + 4 * CAP, lanes), BF)
    pos, hot_own, *messages = call(
        functools.partial(dispatch_kernel, base),
        [shape((TOP, token_count), jnp.int32), shape((used, width), BF)] + [message] * z_count,
        "dispatch",
        scratch=[((cold_rows, lanes), BF)],
        smem=(5, 6),
        limit=VMEM_LIMIT,
    )(
        tokens,
        grad_out,
        gate_probs.T,
        expert_ids.T,
        route_slots.T,
        hot_flags,
        owner_slot,
        *hot_weights,
    )

    chunks = [messages[0]] + [along_z(messages[k], k) for k in range(1, z_count)]
    by_pair = swap(hot_own, 2)
    by_x = swap(hot_own, 1)
    first_out, by_pair_out, _ = lax.optimization_barrier((messages[0], by_pair, chunks[1]))
    weights = [hot_own, by_x, by_pair, swap(by_pair_out, 1)]
    (away,) = call(away_kernel, [shape((cold_rows // 2, lanes), BF)], "cold_away")(*chunks)
    chunks = chunks + [other_core(first_out)] + [other_core(chunk) for chunk in chunks[1:]]
    cold_mine = swap(away, 1)
    cold_other = other_core(cold_mine)

    cold_units = cold_gate.shape[1]
    cold_shape = shape(cold_gate.shape, BF)
    all_rows = chunk_count * HCAP
    half_rows = chunk_count * HALF // 2
    term = shape((used, width), BF)
    hot_dx, hot_dx_out, own_term, *sent_terms = call(
        functools.partial(hot_kernel, chunk_count, units_padded),
        [
            shape((half_rows, lanes), F32),
            shape((half_rows, lanes), BF),
            shape(term.shape, F32),
            term,
            term,
            term,
        ],
        "hot",
        scratch=[
            ((all_rows, width), BF),
            ((all_rows, TAIL), BF),
            ((4 * UNIT_BLOCK, width), BF),
            ((4, used, width) if chunk_count > CHUNK_BLOCK else (8, 128), F32),
        ],
    )(*chunks, *weights)

    cold_mine, hot_dx = lax.optimization_barrier((cold_mine, hot_dx))
    cold_own, cold_out, grad_cold_gate, grad_cold_up, grad_cold_down = call(
        functools.partial(cold_kernel, chunk_count),
        [shape((cold_rows // 2, lanes), F32), shape((cold_rows // 2, lanes), BF)] + [cold_shape] * 3,
        "cold",
        scratch=[
            ((2 * cold_rows, lanes), BF),
            ((cold_rows, lanes), F32),
            ((3, cold_units, width), BF),
            ((3, cold_units, width), BF),
            ((3, cold_units, width) if 2 * cold_rows > COLD_ROWS else (8, 128), F32),
            pltpu.SemaphoreType.DMA((3,)),
            pltpu.SemaphoreType.DMA((3,)),
        ],
        hbm=range(chunk_count + 2, chunk_count + 5),
        out_hbm=(2, 3, 4),
    )(*chunks, cold_mine, cold_other, cold_gate, cold_up, cold_down)

    hot_got, cold_got = other_core(hot_dx_out), other_core(cold_out)
    part = (HALF + 2 * CAP, lanes)
    parts = call(
        add_kernel, [shape(part, F32)] + [shape(part, BF)] * (z_count - 1), "add_cores"
    )(hot_dx, hot_got, cold_own, cold_got)
    got_x, got_y = swap(sent_terms[0], 1), swap(sent_terms[1], 2)
    *parts, got_x, got_y, last_term = lax.optimization_barrier((*parts, got_x, got_y, sent_terms[2]))
    parts = [parts[0]] + [along_z(parts[k], k) for k in range(1, z_count)]
    got_terms = [got_x, got_y, swap(last_term, 3)]

    cold_back = z_count * CAP
    own_rows, send_y, send_x = call(
        combine_kernel,
        [
            shape((HALF + cold_back, lanes), F32),
            shape((HALF + cold_back, lanes), BF),
            shape((cold_back, lanes), BF),
        ],
        "combine",
    )(*parts)
    rows_y, rows_x, rows_xy = swap(send_y, 2), swap(send_x, 1), swap(send_x, 3)
    dx, prob_t = call(
        functools.partial(finish_kernel, base),
        [shape((half, width), BF), shape((TOP, half), F32)],
        "finish",
    )(own_rows, rows_y, rows_x, rows_xy, pos)

    out_shape = shape((units_padded, width), BF)
    hot_grads = call(sum_kernel, [out_shape] * 3, "hot_sum")(
        own_term, *got_terms
    )
    if pad:
        hot_grads = [value[:units] for value in hot_grads]
    return (dx, prob_t.T, grad_cold_gate, grad_cold_up, grad_cold_down, *hot_grads)


def solution(mesh):
    return jax.shard_map(
        local,
        mesh=mesh,
        in_specs=(
            P("dp", None),
            P("dp", None),
            P("dp", None),
            P("dp", None),
            P("dp", None),
            P(),
            P(),
            P("dp", "pair", None),
            P("dp", "pair", None),
            P("dp", "pair", None),
            P(("dp", "pair"), None),
            P(("dp", "pair"), None),
            P(("dp", "pair"), None),
        ),
        out_specs=(
            P(("dp", "pair"), None),
            P(("dp", "pair"), None),
            P("dp", "pair", None),
            P("dp", "pair", None),
            P("dp", "pair", None),
            P(("dp", "pair"), None),
            P(("dp", "pair"), None),
            P(("dp", "pair"), None),
        ),
        check_vma=False,
    )
```

```python
import functools

import jax
import jax.numpy as jnp
from jax import lax
from jax.experimental import pallas as pl
from jax.experimental.pallas import tpu as pltpu
from jax.sharding import PartitionSpec as P

TOP = 2
CAP = 4
HCAP = 48
HALF = HCAP // 2
TAIL = 128
CHUNK_BLOCK = 8
COLD_BLOCK = 64
COLD_ROWS = 128
UNIT_BLOCK = 128
BF = jnp.bfloat16
F32 = jnp.float32
VMEM_LIMIT = 56 * 1024 * 1024
VMEM_BASE = 12 * 1024 * 1024

NT = (((1,), (1,)), ((), ()))
TN = (((0,), (0,)), ((), ()))


def dot(a, b, dims=(((1,), (0,)), ((), ()))):
    return lax.dot_general(a, b, dims, preferred_element_type=F32)


def iota(shape, dim):
    return lax.broadcasted_iota(jnp.int32, shape, dim)


def positions(ids, slots, flags_ref, owner_ref, base):
    hot = jnp.zeros_like(ids)
    own = jnp.zeros_like(ids)
    for e in range(flags_ref.shape[0]):
        named = ids == e
        hot = jnp.where(named, flags_ref[e], hot)
        own = jnp.where(named, owner_ref[e], own)
    cold_pos = jnp.where(slots < CAP, own * CAP + slots, -1)
    hot_pos = jnp.where(slots < HCAP, base + slots, -1)
    return jnp.where(hot == 1, hot_pos, cold_pos)


def tail_lanes(first, second=None):
    lane = iota((first.shape[0], TAIL), 1)
    out = jnp.where(lane == 0, first, 0.0)
    if second is not None:
        out = jnp.where(lane == 1, second, out)
    return out


def split_tail(value):
    high = value.astype(BF).astype(F32)
    return tail_lanes(high, value - high)


def each_block(total, size, body):
    if total == size:
        body(0)
    else:

        def step(block, carry):
            body(pl.multiple_of(block * size, size))
            return carry

        lax.fori_loop(0, total // size, step, 0)


def add_to(ref, value, single):
    if single:
        ref[...] = value.astype(ref.dtype)
    else:
        ref[...] += value


def gather_rows(out_ref, start, target, is_grad, pos, prob, tok_ref, grad_ref):
    width = tok_ref.shape[1]
    at = pl.ds(start, target.shape[0])
    first = pos[0:1, :] == target
    second = pos[1:2, :] == target
    chosen = jnp.where(first | second, 1.0, 0.0)
    rows = dot(jnp.where(is_grad, 0.0, chosen).astype(BF), tok_ref[...]) + dot(
        jnp.where(is_grad, chosen, 0.0).astype(BF), grad_ref[...]
    )
    out_ref[at, :width] = rows.astype(BF)
    weight = jnp.where(first, prob[0:1, :], 0.0) + jnp.where(second, prob[1:2, :], 0.0)
    weight = jnp.sum(jnp.where(is_grad, 0.0, weight), axis=1, keepdims=True)
    out_ref[at, width:] = tail_lanes(weight).astype(BF)


def dispatch_kernel(base, *refs):
    tok_ref, grad_ref, prob_ref, ids_ref, slot_ref, flags_ref, owner_ref = refs[:7]
    gate_ref, up_ref, down_ref, pos_ref, weight_ref, *messages, cold_ref = refs[7:]
    pair = lax.axis_index("pair")
    me = lax.axis_index("dp")
    z, x = me // 4, (me // 2) % 2
    pos = positions(ids_ref[...], slot_ref[...], flags_ref, owner_ref, base)
    pos_ref[...] = pos
    joined = [ref[...].astype(F32) for ref in (gate_ref, up_ref, down_ref)]
    weight_ref[...] = jnp.concatenate(joined, axis=0).astype(BF)
    prob = prob_ref[...].astype(F32)

    def gather(out_ref, start, target, is_grad):
        gather_rows(out_ref, start, target, is_grad, pos, prob, tok_ref, grad_ref)

    row = iota((HCAP, tok_ref.shape[0]), 0)
    target = base + HALF * pair + jnp.where(row >= HALF, row - HALF, row)
    gather(messages[0], 0, target, row >= HALF)

    def block(start):
        row = start + iota((COLD_BLOCK, tok_ref.shape[0]), 0)
        chip = 2 * (z ^ (row >> 4)) + (x ^ ((row >> 3) & 1))
        gather(cold_ref, start, chip * CAP + (row & 3), (row & 4) != 0)

    each_block(cold_ref.shape[0], COLD_BLOCK, block)
    for k, message in enumerate(messages):
        if k:
            message[:HCAP, :] = messages[0][:HCAP, :]
        message[HCAP:, :] = cold_ref[k * 16 : (k + 1) * 16, :]


def away_kernel(*refs):
    *messages, out_ref = refs
    rows = [ref[HCAP:, :].astype(F32)[2 * CAP :] for ref in messages]
    out_ref[...] = jnp.concatenate(rows, axis=0).astype(BF)


def swiglu_back(pre_gate, pre_up, back, prob):
    sig = 1.0 / (1.0 + jnp.exp(-pre_gate))
    act = pre_gate * sig
    hidden = act * pre_up
    scaled = prob * back
    gate_grad = scaled * pre_up * sig * (1.0 + pre_gate * (1.0 - sig))
    return gate_grad, scaled * act, prob * hidden, hidden * back


def write_rows(out_ref, rows, prob):
    width = rows.shape[1]
    out_ref[:, :width] = rows.astype(out_ref.dtype)
    tail = tail_lanes(prob) if out_ref.dtype == F32 else split_tail(prob).astype(BF)
    out_ref[:, width:] = tail


def read_rows(value):
    value = value.astype(F32)
    width = value.shape[1] - TAIL
    return value[:, :width], value[:, width : width + 1] + value[:, width + 1 : width + 2]


def hot_kernel(chunk_count, units, *refs):
    chunks = refs[:chunk_count]
    weights = refs[chunk_count : chunk_count + 4]
    own_ref, send_ref, *terms = refs[chunk_count + 4 : chunk_count + 10]
    rows_ref, tail_ref, wide_ref, sum_ref = refs[chunk_count + 10 :]
    width = rows_ref.shape[1]
    for k, chunk in enumerate(chunks):
        rows_ref[k * HCAP : (k + 1) * HCAP, :] = chunk[:HCAP, :width]
        tail_ref[k * HCAP : (k + 1) * HCAP, :] = chunk[:HCAP, width:]
    used = 3 * units
    for j, w_ref in enumerate(weights):
        start = j * UNIT_BLOCK
        clear = used // 16 * 16
        if clear < UNIT_BLOCK:
            wide_ref[start + clear : start + UNIT_BLOCK, :] = jnp.zeros((UNIT_BLOCK - clear, width), BF)
        wide_ref[start : start + used, :] = w_ref[...]
    columns = 4 * UNIT_BLOCK
    block_chunks = min(CHUNK_BLOCK, chunk_count)
    block_rows = block_chunks * HCAP
    half_rows = block_rows // 2
    single = block_chunks == chunk_count

    def block(start):
        at = pl.ds(start, block_rows)
        prob = tail_ref[at, :].astype(F32).reshape(block_chunks, HCAP, TAIL)[:, :HALF, 0:1]
        prob = prob.reshape(half_rows, 1)
        pre = dot(rows_ref[at, :], wide_ref[...], NT).reshape(block_chunks, HCAP, columns)
        pre_x = pre[:, :HALF].reshape(half_rows, columns)
        pre_g = pre[:, HALF:].reshape(half_rows, columns)
        first = (iota(pre_x.shape, 1) & (UNIT_BLOCK - 1)) < units
        gate_grad, up_grad, weighted, prob_term = swiglu_back(
            pre_x,
            pltpu.roll(pre_x, columns - units, 1),
            pltpu.roll(pre_g, columns - 2 * units, 1),
            prob,
        )
        gate_grad, up_grad, weighted, prob_term = (
            jnp.where(first, value, 0.0) for value in (gate_grad, up_grad, weighted, prob_term)
        )
        grad_prob = jnp.sum(prob_term, axis=1, keepdims=True)
        x_side = gate_grad + pltpu.roll(up_grad, units, 1)
        g_side = pltpu.roll(weighted, 2 * units, 1)
        both = jnp.concatenate(
            [x_side.reshape(block_chunks, HALF, columns), g_side.reshape(block_chunks, HALF, columns)],
            axis=1,
        )
        both = both.reshape(block_rows, columns).astype(BF)
        dx = dot(x_side.astype(BF), wide_ref[...])
        for j in range(4):
            term = dot(both[:, j * UNIT_BLOCK : (j + 1) * UNIT_BLOCK], rows_ref[at, :], TN)
            add_to(terms[j] if single else sum_ref.at[j], term[:used], single)
        return dx, grad_prob

    if single:
        dx, grad_prob = block(0)
        write_rows(own_ref, dx[: half_rows // 2], grad_prob[: half_rows // 2])
        write_rows(send_ref, dx[half_rows // 2 :], grad_prob[half_rows // 2 :])
    else:
        sum_ref[...] = jnp.zeros_like(sum_ref)
        for out_ref, offset in ((own_ref, 0), (send_ref, chunk_count * HCAP // 2)):

            def step(index, carry, out_ref=out_ref, offset=offset):
                dx, grad_prob = block(pl.multiple_of(offset + index * block_rows, 16))
                at = pl.ds(pl.multiple_of(index * half_rows, 16), half_rows)
                write_rows(out_ref.at[at], dx, grad_prob)
                return carry

            lax.fori_loop(0, chunk_count // block_chunks // 2, step, 0)
        for j, out_ref in enumerate(terms):
            out_ref[...] = sum_ref[j].astype(out_ref.dtype)


def cold_kernel(message_count, *refs):
    messages = refs[:message_count]
    mine_x_ref, other_x_ref, gate_hbm, up_hbm, down_hbm = refs[message_count : message_count + 5]
    own_ref, send_ref, *outs = refs[message_count + 5 : message_count + 10]
    data_ref, dx_ref, w_ref, grad_ref, sum_ref, in_sem, out_sem = refs[message_count + 10 :]
    total, width = data_ref.shape[0], gate_hbm.shape[2]
    rows = COLD_ROWS
    single = rows == total
    loads = [
        pltpu.make_async_copy(ref.at[0], w_ref.at[j], in_sem.at[j])
        for j, ref in enumerate((gate_hbm, up_hbm, down_hbm))
    ]
    stores = [
        pltpu.make_async_copy(grad_ref.at[j], ref.at[0], out_sem.at[j]) for j, ref in enumerate(outs)
    ]
    for load in loads:
        load.start()
    quarter = total // 4
    z_count = message_count // 2
    for flip, away_ref in enumerate((mine_x_ref, other_x_ref)):
        near = [ref[HCAP:, :].astype(F32)[: 2 * CAP] for ref in messages[flip * z_count :][:z_count]]
        start = 2 * flip * quarter
        data_ref[start : start + quarter, :] = jnp.concatenate(near, axis=0).astype(BF)
        data_ref[start + quarter : start + 2 * quarter, :] = away_ref[...]
    if not single:
        sum_ref[...] = jnp.zeros_like(sum_ref)
        for load in loads:
            load.wait()

    def weight(j):
        if single:
            loads[j].wait()
        return w_ref[j]

    def block(start):
        at = pl.ds(start, rows)
        data = data_ref[at, :width]
        prob = data_ref[at, width:].astype(F32)[:, 0:1]
        gate = weight(0)
        pre_gate = dot(data, gate, NT)
        up = weight(1)
        pre_up = dot(data, up, NT)
        back = pltpu.roll(dot(data, weight(2), NT), rows - CAP, 0)
        gate_grad, up_grad, weighted, prob_term = swiglu_back(pre_gate, pre_up, back, prob)
        x_row = (iota(pre_gate.shape, 0) & 4) == 0
        gate_grad = jnp.where(x_row, gate_grad, 0.0).astype(BF)
        up_grad = jnp.where(x_row, up_grad, 0.0).astype(BF)
        weighted = pltpu.roll(jnp.where(x_row, weighted, 0.0), CAP, 0).astype(BF)
        prob_term = jnp.where(x_row, prob_term, 0.0)
        for j, grad in enumerate((gate_grad, up_grad, weighted)):
            term = dot(grad, data, TN)
            if single:
                grad_ref[j] = term.astype(BF)
                stores[j].start()
            else:
                sum_ref[j] += term
        shape = (rows // 2, rows)
        row, col = iota(shape, 0), iota(shape, 1)
        pick = jnp.where(col == (row >> 2) * 8 + (row & 3), 1.0, 0.0).astype(BF)
        gate_rows = dot(pick, gate_grad).astype(BF)
        up_rows = dot(pick, up_grad).astype(BF)
        dx = dot(gate_rows, gate) + dot(up_rows, up)
        tail = dot(pick, split_tail(jnp.sum(prob_term, axis=1, keepdims=True)).astype(BF))
        grad_prob = tail[:, 0:1] + tail[:, 1:2]
        half_at = pl.ds(start // 2 if single else pl.multiple_of(start // 2, 16), rows // 2)
        write_rows(dx_ref.at[half_at], dx, grad_prob)

    each_block(total, rows, block)
    own_ref[...] = dx_ref[: total // 4, :]
    dx_rows, dx_prob = read_rows(dx_ref[total // 4 :, :])
    write_rows(send_ref, dx_rows, dx_prob)
    if not single:
        for j in range(3):
            grad_ref[j] = sum_ref[j].astype(BF)
            stores[j].start()
    for store in stores:
        store.wait()


def add_kernel(hot_own_ref, hot_got_ref, cold_own_ref, cold_got_ref, *outs):
    def added(own_ref, got_ref):
        rows, prob = read_rows(own_ref[...])
        got_rows, got_prob = read_rows(got_ref[...])
        return jnp.concatenate([rows + got_rows, tail_lanes(prob + got_prob)], axis=1)

    hot = added(hot_own_ref, hot_got_ref)
    cold = added(cold_own_ref, cold_got_ref)
    half = cold.shape[0] // 2
    width = cold.shape[1] - TAIL
    for k, out_ref in enumerate(outs):
        at = k // 2 * 2 * CAP
        near, far = cold[at : at + 2 * CAP], cold[half + at : half + at + 2 * CAP]
        low = (iota(near.shape, 0) & 4) == 0
        if k % 2:
            part = jnp.where(low, pltpu.roll(near, CAP, 0), far)
        else:
            part = jnp.where(low, near, pltpu.roll(far, CAP, 0))
        rows = jnp.concatenate([hot[k * HALF : (k + 1) * HALF], part], axis=0)
        write_rows(out_ref, rows[:, :width], rows[:, width : width + 1])


def combine_kernel(*refs):
    *parts, own_ref, send_y_ref, send_x_ref = refs
    hot, cold = 0.0, []
    for ref in parts:
        rows, prob = read_rows(ref[...])
        both = jnp.concatenate([rows, tail_lanes(prob)], axis=1)
        hot = hot + both[:HALF]
        cold.append(both[HALF:])
    low = (iota(cold[0].shape, 0) & 4) == 0
    mine, other = [], []
    for even, odd in zip(cold[0::2], cold[1::2]):
        mine.append(jnp.where(low, even, pltpu.roll(odd, CAP, 0)))
        other.append(jnp.where(low, pltpu.roll(even, CAP, 0), odd))
    rows = jnp.concatenate([hot] + mine, axis=0)
    away = jnp.concatenate(other, axis=0)
    width = rows.shape[1] - TAIL
    own_ref[...] = rows
    write_rows(send_y_ref, rows[:, :width], rows[:, width : width + 1])
    write_rows(send_x_ref, away[:, :width], away[:, width : width + 1])


def finish_kernel(base, own_ref, y_ref, x_ref, xy_ref, pos_ref, dx_ref, prob_ref):
    pair = lax.axis_index("pair")
    me = lax.axis_index("dp")
    z, x = me // 4, (me // 2) % 2
    half = dx_ref.shape[0]
    pos = jnp.where(pair == 0, pos_ref[:, :half], pos_ref[:, half:])

    def cold_target(row, side):
        return (2 * (z ^ (row >> 2)) + side) * CAP + (row & 3)

    def with_hot(side):
        row = iota((own_ref.shape[0], half), 0)
        return jnp.where(row < HALF, base + HALF * side + row, cold_target(row - HALF, x))

    away = cold_target(iota((x_ref.shape[0], half), 0), 1 - x)
    total = 0.0
    grad_prob = [0.0] * TOP
    for ref, target in (
        (own_ref, with_hot(pair)),
        (y_ref, with_hot(1 - pair)),
        (x_ref, away),
        (xy_ref, away),
    ):
        routes = [pos[k : k + 1, :] == target for k in range(TOP)]
        onehot = jnp.where(routes[0] | routes[1], 1.0, 0.0).astype(BF)
        rows, prob = read_rows(ref[...])
        high = rows.astype(BF)
        total = total + dot(onehot, high, TN)
        if ref.dtype == F32:
            total = total + dot(onehot, (rows - high.astype(F32)).astype(BF), TN)
        for k in range(TOP):
            terms = jnp.sum(jnp.where(routes[k], prob, 0.0), axis=0, keepdims=True)
            grad_prob[k] = grad_prob[k] + terms
    dx_ref[...] = total.astype(BF)
    for k in range(TOP):
        prob_ref[k : k + 1, :] = grad_prob[k]


def sum_kernel(own_ref, a_ref, b_ref, c_ref, gate_ref, up_ref, down_ref):
    total = own_ref[...] + a_ref[...].astype(F32) + b_ref[...].astype(F32) + c_ref[...].astype(F32)
    units = gate_ref.shape[0]
    for index, out_ref in enumerate((gate_ref, up_ref, down_ref)):
        out_ref[...] = total[index * units : (index + 1) * units].astype(BF)


def call(kernel, outs, name, scratch=(), smem=(), hbm=(), out_hbm=(), limit=0):
    def run(*args):
        def space(index, far, smem=()):
            return pltpu.SMEM if index in smem else pltpu.HBM if index in far else pltpu.VMEM

        moved = sum(a.size * a.dtype.itemsize for a in args)
        moved += sum(o.size * o.dtype.itemsize for o in outs)
        return pl.pallas_call(
            kernel,
            out_shape=outs,
            in_specs=[pl.BlockSpec(memory_space=space(i, hbm, smem)) for i in range(len(args))],
            out_specs=[pl.BlockSpec(memory_space=space(i, out_hbm)) for i in range(len(outs))],
            scratch_shapes=[pltpu.VMEM(*s) if isinstance(s, tuple) else s for s in scratch],
            compiler_params=pltpu.CompilerParams(
                vmem_limit_bytes=limit or min(VMEM_LIMIT, VMEM_BASE + 3 * moved // 2)
            ),
            cost_estimate=pl.CostEstimate(flops=1024, bytes_accessed=1024, transcendentals=0),
            name=name,
        )(*args)

    return run


def local(
    tokens,
    grad_out,
    gate_probs,
    expert_ids,
    route_slots,
    hot_flags,
    owner_slot,
    cold_gate,
    cold_up,
    cold_down,
    hot_gate,
    hot_up,
    hot_down,
):
    count = lax.axis_size("dp")
    z_count = count // 4
    chunk_count = 2 * z_count
    token_count, width = tokens.shape
    lanes = width + TAIL
    units = hot_gate.shape[0]
    base = (count // 2) * CAP
    shape = jax.ShapeDtypeStruct
    half = token_count // 2
    pad = -units % 8

    def swap(value, mask):
        flip_dp, flip_pair = 2 * (mask & 1), mask >> 1
        perm = [
            (2 * i + p, 2 * (i ^ flip_dp) + (p ^ flip_pair)) for i in range(count) for p in range(2)
        ]
        return lax.ppermute(value, ("dp", "pair"), perm)

    def along_z(value, k):
        perm = [(i, 4 * ((i // 4) ^ k) + i % 4) for i in range(count)]
        return lax.ppermute(value, "dp", perm)

    def all_along_z(values):
        order = sorted(range(1, z_count), key=lambda k: (k == 1, k))
        got = {k: along_z(values[k], k) for k in order}
        return [values[0]] + [got[k] for k in range(1, z_count)]

    def other_core(value):
        return lax.ppermute(value, "dp", [(i, i ^ 1) for i in range(count)])

    hot_weights = [jnp.pad(w, ((0, pad), (0, 0))) if pad else w for w in (hot_gate, hot_up, hot_down)]
    units_padded = units + pad
    used = 3 * units_padded
    cold_rows = z_count * 2 * 2 * CAP
    message = shape((HCAP + 4 * CAP, lanes), BF)
    pos, hot_own, *messages = call(
        functools.partial(dispatch_kernel, base),
        [shape((TOP, token_count), jnp.int32), shape((used, width), BF)] + [message] * z_count,
        "dispatch",
        scratch=[((cold_rows, lanes), BF)],
        smem=(5, 6),
        limit=VMEM_LIMIT,
    )(
        tokens,
        grad_out,
        gate_probs.T,
        expert_ids.T,
        route_slots.T,
        hot_flags,
        owner_slot,
        *hot_weights,
    )

    chunks = all_along_z(messages)
    by_pair = swap(hot_own, 2)
    by_x = swap(hot_own, 1)
    first_out, by_pair_out, _ = lax.optimization_barrier((messages[0], by_pair, chunks[1]))
    weights = [hot_own, by_x, by_pair, swap(by_pair_out, 1)]
    (away,) = call(away_kernel, [shape((cold_rows // 2, lanes), BF)], "cold_away")(*chunks)
    chunks = chunks + [other_core(first_out)] + [other_core(chunk) for chunk in chunks[1:]]
    cold_mine = swap(away, 1)
    cold_other = other_core(cold_mine)

    cold_units = cold_gate.shape[1]
    cold_shape = shape(cold_gate.shape, BF)
    all_rows = chunk_count * HCAP
    half_rows = chunk_count * HALF // 2
    term = shape((used, width), BF)
    hot_dx, hot_dx_out, own_term, *sent_terms = call(
        functools.partial(hot_kernel, chunk_count, units_padded),
        [
            shape((half_rows, lanes), F32),
            shape((half_rows, lanes), BF),
            shape(term.shape, F32),
            term,
            term,
            term,
        ],
        "hot",
        scratch=[
            ((all_rows, width), BF),
            ((all_rows, TAIL), BF),
            ((4 * UNIT_BLOCK, width), BF),
            ((4, used, width) if chunk_count > CHUNK_BLOCK else (8, 128), F32),
        ],
    )(*chunks, *weights)

    cold_mine, hot_dx = lax.optimization_barrier((cold_mine, hot_dx))
    cold_own, cold_out, grad_cold_gate, grad_cold_up, grad_cold_down = call(
        functools.partial(cold_kernel, chunk_count),
        [shape((cold_rows // 2, lanes), F32), shape((cold_rows // 2, lanes), BF)] + [cold_shape] * 3,
        "cold",
        scratch=[
            ((2 * cold_rows, lanes), BF),
            ((cold_rows, lanes), F32),
            ((3, cold_units, width), BF),
            ((3, cold_units, width), BF),
            ((3, cold_units, width) if 2 * cold_rows > COLD_ROWS else (8, 128), F32),
            pltpu.SemaphoreType.DMA((3,)),
            pltpu.SemaphoreType.DMA((3,)),
        ],
        hbm=range(chunk_count + 2, chunk_count + 5),
        out_hbm=(2, 3, 4),
    )(*chunks, cold_mine, cold_other, cold_gate, cold_up, cold_down)

    hot_got, cold_got = other_core(hot_dx_out), other_core(cold_out)
    part = (HALF + 2 * CAP, lanes)
    parts = call(
        add_kernel, [shape(part, F32)] + [shape(part, BF)] * (z_count - 1), "add_cores"
    )(hot_dx, hot_got, cold_own, cold_got)
    term_x, _ = lax.optimization_barrier((sent_terms[0], cold_mine))
    got_x, got_y = swap(term_x, 1), swap(sent_terms[1], 2)
    *parts, got_x, got_y, last_term = lax.optimization_barrier((*parts, got_x, got_y, sent_terms[2]))
    parts = all_along_z(parts)
    got_terms = [got_x, got_y, swap(last_term, 3)]

    cold_back = z_count * CAP
    own_rows, send_y, send_x = call(
        combine_kernel,
        [
            shape((HALF + cold_back, lanes), F32),
            shape((HALF + cold_back, lanes), BF),
            shape((cold_back, lanes), BF),
        ],
        "combine",
    )(*parts)
    rows_y, rows_x, rows_xy = swap(send_y, 2), swap(send_x, 1), swap(send_x, 3)
    dx, prob_t = call(
        functools.partial(finish_kernel, base),
        [shape((half, width), BF), shape((TOP, half), F32)],
        "finish",
    )(own_rows, rows_y, rows_x, rows_xy, pos)

    out_shape = shape((units_padded, width), BF)
    hot_grads = call(sum_kernel, [out_shape] * 3, "hot_sum")(
        own_term, *got_terms
    )
    if pad:
        hot_grads = [value[:units] for value in hot_grads]
    return (dx, prob_t.T, grad_cold_gate, grad_cold_up, grad_cold_down, *hot_grads)


def solution(mesh):
    return jax.shard_map(
        local,
        mesh=mesh,
        in_specs=(
            P("dp", None),
            P("dp", None),
            P("dp", None),
            P("dp", None),
            P("dp", None),
            P(),
            P(),
            P("dp", "pair", None),
            P("dp", "pair", None),
            P("dp", "pair", None),
            P(("dp", "pair"), None),
            P(("dp", "pair"), None),
            P(("dp", "pair"), None),
        ),
        out_specs=(
            P(("dp", "pair"), None),
            P(("dp", "pair"), None),
            P("dp", "pair", None),
            P("dp", "pair", None),
            P("dp", "pair", None),
            P(("dp", "pair"), None),
            P(("dp", "pair"), None),
            P(("dp", "pair"), None),
        ),
        check_vma=False,
    )
```

```python
import functools

import jax
import jax.numpy as jnp
from jax import lax
from jax.experimental import pallas as pl
from jax.experimental.pallas import tpu as pltpu
from jax.sharding import PartitionSpec as P

TOP = 2
CAP = 4
HCAP = 48
HALF = HCAP // 2
TAIL = 128
CHUNK_BLOCK = 8
COLD_BLOCK = 64
COLD_ROWS = 128
UNIT_BLOCK = 128
BF = jnp.bfloat16
F32 = jnp.float32
VMEM_LIMIT = 56 * 1024 * 1024
VMEM_BASE = 12 * 1024 * 1024

NT = (((1,), (1,)), ((), ()))
TN = (((0,), (0,)), ((), ()))


def dot(a, b, dims=(((1,), (0,)), ((), ()))):
    return lax.dot_general(a, b, dims, preferred_element_type=F32)


def iota(shape, dim):
    return lax.broadcasted_iota(jnp.int32, shape, dim)


def positions(ids, slots, flags_ref, owner_ref, base):
    hot = jnp.zeros_like(ids)
    own = jnp.zeros_like(ids)
    for e in range(flags_ref.shape[0]):
        named = ids == e
        hot = jnp.where(named, flags_ref[e], hot)
        own = jnp.where(named, owner_ref[e], own)
    cold_pos = jnp.where(slots < CAP, own * CAP + slots, -1)
    hot_pos = jnp.where(slots < HCAP, base + slots, -1)
    return jnp.where(hot == 1, hot_pos, cold_pos)


def tail_lanes(first, second=None):
    lane = iota((first.shape[0], TAIL), 1)
    out = jnp.where(lane == 0, first, 0.0)
    if second is not None:
        out = jnp.where(lane == 1, second, out)
    return out


def split_tail(value):
    high = value.astype(BF).astype(F32)
    return tail_lanes(high, value - high)


def each_block(total, size, body):
    if total == size:
        body(0)
    else:

        def step(block, carry):
            body(pl.multiple_of(block * size, size))
            return carry

        lax.fori_loop(0, total // size, step, 0)


def add_to(ref, value, single):
    if single:
        ref[...] = value.astype(ref.dtype)
    else:
        ref[...] += value


def gather_rows(out_ref, start, target, is_grad, pos, prob, tok_ref, grad_ref):
    width = tok_ref.shape[1]
    at = pl.ds(start, target.shape[0])
    first = pos[0:1, :] == target
    second = pos[1:2, :] == target
    chosen = jnp.where(first | second, 1.0, 0.0)
    rows = dot(jnp.where(is_grad, 0.0, chosen).astype(BF), tok_ref[...]) + dot(
        jnp.where(is_grad, chosen, 0.0).astype(BF), grad_ref[...]
    )
    out_ref[at, :width] = rows.astype(BF)
    weight = jnp.where(first, prob[0:1, :], 0.0) + jnp.where(second, prob[1:2, :], 0.0)
    weight = jnp.sum(jnp.where(is_grad, 0.0, weight), axis=1, keepdims=True)
    out_ref[at, width:] = tail_lanes(weight).astype(BF)


def dispatch_kernel(base, *refs):
    tok_ref, grad_ref, prob_ref, ids_ref, slot_ref, flags_ref, owner_ref = refs[:7]
    gate_ref, up_ref, down_ref, pos_ref, weight_ref, *messages, cold_ref = refs[7:]
    pair = lax.axis_index("pair")
    me = lax.axis_index("dp")
    z, x = me // 4, (me // 2) % 2
    pos = positions(ids_ref[...], slot_ref[...], flags_ref, owner_ref, base)
    pos_ref[...] = pos
    joined = [ref[...].astype(F32) for ref in (gate_ref, up_ref, down_ref)]
    weight_ref[...] = jnp.concatenate(joined, axis=0).astype(BF)
    prob = prob_ref[...].astype(F32)

    def gather(out_ref, start, target, is_grad):
        gather_rows(out_ref, start, target, is_grad, pos, prob, tok_ref, grad_ref)

    row = iota((HCAP, tok_ref.shape[0]), 0)
    target = base + HALF * pair + jnp.where(row >= HALF, row - HALF, row)
    gather(messages[0], 0, target, row >= HALF)

    def block(start):
        row = start + iota((COLD_BLOCK, tok_ref.shape[0]), 0)
        chip = 2 * (z ^ (row >> 4)) + (x ^ ((row >> 3) & 1))
        gather(cold_ref, start, chip * CAP + (row & 3), (row & 4) != 0)

    each_block(cold_ref.shape[0], COLD_BLOCK, block)
    for k, message in enumerate(messages):
        if k:
            message[:HCAP, :] = messages[0][:HCAP, :]
        message[HCAP:, :] = cold_ref[k * 16 : (k + 1) * 16, :]


def copy_kernel(*refs):
    half = len(refs) // 2
    for in_ref, out_ref in zip(refs[:half], refs[half:]):
        out_ref[...] = in_ref[...]


def away_kernel(*refs):
    *messages, out_ref = refs
    rows = [ref[HCAP:, :].astype(F32)[2 * CAP :] for ref in messages]
    out_ref[...] = jnp.concatenate(rows, axis=0).astype(BF)


def swiglu_back(pre_gate, pre_up, back, prob):
    sig = 1.0 / (1.0 + jnp.exp(-pre_gate))
    act = pre_gate * sig
    hidden = act * pre_up
    scaled = prob * back
    gate_grad = scaled * pre_up * sig * (1.0 + pre_gate * (1.0 - sig))
    return gate_grad, scaled * act, prob * hidden, hidden * back


def write_rows(out_ref, rows, prob):
    width = rows.shape[1]
    out_ref[:, :width] = rows.astype(out_ref.dtype)
    tail = tail_lanes(prob) if out_ref.dtype == F32 else split_tail(prob).astype(BF)
    out_ref[:, width:] = tail


def read_rows(value):
    value = value.astype(F32)
    width = value.shape[1] - TAIL
    return value[:, :width], value[:, width : width + 1] + value[:, width + 1 : width + 2]


def hot_kernel(chunk_count, units, *refs):
    chunks = refs[:chunk_count]
    weights = refs[chunk_count : chunk_count + 4]
    own_ref, send_ref, *terms = refs[chunk_count + 4 : chunk_count + 10]
    rows_ref, tail_ref, wide_ref, sum_ref = refs[chunk_count + 10 :]
    width = rows_ref.shape[1]
    for k, chunk in enumerate(chunks):
        rows_ref[k * HCAP : (k + 1) * HCAP, :] = chunk[:HCAP, :width]
        tail_ref[k * HCAP : (k + 1) * HCAP, :] = chunk[:HCAP, width:]
    used = 3 * units
    for j, w_ref in enumerate(weights):
        start = j * UNIT_BLOCK
        clear = used // 16 * 16
        if clear < UNIT_BLOCK:
            wide_ref[start + clear : start + UNIT_BLOCK, :] = jnp.zeros((UNIT_BLOCK - clear, width), BF)
        wide_ref[start : start + used, :] = w_ref[...]
    columns = 4 * UNIT_BLOCK
    block_chunks = min(CHUNK_BLOCK, chunk_count)
    block_rows = block_chunks * HCAP
    half_rows = block_rows // 2
    single = block_chunks == chunk_count

    def block(start):
        at = pl.ds(start, block_rows)
        prob = tail_ref[at, :].astype(F32).reshape(block_chunks, HCAP, TAIL)[:, :HALF, 0:1]
        prob = prob.reshape(half_rows, 1)
        pre = dot(rows_ref[at, :], wide_ref[...], NT).reshape(block_chunks, HCAP, columns)
        pre_x = pre[:, :HALF].reshape(half_rows, columns)
        pre_g = pre[:, HALF:].reshape(half_rows, columns)
        first = (iota(pre_x.shape, 1) & (UNIT_BLOCK - 1)) < units
        gate_grad, up_grad, weighted, prob_term = swiglu_back(
            pre_x,
            pltpu.roll(pre_x, columns - units, 1),
            pltpu.roll(pre_g, columns - 2 * units, 1),
            prob,
        )
        gate_grad, up_grad, weighted, prob_term = (
            jnp.where(first, value, 0.0) for value in (gate_grad, up_grad, weighted, prob_term)
        )
        grad_prob = jnp.sum(prob_term, axis=1, keepdims=True)
        x_side = gate_grad + pltpu.roll(up_grad, units, 1)
        g_side = pltpu.roll(weighted, 2 * units, 1)
        both = jnp.concatenate(
            [x_side.reshape(block_chunks, HALF, columns), g_side.reshape(block_chunks, HALF, columns)],
            axis=1,
        )
        both = both.reshape(block_rows, columns).astype(BF)
        dx = dot(x_side.astype(BF), wide_ref[...])
        for j in range(4):
            term = dot(both[:, j * UNIT_BLOCK : (j + 1) * UNIT_BLOCK], rows_ref[at, :], TN)
            add_to(terms[j] if single else sum_ref.at[j], term[:used], single)
        return dx, grad_prob

    if single:
        dx, grad_prob = block(0)
        write_rows(own_ref, dx[: half_rows // 2], grad_prob[: half_rows // 2])
        write_rows(send_ref, dx[half_rows // 2 :], grad_prob[half_rows // 2 :])
    else:
        sum_ref[...] = jnp.zeros_like(sum_ref)
        for out_ref, offset in ((own_ref, 0), (send_ref, chunk_count * HCAP // 2)):

            def step(index, carry, out_ref=out_ref, offset=offset):
                dx, grad_prob = block(pl.multiple_of(offset + index * block_rows, 16))
                at = pl.ds(pl.multiple_of(index * half_rows, 16), half_rows)
                write_rows(out_ref.at[at], dx, grad_prob)
                return carry

            lax.fori_loop(0, chunk_count // block_chunks // 2, step, 0)
        for j, out_ref in enumerate(terms):
            out_ref[...] = sum_ref[j].astype(out_ref.dtype)


def cold_kernel(message_count, *refs):
    messages = refs[:message_count]
    mine_x_ref, other_x_ref, gate_hbm, up_hbm, down_hbm = refs[message_count : message_count + 5]
    own_ref, send_ref, *outs = refs[message_count + 5 : message_count + 10]
    data_ref, dx_ref, w_ref, grad_ref, sum_ref, in_sem, out_sem = refs[message_count + 10 :]
    total, units, width = data_ref.shape[0], gate_hbm.shape[1], gate_hbm.shape[2]
    rows = COLD_ROWS
    single = rows == total
    loads = [
        pltpu.make_async_copy(ref.at[0], w_ref.at[pl.ds(j * units, units)], in_sem.at[j])
        for j, ref in enumerate((gate_hbm, up_hbm, down_hbm))
    ]
    stores = [
        pltpu.make_async_copy(grad_ref.at[j], ref.at[0], out_sem.at[j]) for j, ref in enumerate(outs)
    ]
    for load in loads:
        load.start()
    quarter = total // 4
    z_count = message_count // 2
    for flip, away_ref in enumerate((mine_x_ref, other_x_ref)):
        near = [ref[HCAP:, :].astype(F32)[: 2 * CAP] for ref in messages[flip * z_count :][:z_count]]
        start = 2 * flip * quarter
        data_ref[start : start + quarter, :] = jnp.concatenate(near, axis=0).astype(BF)
        data_ref[start + quarter : start + 2 * quarter, :] = away_ref[...]
    if not single:
        sum_ref[...] = jnp.zeros_like(sum_ref)
        for load in loads:
            load.wait()

    def weight(j):
        if single:
            loads[j].wait()
        return w_ref[j * units : (j + 1) * units, :]

    def block(start):
        at = pl.ds(start, rows)
        data = data_ref[at, :width]
        first = jnp.where((iota((8, TAIL), 0) == 0) & (iota((8, TAIL), 1) == 0), 1.0, 0.0)
        prob = dot(first.astype(BF), data_ref[at, width:], NT)[0:1, :]
        pre_gate = dot(weight(0), data, NT)
        pre_up = dot(weight(1), data, NT)
        back = pltpu.roll(dot(weight(2), data, NT), rows - CAP, 1)
        gate_grad, up_grad, weighted, prob_term = swiglu_back(pre_gate, pre_up, back, prob)
        x_lane = (iota(pre_gate.shape, 1) & 4) == 0
        gate_grad = jnp.where(x_lane, gate_grad, 0.0)
        up_grad = jnp.where(x_lane, up_grad, 0.0)
        weighted = pltpu.roll(jnp.where(x_lane, weighted, 0.0), CAP, 1)
        grad_prob = jnp.sum(jnp.where(x_lane, prob_term, 0.0), axis=0, keepdims=True)
        inner = jnp.concatenate([gate_grad, up_grad], axis=0).astype(BF)
        for j, grad in enumerate((gate_grad, up_grad, weighted)):
            term = dot(grad.astype(BF), data)
            if single:
                grad_ref[j] = term.astype(BF)
                stores[j].start()
            else:
                sum_ref[j] += term
        shape = (rows, rows // 2)
        row, col = iota(shape, 0), iota(shape, 1)
        pick = jnp.where(row == (col >> 2) * 8 + (col & 3), 1.0, 0.0).astype(BF)
        dx = dot(dot(inner, pick).astype(BF), w_ref[: 2 * units, :], TN)
        shape = (rows // 2, rows)
        row, col = iota(shape, 0), iota(shape, 1)
        pick = jnp.where(col == (row >> 2) * 8 + (row & 3), 1.0, 0.0).astype(BF)
        high = grad_prob.astype(BF).astype(F32)
        row = iota((8, rows), 0)
        both = jnp.where(row == 0, high, jnp.where(row == 1, grad_prob - high, 0.0))
        both = dot(pick, both.astype(BF), NT)
        grad_prob = both[:, 0:1] + both[:, 1:2]
        half_at = pl.ds(start // 2 if single else pl.multiple_of(start // 2, 16), rows // 2)
        write_rows(dx_ref.at[half_at], dx, grad_prob)

    each_block(total, rows, block)
    own_ref[...] = dx_ref[: total // 4, :]
    dx_rows, dx_prob = read_rows(dx_ref[total // 4 :, :])
    write_rows(send_ref, dx_rows, dx_prob)
    if not single:
        for j in range(3):
            grad_ref[j] = sum_ref[j].astype(BF)
            stores[j].start()
    for store in stores:
        store.wait()


def add_kernel(hot_own_ref, hot_got_ref, cold_own_ref, cold_got_ref, *outs):
    def added(own_ref, got_ref):
        rows, prob = read_rows(own_ref[...])
        got_rows, got_prob = read_rows(got_ref[...])
        return jnp.concatenate([rows + got_rows, tail_lanes(prob + got_prob)], axis=1)

    hot = added(hot_own_ref, hot_got_ref)
    cold = added(cold_own_ref, cold_got_ref)
    half = cold.shape[0] // 2
    width = cold.shape[1] - TAIL
    for k, out_ref in enumerate(outs):
        at = k // 2 * 2 * CAP
        near, far = cold[at : at + 2 * CAP], cold[half + at : half + at + 2 * CAP]
        low = (iota(near.shape, 0) & 4) == 0
        if k % 2:
            part = jnp.where(low, pltpu.roll(near, CAP, 0), far)
        else:
            part = jnp.where(low, near, pltpu.roll(far, CAP, 0))
        rows = jnp.concatenate([hot[k * HALF : (k + 1) * HALF], part], axis=0)
        write_rows(out_ref, rows[:, :width], rows[:, width : width + 1])


def combine_kernel(*refs):
    *parts, own_ref, send_y_ref, send_x_ref = refs
    hot, cold = 0.0, []
    for ref in parts:
        rows, prob = read_rows(ref[...])
        both = jnp.concatenate([rows, tail_lanes(prob)], axis=1)
        hot = hot + both[:HALF]
        cold.append(both[HALF:])
    low = (iota(cold[0].shape, 0) & 4) == 0
    mine, other = [], []
    for even, odd in zip(cold[0::2], cold[1::2]):
        mine.append(jnp.where(low, even, pltpu.roll(odd, CAP, 0)))
        other.append(jnp.where(low, pltpu.roll(even, CAP, 0), odd))
    rows = jnp.concatenate([hot] + mine, axis=0)
    away = jnp.concatenate(other, axis=0)
    width = rows.shape[1] - TAIL
    own_ref[...] = rows
    write_rows(send_y_ref, rows[:, :width], rows[:, width : width + 1])
    write_rows(send_x_ref, away[:, :width], away[:, width : width + 1])


def finish_kernel(base, own_ref, y_ref, x_ref, xy_ref, pos_ref, dx_ref, prob_ref):
    pair = lax.axis_index("pair")
    me = lax.axis_index("dp")
    z, x = me // 4, (me // 2) % 2
    half = dx_ref.shape[0]
    pos = jnp.where(pair == 0, pos_ref[:, :half], pos_ref[:, half:])

    def cold_target(row, side):
        return (2 * (z ^ (row >> 2)) + side) * CAP + (row & 3)

    def with_hot(side):
        row = iota((own_ref.shape[0], half), 0)
        return jnp.where(row < HALF, base + HALF * side + row, cold_target(row - HALF, x))

    away = cold_target(iota((x_ref.shape[0], half), 0), 1 - x)
    total = 0.0
    grad_prob = [0.0] * TOP
    for ref, target in (
        (own_ref, with_hot(pair)),
        (y_ref, with_hot(1 - pair)),
        (x_ref, away),
        (xy_ref, away),
    ):
        routes = [pos[k : k + 1, :] == target for k in range(TOP)]
        onehot = jnp.where(routes[0] | routes[1], 1.0, 0.0).astype(BF)
        rows, prob = read_rows(ref[...])
        high = rows.astype(BF)
        total = total + dot(onehot, high, TN)
        if ref.dtype == F32:
            total = total + dot(onehot, (rows - high.astype(F32)).astype(BF), TN)
        for k in range(TOP):
            terms = jnp.sum(jnp.where(routes[k], prob, 0.0), axis=0, keepdims=True)
            grad_prob[k] = grad_prob[k] + terms
    dx_ref[...] = total.astype(BF)
    for k in range(TOP):
        prob_ref[k : k + 1, :] = grad_prob[k]


def sum_kernel(own_ref, a_ref, b_ref, c_ref, gate_ref, up_ref, down_ref):
    total = own_ref[...] + a_ref[...].astype(F32) + b_ref[...].astype(F32) + c_ref[...].astype(F32)
    units = gate_ref.shape[0]
    for index, out_ref in enumerate((gate_ref, up_ref, down_ref)):
        out_ref[...] = total[index * units : (index + 1) * units].astype(BF)


def call(kernel, outs, name, scratch=(), smem=(), hbm=(), out_hbm=(), limit=0):
    def run(*args):
        def space(index, far, smem=()):
            return pltpu.SMEM if index in smem else pltpu.HBM if index in far else pltpu.VMEM

        moved = sum(a.size * a.dtype.itemsize for a in args)
        moved += sum(o.size * o.dtype.itemsize for o in outs)
        return pl.pallas_call(
            kernel,
            out_shape=outs,
            in_specs=[pl.BlockSpec(memory_space=space(i, hbm, smem)) for i in range(len(args))],
            out_specs=[pl.BlockSpec(memory_space=space(i, out_hbm)) for i in range(len(outs))],
            scratch_shapes=[pltpu.VMEM(*s) if isinstance(s, tuple) else s for s in scratch],
            compiler_params=pltpu.CompilerParams(
                vmem_limit_bytes=limit or min(VMEM_LIMIT, VMEM_BASE + 3 * moved // 2)
            ),
            cost_estimate=pl.CostEstimate(flops=1024, bytes_accessed=1024, transcendentals=0),
            name=name,
        )(*args)

    return run


def local(
    tokens,
    grad_out,
    gate_probs,
    expert_ids,
    route_slots,
    hot_flags,
    owner_slot,
    cold_gate,
    cold_up,
    cold_down,
    hot_gate,
    hot_up,
    hot_down,
):
    count = lax.axis_size("dp")
    z_count = count // 4
    chunk_count = 2 * z_count
    token_count, width = tokens.shape
    lanes = width + TAIL
    units = hot_gate.shape[0]
    base = (count // 2) * CAP
    shape = jax.ShapeDtypeStruct
    half = token_count // 2
    pad = -units % 8

    def swap(value, mask):
        flip_dp, flip_pair = 2 * (mask & 1), mask >> 1
        perm = [
            (2 * i + p, 2 * (i ^ flip_dp) + (p ^ flip_pair)) for i in range(count) for p in range(2)
        ]
        return lax.ppermute(value, ("dp", "pair"), perm)

    def along_z(value, k):
        perm = [(i, 4 * ((i // 4) ^ k) + i % 4) for i in range(count)]
        return lax.ppermute(value, "dp", perm)

    def all_along_z(values):
        order = sorted(range(1, z_count), key=lambda k: (k == 1, k))
        got = {k: along_z(values[k], k) for k in order}
        return [values[0]] + [got[k] for k in range(1, z_count)]

    def other_core(value):
        return lax.ppermute(value, "dp", [(i, i ^ 1) for i in range(count)])

    hot_weights = [jnp.pad(w, ((0, pad), (0, 0))) if pad else w for w in (hot_gate, hot_up, hot_down)]
    units_padded = units + pad
    used = 3 * units_padded
    cold_rows = z_count * 2 * 2 * CAP
    message = shape((HCAP + 4 * CAP, lanes), BF)
    pos, hot_own, *messages = call(
        functools.partial(dispatch_kernel, base),
        [shape((TOP, token_count), jnp.int32), shape((used, width), BF)] + [message] * z_count,
        "dispatch",
        scratch=[((cold_rows, lanes), BF)],
        smem=(5, 6),
        limit=VMEM_LIMIT,
    )(
        tokens,
        grad_out,
        gate_probs.T,
        expert_ids.T,
        route_slots.T,
        hot_flags,
        owner_slot,
        *hot_weights,
    )

    chunks = all_along_z(messages)
    by_pair = swap(hot_own, 2)
    by_x = swap(hot_own, 1)
    first_out, hot_own, _ = lax.optimization_barrier((messages[0], hot_own, chunks[1]))
    first_out, hot_own = call(
        copy_kernel, [message, shape(hot_own.shape, BF)], "own_rows"
    )(first_out, hot_own)
    chunks[0] = first_out
    by_pair_out, first_out, hot_own = lax.optimization_barrier((by_pair, first_out, hot_own))
    weights = [hot_own, by_x, by_pair, swap(by_pair_out, 1)]
    (away,) = call(away_kernel, [shape((cold_rows // 2, lanes), BF)], "cold_away")(*chunks)
    chunks = chunks + [other_core(first_out)] + [other_core(chunk) for chunk in chunks[1:]]
    cold_mine = swap(away, 1)
    cold_other = other_core(cold_mine)

    cold_units = cold_gate.shape[1]
    cold_shape = shape(cold_gate.shape, BF)
    all_rows = chunk_count * HCAP
    half_rows = chunk_count * HALF // 2
    term = shape((used, width), BF)
    hot_dx, hot_dx_out, own_term, *sent_terms = call(
        functools.partial(hot_kernel, chunk_count, units_padded),
        [
            shape((half_rows, lanes), F32),
            shape((half_rows, lanes), BF),
            shape(term.shape, F32),
            term,
            term,
            term,
        ],
        "hot",
        scratch=[
            ((all_rows, width), BF),
            ((all_rows, TAIL), BF),
            ((4 * UNIT_BLOCK, width), BF),
            ((4, used, width) if chunk_count > CHUNK_BLOCK else (8, 128), F32),
        ],
    )(*chunks, *weights)

    cold_mine, hot_dx = lax.optimization_barrier((cold_mine, hot_dx))
    cold_own, cold_out, grad_cold_gate, grad_cold_up, grad_cold_down = call(
        functools.partial(cold_kernel, chunk_count),
        [shape((cold_rows // 2, lanes), F32), shape((cold_rows // 2, lanes), BF)] + [cold_shape] * 3,
        "cold",
        scratch=[
            ((2 * cold_rows, lanes), BF),
            ((cold_rows, lanes), F32),
            ((3 * cold_units, width), BF),
            ((3, cold_units, width), BF),
            ((3, cold_units, width) if 2 * cold_rows > COLD_ROWS else (8, 128), F32),
            pltpu.SemaphoreType.DMA((3,)),
            pltpu.SemaphoreType.DMA((3,)),
        ],
        hbm=range(chunk_count + 2, chunk_count + 5),
        out_hbm=(2, 3, 4),
    )(*chunks, cold_mine, cold_other, cold_gate, cold_up, cold_down)

    hot_got, cold_got = other_core(hot_dx_out), other_core(cold_out)
    part = (HALF + 2 * CAP, lanes)
    parts = call(
        add_kernel, [shape(part, F32)] + [shape(part, BF)] * (z_count - 1), "add_cores"
    )(hot_dx, hot_got, cold_own, cold_got)
    term_x, _ = lax.optimization_barrier((sent_terms[0], cold_mine))
    got_x, got_y = swap(term_x, 1), swap(sent_terms[1], 2)
    last_term, cold_out = lax.optimization_barrier((sent_terms[2], cold_out))
    *parts, got_x, got_y = lax.optimization_barrier((*parts, got_x, got_y))
    parts = all_along_z(parts)
    got_terms = [got_x, got_y, swap(last_term, 3)]

    cold_back = z_count * CAP
    own_rows, send_y, send_x = call(
        combine_kernel,
        [
            shape((HALF + cold_back, lanes), F32),
            shape((HALF + cold_back, lanes), BF),
            shape((cold_back, lanes), BF),
        ],
        "combine",
    )(*parts)
    rows_y, rows_x, rows_xy = swap(send_y, 2), swap(send_x, 1), swap(send_x, 3)
    out_shape = shape((units_padded, width), BF)
    hot_grads = call(sum_kernel, [out_shape] * 3, "hot_sum")(
        own_term, *got_terms
    )
    own_rows, *hot_grads = lax.optimization_barrier((own_rows, *hot_grads))
    dx, prob_t = call(
        functools.partial(finish_kernel, base),
        [shape((half, width), BF), shape((TOP, half), F32)],
        "finish",
    )(own_rows, rows_y, rows_x, rows_xy, pos)

    if pad:
        hot_grads = [value[:units] for value in hot_grads]
    return (dx, prob_t.T, grad_cold_gate, grad_cold_up, grad_cold_down, *hot_grads)


def solution(mesh):
    return jax.shard_map(
        local,
        mesh=mesh,
        in_specs=(
            P("dp", None),
            P("dp", None),
            P("dp", None),
            P("dp", None),
            P("dp", None),
            P(),
            P(),
            P("dp", "pair", None),
            P("dp", "pair", None),
            P("dp", "pair", None),
            P(("dp", "pair"), None),
            P(("dp", "pair"), None),
            P(("dp", "pair"), None),
        ),
        out_specs=(
            P(("dp", "pair"), None),
            P(("dp", "pair"), None),
            P("dp", "pair", None),
            P("dp", "pair", None),
            P("dp", "pair", None),
            P(("dp", "pair"), None),
            P(("dp", "pair"), None),
            P(("dp", "pair"), None),
        ),
        check_vma=False,
    )
```

```python
import functools

import jax
import jax.numpy as jnp
from jax import lax
from jax.experimental import pallas as pl
from jax.experimental.pallas import tpu as pltpu
from jax.sharding import PartitionSpec as P

TOP = 2
CAP = 4
HCAP = 48
HALF = HCAP // 2
TAIL = 128
CHUNK_BLOCK = 8
GATHER_BLOCK = 112
COLD_PART = 4 * CAP
COLD_ROWS = 128
UNIT_BLOCK = 128
BF = jnp.bfloat16
F32 = jnp.float32
VMEM_LIMIT = 56 * 1024 * 1024
VMEM_BASE = 12 * 1024 * 1024

NT = (((1,), (1,)), ((), ()))
TN = (((0,), (0,)), ((), ()))


def dot(a, b, dims=(((1,), (0,)), ((), ()))):
    return lax.dot_general(a, b, dims, preferred_element_type=F32)


def iota(shape, dim):
    return lax.broadcasted_iota(jnp.int32, shape, dim)


def positions(ids, slots, flags_ref, owner_ref, base):
    hot = jnp.zeros_like(ids)
    own = jnp.zeros_like(ids)
    for e in range(flags_ref.shape[0]):
        named = ids == e
        hot = jnp.where(named, flags_ref[e], hot)
        own = jnp.where(named, owner_ref[e], own)
    cold_pos = jnp.where(slots < CAP, own * CAP + slots, -1)
    hot_pos = jnp.where(slots < HCAP, base + slots, -1)
    return jnp.where(hot == 1, hot_pos, cold_pos)


def tail_lanes(first, second=None):
    lane = iota((first.shape[0], TAIL), 1)
    out = jnp.where(lane == 0, first, 0.0)
    if second is not None:
        out = jnp.where(lane == 1, second, out)
    return out


def split_tail(value):
    high = value.astype(BF).astype(F32)
    return tail_lanes(high, value - high)


def each_block(total, size, body):
    if total == size:
        body(0)
    else:

        def step(block, carry):
            body(pl.multiple_of(block * size, size))
            return carry

        lax.fori_loop(0, total // size, step, 0)


def add_to(ref, value, single):
    if single:
        ref[...] = value.astype(ref.dtype)
    else:
        ref[...] += value


def gather_rows(out_ref, start, target, is_grad, pos, prob, tok_ref, grad_ref):
    width = tok_ref.shape[1]
    at = pl.ds(start, target.shape[0])
    first = pos[0:1, :] == target
    second = pos[1:2, :] == target
    chosen = jnp.where(first | second, 1.0, 0.0)
    rows = dot(jnp.where(is_grad, 0.0, chosen).astype(BF), tok_ref[...]) + dot(
        jnp.where(is_grad, chosen, 0.0).astype(BF), grad_ref[...]
    )
    out_ref[at, :width] = rows.astype(BF)
    weight = jnp.where(first, prob[0:1, :], 0.0) + jnp.where(second, prob[1:2, :], 0.0)
    weight = jnp.sum(jnp.where(is_grad, 0.0, weight), axis=1, keepdims=True)
    out_ref[at, width:] = tail_lanes(weight).astype(BF)


def dispatch_kernel(base, *refs):
    tok_ref, grad_ref, prob_ref, ids_ref, slot_ref, flags_ref, owner_ref = refs[:7]
    gate_ref, up_ref, down_ref, pos_ref, weight_ref, *messages, rows_ref = refs[7:]
    pair = lax.axis_index("pair")
    me = lax.axis_index("dp")
    z, x = me // 4, (me // 2) % 2
    pos = positions(ids_ref[...], slot_ref[...], flags_ref, owner_ref, base)
    pos_ref[...] = pos
    joined = [ref[...].astype(F32) for ref in (gate_ref, up_ref, down_ref)]
    weight_ref[...] = jnp.concatenate(joined, axis=0).astype(BF)
    prob = prob_ref[...].astype(F32)

    def block(start):
        row = start + iota((GATHER_BLOCK, tok_ref.shape[0]), 0)
        hot = row < HCAP
        cold_row = row - HCAP
        chip = 2 * (z ^ (cold_row >> 4)) + (x ^ ((cold_row >> 3) & 1))
        hot_target = base + HALF * pair + jnp.where(row >= HALF, row - HALF, row)
        target = jnp.where(hot, hot_target, chip * CAP + (row & 3))
        is_grad = (hot & (row >= HALF)) | (~hot & ((row & 4) != 0))
        gather_rows(rows_ref, start, target, is_grad, pos, prob, tok_ref, grad_ref)

    each_block(rows_ref.shape[0], GATHER_BLOCK, block)
    for k, message in enumerate(messages):
        rows = message.shape[0]
        if rows > COLD_PART:
            message[:HCAP, :] = rows_ref[:HCAP, :]
        message[rows - COLD_PART :, :] = rows_ref[HCAP + k * COLD_PART : HCAP + (k + 1) * COLD_PART, :]


def copy_kernel(*refs):
    half = len(refs) // 2
    for in_ref, out_ref in zip(refs[:half], refs[half:]):
        out_ref[...] = in_ref[...]


def away_kernel(*refs):
    *messages, out_ref = refs
    rows = [ref[ref.shape[0] - COLD_PART :, :].astype(F32)[2 * CAP :] for ref in messages]
    out_ref[...] = jnp.concatenate(rows, axis=0).astype(BF)


def swiglu_back(pre_gate, pre_up, back, prob):
    sig = 1.0 / (1.0 + jnp.exp(-pre_gate))
    act = pre_gate * sig
    hidden = act * pre_up
    scaled = prob * back
    gate_grad = scaled * pre_up * sig * (1.0 + pre_gate * (1.0 - sig))
    return gate_grad, scaled * act, prob * hidden, hidden * back


def write_rows(out_ref, rows, prob):
    width = rows.shape[1]
    out_ref[:, :width] = rows.astype(out_ref.dtype)
    tail = tail_lanes(prob) if out_ref.dtype == F32 else split_tail(prob).astype(BF)
    out_ref[:, width:] = tail


def read_rows(value):
    value = value.astype(F32)
    width = value.shape[1] - TAIL
    return value[:, :width], value[:, width : width + 1] + value[:, width + 1 : width + 2]


def hot_kernel(chunk_count, units, *refs):
    chunks = refs[:chunk_count]
    weights = refs[chunk_count : chunk_count + 4]
    own_ref, send_ref, *terms = refs[chunk_count + 4 : chunk_count + 10]
    rows_ref, tail_ref, wide_ref, sum_ref = refs[chunk_count + 10 :]
    width = rows_ref.shape[1]
    for k, chunk in enumerate(chunks):
        rows_ref[k * HCAP : (k + 1) * HCAP, :] = chunk[:HCAP, :width]
        tail_ref[k * HCAP : (k + 1) * HCAP, :] = chunk[:HCAP, width:]
    used = 3 * units
    for j, w_ref in enumerate(weights):
        start = j * UNIT_BLOCK
        clear = used // 16 * 16
        if clear < UNIT_BLOCK:
            wide_ref[start + clear : start + UNIT_BLOCK, :] = jnp.zeros((UNIT_BLOCK - clear, width), BF)
        wide_ref[start : start + used, :] = w_ref[...]
    columns = 4 * UNIT_BLOCK
    block_chunks = min(CHUNK_BLOCK, chunk_count)
    block_rows = block_chunks * HCAP
    half_rows = block_rows // 2
    single = block_chunks == chunk_count

    def block(start):
        at = pl.ds(start, block_rows)
        prob = tail_ref[at, :].astype(F32).reshape(block_chunks, HCAP, TAIL)[:, :HALF, 0:1]
        prob = prob.reshape(half_rows, 1)
        pre = dot(rows_ref[at, :], wide_ref[...], NT).reshape(block_chunks, HCAP, columns)
        pre_x = pre[:, :HALF].reshape(half_rows, columns)
        pre_g = pre[:, HALF:].reshape(half_rows, columns)
        first = (iota(pre_x.shape, 1) & (UNIT_BLOCK - 1)) < units
        gate_grad, up_grad, weighted, prob_term = swiglu_back(
            pre_x,
            pltpu.roll(pre_x, columns - units, 1),
            pltpu.roll(pre_g, columns - 2 * units, 1),
            prob,
        )
        gate_grad, up_grad, weighted, prob_term = (
            jnp.where(first, value, 0.0) for value in (gate_grad, up_grad, weighted, prob_term)
        )
        grad_prob = jnp.sum(prob_term, axis=1, keepdims=True)
        x_side = gate_grad + pltpu.roll(up_grad, units, 1)
        g_side = pltpu.roll(weighted, 2 * units, 1)
        both = jnp.concatenate(
            [x_side.reshape(block_chunks, HALF, columns), g_side.reshape(block_chunks, HALF, columns)],
            axis=1,
        )
        both = both.reshape(block_rows, columns).astype(BF)
        dx = dot(x_side.astype(BF), wide_ref[...])
        for j in range(4):
            term = dot(both[:, j * UNIT_BLOCK : (j + 1) * UNIT_BLOCK], rows_ref[at, :], TN)
            add_to(terms[j] if single else sum_ref.at[j], term[:used], single)
        return dx, grad_prob

    if single:
        dx, grad_prob = block(0)
        write_rows(own_ref, dx[: half_rows // 2], grad_prob[: half_rows // 2])
        write_rows(send_ref, dx[half_rows // 2 :], grad_prob[half_rows // 2 :])
    else:
        sum_ref[...] = jnp.zeros_like(sum_ref)
        for out_ref, offset in ((own_ref, 0), (send_ref, chunk_count * HCAP // 2)):

            def step(index, carry, out_ref=out_ref, offset=offset):
                dx, grad_prob = block(pl.multiple_of(offset + index * block_rows, 16))
                at = pl.ds(pl.multiple_of(index * half_rows, 16), half_rows)
                write_rows(out_ref.at[at], dx, grad_prob)
                return carry

            lax.fori_loop(0, chunk_count // block_chunks // 2, step, 0)
        for j, out_ref in enumerate(terms):
            out_ref[...] = sum_ref[j].astype(out_ref.dtype)


def cold_kernel(message_count, *refs):
    messages = refs[:message_count]
    mine_x_ref, other_x_ref, gate_ref, up_ref, down_ref = refs[message_count : message_count + 5]
    own_ref, send_ref, *outs = refs[message_count + 5 : message_count + 10]
    data_ref, dx_ref, grad_ref, sum_ref, out_sem = refs[message_count + 10 :]
    total, width = data_ref.shape[0], gate_ref.shape[2]
    rows = COLD_ROWS
    single = rows == total
    stores = [
        pltpu.make_async_copy(grad_ref.at[j], ref.at[0], out_sem.at[j]) for j, ref in enumerate(outs)
    ]
    quarter = total // 4
    z_count = message_count // 2
    for flip, away_ref in enumerate((mine_x_ref, other_x_ref)):
        near = [
            ref[ref.shape[0] - COLD_PART :, :].astype(F32)[: 2 * CAP]
            for ref in messages[flip * z_count :][:z_count]
        ]
        start = 2 * flip * quarter
        data_ref[start : start + quarter, :] = jnp.concatenate(near, axis=0).astype(BF)
        data_ref[start + quarter : start + 2 * quarter, :] = away_ref[...]
    if not single:
        sum_ref[...] = jnp.zeros_like(sum_ref)

    def block(start):
        at = pl.ds(start, rows)
        data = data_ref[at, :width]
        first = jnp.where((iota((8, TAIL), 0) == 0) & (iota((8, TAIL), 1) == 0), 1.0, 0.0)
        prob = dot(first.astype(BF), data_ref[at, width:], NT)[0:1, :]
        pre_gate = dot(gate_ref[0], data, NT)
        pre_up = dot(up_ref[0], data, NT)
        back = pltpu.roll(dot(down_ref[0], data, NT), rows - CAP, 1)
        gate_grad, up_grad, weighted, prob_term = swiglu_back(pre_gate, pre_up, back, prob)
        x_lane = (iota(pre_gate.shape, 1) & 4) == 0
        gate_grad = jnp.where(x_lane, gate_grad, 0.0)
        up_grad = jnp.where(x_lane, up_grad, 0.0)
        weighted = pltpu.roll(jnp.where(x_lane, weighted, 0.0), CAP, 1)
        grad_prob = jnp.sum(jnp.where(x_lane, prob_term, 0.0), axis=0, keepdims=True)
        for j, grad in enumerate((gate_grad, up_grad, weighted)):
            term = dot(grad.astype(BF), data)
            if single:
                grad_ref[j] = term.astype(BF)
                stores[j].start()
            else:
                sum_ref[j] += term
        shape = (rows, rows // 2)
        row, col = iota(shape, 0), iota(shape, 1)
        pick = jnp.where(row == (col >> 2) * 8 + (col & 3), 1.0, 0.0).astype(BF)
        dx = dot(dot(gate_grad.astype(BF), pick).astype(BF), gate_ref[0], TN)
        dx = dx + dot(dot(up_grad.astype(BF), pick).astype(BF), up_ref[0], TN)
        shape = (rows // 2, rows)
        row, col = iota(shape, 0), iota(shape, 1)
        pick = jnp.where(col == (row >> 2) * 8 + (row & 3), 1.0, 0.0).astype(BF)
        high = grad_prob.astype(BF).astype(F32)
        row = iota((8, rows), 0)
        both = jnp.where(row == 0, high, jnp.where(row == 1, grad_prob - high, 0.0))
        both = dot(pick, both.astype(BF), NT)
        grad_prob = both[:, 0:1] + both[:, 1:2]
        half_at = pl.ds(start // 2 if single else pl.multiple_of(start // 2, 16), rows // 2)
        write_rows(dx_ref.at[half_at], dx, grad_prob)

    each_block(total, rows, block)
    own_ref[...] = dx_ref[: total // 4, :]
    dx_rows, dx_prob = read_rows(dx_ref[total // 4 :, :])
    write_rows(send_ref, dx_rows, dx_prob)
    if not single:
        for j in range(3):
            grad_ref[j] = sum_ref[j].astype(BF)
            stores[j].start()
    for store in stores:
        store.wait()


def add_kernel(hot_own_ref, hot_got_ref, cold_own_ref, cold_got_ref, *outs):
    def added(own_ref, got_ref):
        rows, prob = read_rows(own_ref[...])
        got_rows, got_prob = read_rows(got_ref[...])
        return jnp.concatenate([rows + got_rows, tail_lanes(prob + got_prob)], axis=1)

    hot = added(hot_own_ref, hot_got_ref)
    cold = added(cold_own_ref, cold_got_ref)
    half = cold.shape[0] // 2
    width = cold.shape[1] - TAIL
    for k, out_ref in enumerate(outs):
        at = k // 2 * 2 * CAP
        near, far = cold[at : at + 2 * CAP], cold[half + at : half + at + 2 * CAP]
        low = (iota(near.shape, 0) & 4) == 0
        if k % 2:
            part = jnp.where(low, pltpu.roll(near, CAP, 0), far)
        else:
            part = jnp.where(low, near, pltpu.roll(far, CAP, 0))
        rows = jnp.concatenate([hot[k * HALF : (k + 1) * HALF], part], axis=0)
        write_rows(out_ref, rows[:, :width], rows[:, width : width + 1])


def combine_kernel(*refs):
    *parts, own_ref, send_y_ref, send_x_ref = refs
    hot, cold = 0.0, []
    for ref in parts:
        rows, prob = read_rows(ref[...])
        both = jnp.concatenate([rows, tail_lanes(prob)], axis=1)
        hot = hot + both[:HALF]
        cold.append(both[HALF:])
    low = (iota(cold[0].shape, 0) & 4) == 0
    mine, other = [], []
    for even, odd in zip(cold[0::2], cold[1::2]):
        mine.append(jnp.where(low, even, pltpu.roll(odd, CAP, 0)))
        other.append(jnp.where(low, pltpu.roll(even, CAP, 0), odd))
    rows = jnp.concatenate([hot] + mine, axis=0)
    away = jnp.concatenate(other, axis=0)
    width = rows.shape[1] - TAIL
    own_ref[...] = rows
    write_rows(send_y_ref, rows[:, :width], rows[:, width : width + 1])
    write_rows(send_x_ref, away[:, :width], away[:, width : width + 1])


def finish_kernel(base, own_ref, y_ref, x_ref, xy_ref, pos_ref, dx_ref, prob_ref):
    pair = lax.axis_index("pair")
    me = lax.axis_index("dp")
    z, x = me // 4, (me // 2) % 2
    half = dx_ref.shape[0]
    pos = jnp.where(pair == 0, pos_ref[:, :half], pos_ref[:, half:])

    def cold_target(row, side):
        return (2 * (z ^ (row >> 2)) + side) * CAP + (row & 3)

    def with_hot(side):
        row = iota((own_ref.shape[0], half), 0)
        return jnp.where(row < HALF, base + HALF * side + row, cold_target(row - HALF, x))

    away = cold_target(iota((x_ref.shape[0], half), 0), 1 - x)
    total = 0.0
    grad_prob = [0.0] * TOP
    for ref, target in (
        (own_ref, with_hot(pair)),
        (y_ref, with_hot(1 - pair)),
        (x_ref, away),
        (xy_ref, away),
    ):
        routes = [pos[k : k + 1, :] == target for k in range(TOP)]
        onehot = jnp.where(routes[0] | routes[1], 1.0, 0.0).astype(BF)
        rows, prob = read_rows(ref[...])
        high = rows.astype(BF)
        total = total + dot(onehot, high, TN)
        if ref.dtype == F32:
            total = total + dot(onehot, (rows - high.astype(F32)).astype(BF), TN)
        for k in range(TOP):
            terms = jnp.sum(jnp.where(routes[k], prob, 0.0), axis=0, keepdims=True)
            grad_prob[k] = grad_prob[k] + terms
    dx_ref[...] = total.astype(BF)
    for k in range(TOP):
        prob_ref[k : k + 1, :] = grad_prob[k]


def sum_kernel(own_ref, a_ref, b_ref, c_ref, gate_ref, up_ref, down_ref):
    total = own_ref[...] + a_ref[...].astype(F32) + b_ref[...].astype(F32) + c_ref[...].astype(F32)
    units = gate_ref.shape[0]
    for index, out_ref in enumerate((gate_ref, up_ref, down_ref)):
        out_ref[...] = total[index * units : (index + 1) * units].astype(BF)


def call(kernel, outs, name, scratch=(), smem=(), out_hbm=(), limit=0):
    def run(*args):
        moved = sum(a.size * a.dtype.itemsize for a in args)
        moved += sum(o.size * o.dtype.itemsize for o in outs)
        return pl.pallas_call(
            kernel,
            out_shape=outs,
            in_specs=[
                pl.BlockSpec(memory_space=pltpu.SMEM if i in smem else pltpu.VMEM)
                for i in range(len(args))
            ],
            out_specs=[
                pl.BlockSpec(memory_space=pltpu.HBM if i in out_hbm else pltpu.VMEM)
                for i in range(len(outs))
            ],
            scratch_shapes=[pltpu.VMEM(*s) if isinstance(s, tuple) else s for s in scratch],
            compiler_params=pltpu.CompilerParams(
                vmem_limit_bytes=limit or min(VMEM_LIMIT, VMEM_BASE + 3 * moved // 2)
            ),
            cost_estimate=pl.CostEstimate(flops=1024, bytes_accessed=1024, transcendentals=0),
            name=name,
        )(*args)

    return run


def local(
    tokens,
    grad_out,
    gate_probs,
    expert_ids,
    route_slots,
    hot_flags,
    owner_slot,
    cold_gate,
    cold_up,
    cold_down,
    hot_gate,
    hot_up,
    hot_down,
):
    count = lax.axis_size("dp")
    z_count = count // 4
    chunk_count = 2 * z_count
    token_count, width = tokens.shape
    lanes = width + TAIL
    units = hot_gate.shape[0]
    base = (count // 2) * CAP
    shape = jax.ShapeDtypeStruct
    half = token_count // 2
    pad = -units % 8

    def swap(value, mask):
        flip_dp, flip_pair = 2 * (mask & 1), mask >> 1
        perm = [
            (2 * i + p, 2 * (i ^ flip_dp) + (p ^ flip_pair)) for i in range(count) for p in range(2)
        ]
        return lax.ppermute(value, ("dp", "pair"), perm)

    def along_z(value, k):
        perm = [(i, 4 * ((i // 4) ^ k) + i % 4) for i in range(count)]
        return lax.ppermute(value, "dp", perm)

    def all_along_z(values):
        order = sorted(range(1, z_count), key=lambda k: (k == 1, k))
        got = {k: along_z(values[k], k) for k in order}
        return [values[0]] + [got[k] for k in range(1, z_count)]

    def other_core(value):
        return lax.ppermute(value, "dp", [(i, i ^ 1) for i in range(count)])

    hot_weights = [jnp.pad(w, ((0, pad), (0, 0))) if pad else w for w in (hot_gate, hot_up, hot_down)]
    units_padded = units + pad
    used = 3 * units_padded
    cold_rows = z_count * COLD_PART
    message = shape((HCAP + COLD_PART, lanes), BF)
    by_relay = range(3, z_count, 2)
    pos, hot_own, *messages = call(
        functools.partial(dispatch_kernel, base),
        [shape((TOP, token_count), jnp.int32), shape((used, width), BF)]
        + [shape((COLD_PART, lanes), BF) if k in by_relay else message for k in range(z_count)],
        "dispatch",
        scratch=[((HCAP + cold_rows, lanes), BF)],
        smem=(5, 6),
        limit=VMEM_LIMIT,
    )(
        tokens,
        grad_out,
        gate_probs.T,
        expert_ids.T,
        route_slots.T,
        hot_flags,
        owner_slot,
        *hot_weights,
    )

    chunks = all_along_z(messages)
    by_pair = swap(hot_own, 2)
    by_x = swap(hot_own, 1)
    first_out, hot_own, _ = lax.optimization_barrier((messages[0], hot_own, chunks[1]))
    first_out, hot_own = call(
        copy_kernel, [message, shape(hot_own.shape, BF)], "own_rows"
    )(first_out, hot_own)
    chunks[0] = first_out
    by_pair_out, first_out, hot_own = lax.optimization_barrier((by_pair, first_out, hot_own))
    weights = [hot_own, by_x, by_pair, swap(by_pair_out, 1)]
    (away,) = call(away_kernel, [shape((cold_rows // 2, lanes), BF)], "cold_away")(*chunks)
    cold_chunks = list(chunks)
    for k in by_relay:
        chunks[k] = along_z(chunks[k - 1], 1)
    other_chunks = [other_core(chunk) for chunk in chunks]
    cold_chunks += [
        other_core(cold_chunks[k]) if k in by_relay else other_chunks[k] for k in range(z_count)
    ]
    chunks = chunks + other_chunks
    cold_mine = swap(away, 1)
    cold_other = other_core(cold_mine)

    cold_units = cold_gate.shape[1]
    cold_shape = shape(cold_gate.shape, BF)
    all_rows = chunk_count * HCAP
    half_rows = chunk_count * HALF // 2
    term = shape((used, width), BF)
    hot_dx, hot_dx_out, own_term, *sent_terms = call(
        functools.partial(hot_kernel, chunk_count, units_padded),
        [
            shape((half_rows, lanes), F32),
            shape((half_rows, lanes), BF),
            shape(term.shape, F32),
            term,
            term,
            term,
        ],
        "hot",
        scratch=[
            ((all_rows, width), BF),
            ((all_rows, TAIL), BF),
            ((4 * UNIT_BLOCK, width), BF),
            ((4, used, width) if chunk_count > CHUNK_BLOCK else (8, 128), F32),
        ],
    )(*chunks, *weights)

    cold_mine, hot_dx = lax.optimization_barrier((cold_mine, hot_dx))
    cold_own, cold_out, grad_cold_gate, grad_cold_up, grad_cold_down = call(
        functools.partial(cold_kernel, chunk_count),
        [shape((cold_rows // 2, lanes), F32), shape((cold_rows // 2, lanes), BF)] + [cold_shape] * 3,
        "cold",
        scratch=[
            ((2 * cold_rows, lanes), BF),
            ((cold_rows, lanes), F32),
            ((3, cold_units, width), BF),
            ((3, cold_units, width) if 2 * cold_rows > COLD_ROWS else (8, 128), F32),
            pltpu.SemaphoreType.DMA((3,)),
        ],
        out_hbm=(2, 3, 4),
    )(*cold_chunks, cold_mine, cold_other, cold_gate, cold_up, cold_down)

    hot_got, cold_got = other_core(hot_dx_out), other_core(cold_out)
    part = (HALF + 2 * CAP, lanes)
    parts = call(
        add_kernel, [shape(part, F32)] + [shape(part, BF)] * (z_count - 1), "add_cores"
    )(hot_dx, hot_got, cold_own, cold_got)
    term_x, _ = lax.optimization_barrier((sent_terms[0], cold_mine))
    got_x, got_y = swap(term_x, 1), swap(sent_terms[1], 2)
    last_term, cold_out = lax.optimization_barrier((sent_terms[2], cold_out))
    *parts, got_x, got_y = lax.optimization_barrier((*parts, got_x, got_y))
    parts = all_along_z(parts)
    got_terms = [got_x, got_y, swap(last_term, 3)]

    cold_back = z_count * CAP
    own_rows, send_y, send_x = call(
        combine_kernel,
        [
            shape((HALF + cold_back, lanes), F32),
            shape((HALF + cold_back, lanes), BF),
            shape((cold_back, lanes), BF),
        ],
        "combine",
    )(*parts)
    rows_y, rows_x, rows_xy = swap(send_y, 2), swap(send_x, 1), swap(send_x, 3)
    out_shape = shape((units_padded, width), BF)
    hot_grads = call(sum_kernel, [out_shape] * 3, "hot_sum")(
        own_term, *got_terms
    )
    own_rows, *hot_grads = lax.optimization_barrier((own_rows, *hot_grads))
    dx, prob_t = call(
        functools.partial(finish_kernel, base),
        [shape((half, width), BF), shape((TOP, half), F32)],
        "finish",
    )(own_rows, rows_y, rows_x, rows_xy, pos)

    if pad:
        hot_grads = [value[:units] for value in hot_grads]
    return (dx, prob_t.T, grad_cold_gate, grad_cold_up, grad_cold_down, *hot_grads)


def solution(mesh):
    return jax.shard_map(
        local,
        mesh=mesh,
        in_specs=(
            P("dp", None),
            P("dp", None),
            P("dp", None),
            P("dp", None),
            P("dp", None),
            P(),
            P(),
            P("dp", "pair", None),
            P("dp", "pair", None),
            P("dp", "pair", None),
            P(("dp", "pair"), None),
            P(("dp", "pair"), None),
            P(("dp", "pair"), None),
        ),
        out_specs=(
            P(("dp", "pair"), None),
            P(("dp", "pair"), None),
            P("dp", "pair", None),
            P("dp", "pair", None),
            P("dp", "pair", None),
            P(("dp", "pair"), None),
            P(("dp", "pair"), None),
            P(("dp", "pair"), None),
        ),
        check_vma=False,
    )
```

```python
import functools

import jax
import jax.numpy as jnp
from jax import lax
from jax.experimental import pallas as pl
from jax.experimental.pallas import tpu as pltpu
from jax.sharding import PartitionSpec as P

TOP = 2
CAP = 4
HCAP = 48
HALF = HCAP // 2
TAIL = 128
CHUNK_BLOCK = 8
GATHER_BLOCK = 112
COLD_PART = 4 * CAP
MESSAGE = HCAP + COLD_PART
COLD_ROWS = 128
UNIT_BLOCK = 128
BF = jnp.bfloat16
F32 = jnp.float32
VMEM_LIMIT = 56 * 1024 * 1024
VMEM_BASE = 12 * 1024 * 1024

NT = (((1,), (1,)), ((), ()))
TN = (((0,), (0,)), ((), ()))


def dot(a, b, dims=(((1,), (0,)), ((), ()))):
    return lax.dot_general(a, b, dims, preferred_element_type=F32)


def iota(shape, dim):
    return lax.broadcasted_iota(jnp.int32, shape, dim)


def positions(ids, slots, flags_ref, owner_ref, base):
    hot = jnp.zeros_like(ids)
    own = jnp.zeros_like(ids)
    for e in range(flags_ref.shape[0]):
        named = ids == e
        hot = jnp.where(named, flags_ref[e], hot)
        own = jnp.where(named, owner_ref[e], own)
    cold_pos = jnp.where(slots < CAP, own * CAP + slots, -1)
    hot_pos = jnp.where(slots < HCAP, base + slots, -1)
    return jnp.where(hot == 1, hot_pos, cold_pos)


def tail_lanes(first, second=None):
    lane = iota((first.shape[0], TAIL), 1)
    out = jnp.where(lane == 0, first, 0.0)
    if second is not None:
        out = jnp.where(lane == 1, second, out)
    return out


def split_tail(value):
    high = value.astype(BF).astype(F32)
    return tail_lanes(high, value - high)


def each_block(total, size, body):
    if total == size:
        body(0)
    else:

        def step(block, carry):
            body(pl.multiple_of(block * size, size))
            return carry

        lax.fori_loop(0, total // size, step, 0)


def add_to(ref, value, single):
    if single:
        ref[...] = value.astype(ref.dtype)
    else:
        ref[...] += value


def gather_rows(out_ref, start, target, is_grad, pos, prob, tok_ref, grad_ref):
    width = tok_ref.shape[1]
    at = pl.ds(start, target.shape[0])
    first = pos[0:1, :] == target
    second = pos[1:2, :] == target
    chosen = jnp.where(first | second, 1.0, 0.0)
    rows = dot(jnp.where(is_grad, 0.0, chosen).astype(BF), tok_ref[...]) + dot(
        jnp.where(is_grad, chosen, 0.0).astype(BF), grad_ref[...]
    )
    out_ref[at, :width] = rows.astype(BF)
    weight = jnp.where(first, prob[0:1, :], 0.0) + jnp.where(second, prob[1:2, :], 0.0)
    weight = jnp.sum(jnp.where(is_grad, 0.0, weight), axis=1, keepdims=True)
    out_ref[at, width:] = tail_lanes(weight).astype(BF)


def dispatch_kernel(base, *refs):
    tok_ref, grad_ref, prob_ref, ids_ref, slot_ref, flags_ref, owner_ref = refs[:7]
    gate_ref, up_ref, down_ref, pos_ref, weight_ref, *messages, rows_ref = refs[7:]
    pair = lax.axis_index("pair")
    me = lax.axis_index("dp")
    z, x = me // 4, (me // 2) % 2
    pos = positions(ids_ref[...], slot_ref[...], flags_ref, owner_ref, base)
    pos_ref[...] = pos
    joined = [ref[...].astype(F32) for ref in (gate_ref, up_ref, down_ref)]
    weight_ref[...] = jnp.concatenate(joined, axis=0).astype(BF)
    prob = prob_ref[...].astype(F32)

    def block(start):
        row = start + iota((GATHER_BLOCK, tok_ref.shape[0]), 0)
        hot = row < HCAP
        cold_row = row - HCAP
        chip = 2 * (z ^ (cold_row >> 4)) + (x ^ ((cold_row >> 3) & 1))
        hot_target = base + HALF * pair + jnp.where(row >= HALF, row - HALF, row)
        target = jnp.where(hot, hot_target, chip * CAP + (row & 3))
        is_grad = (hot & (row >= HALF)) | (~hot & ((row & 4) != 0))
        gather_rows(rows_ref, start, target, is_grad, pos, prob, tok_ref, grad_ref)

    each_block(rows_ref.shape[0], GATHER_BLOCK, block)
    for message, k in zip(messages, [0, 1] + list(range(2, 2 * len(messages) - 2, 2))):
        message[:COLD_PART, :] = rows_ref[HCAP + k * COLD_PART : HCAP + (k + 1) * COLD_PART, :]
        message[COLD_PART:MESSAGE, :] = rows_ref[:HCAP, :]
        if k > 1:
            message[MESSAGE:, :] = rows_ref[HCAP + (k + 1) * COLD_PART : HCAP + (k + 2) * COLD_PART, :]


def copy_kernel(*refs):
    half = len(refs) // 2
    for in_ref, out_ref in zip(refs[:half], refs[half:]):
        out_ref[...] = in_ref[...]


def relay_kernel(in_ref, out_ref):
    out_ref[:COLD_PART, :] = in_ref[MESSAGE:, :]
    out_ref[COLD_PART:, :] = in_ref[COLD_PART:MESSAGE, :]


def away_kernel(*refs):
    *messages, out_ref = refs
    rows = [ref[:COLD_PART, :].astype(F32)[2 * CAP :] for ref in messages]
    out_ref[...] = jnp.concatenate(rows, axis=0).astype(BF)


def swiglu_back(pre_gate, pre_up, back, prob):
    sig = 1.0 / (1.0 + jnp.exp(-pre_gate))
    act = pre_gate * sig
    hidden = act * pre_up
    scaled = prob * back
    gate_grad = scaled * pre_up * sig * (1.0 + pre_gate * (1.0 - sig))
    return gate_grad, scaled * act, prob * hidden, hidden * back


def write_rows(out_ref, rows, prob):
    width = rows.shape[1]
    out_ref[:, :width] = rows.astype(out_ref.dtype)
    tail = tail_lanes(prob) if out_ref.dtype == F32 else split_tail(prob).astype(BF)
    out_ref[:, width:] = tail


def read_rows(value):
    value = value.astype(F32)
    width = value.shape[1] - TAIL
    return value[:, :width], value[:, width : width + 1] + value[:, width + 1 : width + 2]


def hot_kernel(chunk_count, units, *refs):
    chunks = refs[:chunk_count]
    weights = refs[chunk_count : chunk_count + 4]
    own_ref, send_ref, *terms = refs[chunk_count + 4 : chunk_count + 10]
    rows_ref, tail_ref, wide_ref, sum_ref = refs[chunk_count + 10 :]
    width = rows_ref.shape[1]
    for k, chunk in enumerate(chunks):
        rows_ref[k * HCAP : (k + 1) * HCAP, :] = chunk[COLD_PART:MESSAGE, :width]
        tail_ref[k * HCAP : (k + 1) * HCAP, :] = chunk[COLD_PART:MESSAGE, width:]
    used = 3 * units
    for j, w_ref in enumerate(weights):
        start = j * UNIT_BLOCK
        clear = used // 16 * 16
        if clear < UNIT_BLOCK:
            wide_ref[start + clear : start + UNIT_BLOCK, :] = jnp.zeros((UNIT_BLOCK - clear, width), BF)
        wide_ref[start : start + used, :] = w_ref[...]
    columns = 4 * UNIT_BLOCK
    block_chunks = min(CHUNK_BLOCK, chunk_count)
    block_rows = block_chunks * HCAP
    half_rows = block_rows // 2
    single = block_chunks == chunk_count

    def block(start):
        at = pl.ds(start, block_rows)
        prob = tail_ref[at, :].astype(F32).reshape(block_chunks, HCAP, TAIL)[:, :HALF, 0:1]
        prob = prob.reshape(half_rows, 1)
        pre = dot(rows_ref[at, :], wide_ref[...], NT).reshape(block_chunks, HCAP, columns)
        pre_x = pre[:, :HALF].reshape(half_rows, columns)
        pre_g = pre[:, HALF:].reshape(half_rows, columns)
        first = (iota(pre_x.shape, 1) & (UNIT_BLOCK - 1)) < units
        gate_grad, up_grad, weighted, prob_term = swiglu_back(
            pre_x,
            pltpu.roll(pre_x, columns - units, 1),
            pltpu.roll(pre_g, columns - 2 * units, 1),
            prob,
        )
        gate_grad, up_grad, weighted, prob_term = (
            jnp.where(first, value, 0.0) for value in (gate_grad, up_grad, weighted, prob_term)
        )
        grad_prob = jnp.sum(prob_term, axis=1, keepdims=True)
        x_side = gate_grad + pltpu.roll(up_grad, units, 1)
        g_side = pltpu.roll(weighted, 2 * units, 1)
        both = jnp.concatenate(
            [x_side.reshape(block_chunks, HALF, columns), g_side.reshape(block_chunks, HALF, columns)],
            axis=1,
        )
        both = both.reshape(block_rows, columns).astype(BF)
        dx = dot(x_side.astype(BF), wide_ref[...])
        for j in range(4):
            term = dot(both[:, j * UNIT_BLOCK : (j + 1) * UNIT_BLOCK], rows_ref[at, :], TN)
            add_to(terms[j] if single else sum_ref.at[j], term[:used], single)
        return dx, grad_prob

    if single:
        dx, grad_prob = block(0)
        write_rows(own_ref, dx[: half_rows // 2], grad_prob[: half_rows // 2])
        write_rows(send_ref, dx[half_rows // 2 :], grad_prob[half_rows // 2 :])
    else:
        sum_ref[...] = jnp.zeros_like(sum_ref)
        for out_ref, offset in ((own_ref, 0), (send_ref, chunk_count * HCAP // 2)):

            def step(index, carry, out_ref=out_ref, offset=offset):
                dx, grad_prob = block(pl.multiple_of(offset + index * block_rows, 16))
                at = pl.ds(pl.multiple_of(index * half_rows, 16), half_rows)
                write_rows(out_ref.at[at], dx, grad_prob)
                return carry

            lax.fori_loop(0, chunk_count // block_chunks // 2, step, 0)
        for j, out_ref in enumerate(terms):
            out_ref[...] = sum_ref[j].astype(out_ref.dtype)


def cold_kernel(message_count, *refs):
    messages = refs[:message_count]
    mine_x_ref, other_x_ref, gate_ref, up_ref, down_ref = refs[message_count : message_count + 5]
    own_ref, send_ref, *outs = refs[message_count + 5 : message_count + 10]
    data_ref, dx_ref, grad_ref, sum_ref, out_sem = refs[message_count + 10 :]
    total, width = data_ref.shape[0], gate_ref.shape[2]
    rows = COLD_ROWS
    single = rows == total
    stores = [
        pltpu.make_async_copy(grad_ref.at[j], ref.at[0], out_sem.at[j]) for j, ref in enumerate(outs)
    ]
    quarter = total // 4
    z_count = message_count // 2
    for flip, away_ref in enumerate((mine_x_ref, other_x_ref)):
        near = [
            ref[:COLD_PART, :].astype(F32)[: 2 * CAP]
            for ref in messages[flip * z_count :][:z_count]
        ]
        start = 2 * flip * quarter
        data_ref[start : start + quarter, :] = jnp.concatenate(near, axis=0).astype(BF)
        data_ref[start + quarter : start + 2 * quarter, :] = away_ref[...]
    if not single:
        sum_ref[...] = jnp.zeros_like(sum_ref)

    def block(start):
        at = pl.ds(start, rows)
        data = data_ref[at, :width]
        first = jnp.where((iota((8, TAIL), 0) == 0) & (iota((8, TAIL), 1) == 0), 1.0, 0.0)
        prob = dot(first.astype(BF), data_ref[at, width:], NT)[0:1, :]
        pre_gate = dot(gate_ref[0], data, NT)
        pre_up = dot(up_ref[0], data, NT)
        back = pltpu.roll(dot(down_ref[0], data, NT), rows - CAP, 1)
        gate_grad, up_grad, weighted, prob_term = swiglu_back(pre_gate, pre_up, back, prob)
        x_lane = (iota(pre_gate.shape, 1) & 4) == 0
        gate_grad = jnp.where(x_lane, gate_grad, 0.0)
        up_grad = jnp.where(x_lane, up_grad, 0.0)
        weighted = pltpu.roll(jnp.where(x_lane, weighted, 0.0), CAP, 1)
        grad_prob = jnp.sum(jnp.where(x_lane, prob_term, 0.0), axis=0, keepdims=True)
        for j, grad in enumerate((gate_grad, up_grad, weighted)):
            term = dot(grad.astype(BF), data)
            if single:
                grad_ref[j] = term.astype(BF)
                stores[j].start()
            else:
                sum_ref[j] += term
        shape = (rows, rows // 2)
        row, col = iota(shape, 0), iota(shape, 1)
        pick = jnp.where(row == (col >> 2) * 8 + (col & 3), 1.0, 0.0).astype(BF)
        dx = dot(dot(gate_grad.astype(BF), pick).astype(BF), gate_ref[0], TN)
        dx = dx + dot(dot(up_grad.astype(BF), pick).astype(BF), up_ref[0], TN)
        shape = (rows // 2, rows)
        row, col = iota(shape, 0), iota(shape, 1)
        pick = jnp.where(col == (row >> 2) * 8 + (row & 3), 1.0, 0.0).astype(BF)
        high = grad_prob.astype(BF).astype(F32)
        row = iota((8, rows), 0)
        both = jnp.where(row == 0, high, jnp.where(row == 1, grad_prob - high, 0.0))
        both = dot(pick, both.astype(BF), NT)
        grad_prob = both[:, 0:1] + both[:, 1:2]
        half_at = pl.ds(start // 2 if single else pl.multiple_of(start // 2, 16), rows // 2)
        write_rows(dx_ref.at[half_at], dx, grad_prob)

    each_block(total, rows, block)
    own_ref[...] = dx_ref[: total // 4, :]
    dx_rows, dx_prob = read_rows(dx_ref[total // 4 :, :])
    write_rows(send_ref, dx_rows, dx_prob)
    if not single:
        for j in range(3):
            grad_ref[j] = sum_ref[j].astype(BF)
            stores[j].start()
    for store in stores:
        store.wait()


def add_kernel(hot_own_ref, hot_got_ref, cold_own_ref, cold_got_ref, *outs):
    def added(own_ref, got_ref):
        rows, prob = read_rows(own_ref[...])
        got_rows, got_prob = read_rows(got_ref[...])
        return jnp.concatenate([rows + got_rows, tail_lanes(prob + got_prob)], axis=1)

    hot = added(hot_own_ref, hot_got_ref)
    cold = added(cold_own_ref, cold_got_ref)
    half = cold.shape[0] // 2
    width = cold.shape[1] - TAIL
    for k, out_ref in enumerate(outs):
        at = k // 2 * 2 * CAP
        near, far = cold[at : at + 2 * CAP], cold[half + at : half + at + 2 * CAP]
        low = (iota(near.shape, 0) & 4) == 0
        if k % 2:
            part = jnp.where(low, pltpu.roll(near, CAP, 0), far)
        else:
            part = jnp.where(low, near, pltpu.roll(far, CAP, 0))
        rows = jnp.concatenate([hot[k * HALF : (k + 1) * HALF], part], axis=0)
        write_rows(out_ref, rows[:, :width], rows[:, width : width + 1])


def combine_kernel(*refs):
    *parts, own_ref, send_y_ref, send_x_ref = refs
    hot, cold = 0.0, []
    for ref in parts:
        rows, prob = read_rows(ref[...])
        both = jnp.concatenate([rows, tail_lanes(prob)], axis=1)
        hot = hot + both[:HALF]
        cold.append(both[HALF:])
    low = (iota(cold[0].shape, 0) & 4) == 0
    mine, other = [], []
    for even, odd in zip(cold[0::2], cold[1::2]):
        mine.append(jnp.where(low, even, pltpu.roll(odd, CAP, 0)))
        other.append(jnp.where(low, pltpu.roll(even, CAP, 0), odd))
    rows = jnp.concatenate([hot] + mine, axis=0)
    away = jnp.concatenate(other, axis=0)
    width = rows.shape[1] - TAIL
    own_ref[...] = rows
    write_rows(send_y_ref, rows[:, :width], rows[:, width : width + 1])
    write_rows(send_x_ref, away[:, :width], away[:, width : width + 1])


def finish_kernel(base, own_ref, y_ref, x_ref, xy_ref, pos_ref, dx_ref, prob_ref):
    pair = lax.axis_index("pair")
    me = lax.axis_index("dp")
    z, x = me // 4, (me // 2) % 2
    half = dx_ref.shape[0]
    pos = jnp.where(pair == 0, pos_ref[:, :half], pos_ref[:, half:])

    def cold_target(row, side):
        return (2 * (z ^ (row >> 2)) + side) * CAP + (row & 3)

    def with_hot(side):
        row = iota((own_ref.shape[0], half), 0)
        return jnp.where(row < HALF, base + HALF * side + row, cold_target(row - HALF, x))

    away = cold_target(iota((x_ref.shape[0], half), 0), 1 - x)
    total = 0.0
    grad_prob = [0.0] * TOP
    for ref, target in (
        (own_ref, with_hot(pair)),
        (y_ref, with_hot(1 - pair)),
        (x_ref, away),
        (xy_ref, away),
    ):
        routes = [pos[k : k + 1, :] == target for k in range(TOP)]
        onehot = jnp.where(routes[0] | routes[1], 1.0, 0.0).astype(BF)
        rows, prob = read_rows(ref[...])
        high = rows.astype(BF)
        total = total + dot(onehot, high, TN)
        if ref.dtype == F32:
            total = total + dot(onehot, (rows - high.astype(F32)).astype(BF), TN)
        for k in range(TOP):
            terms = jnp.sum(jnp.where(routes[k], prob, 0.0), axis=0, keepdims=True)
            grad_prob[k] = grad_prob[k] + terms
    dx_ref[...] = total.astype(BF)
    for k in range(TOP):
        prob_ref[k : k + 1, :] = grad_prob[k]


def sum_kernel(own_ref, a_ref, b_ref, c_ref, gate_ref, up_ref, down_ref):
    total = own_ref[...] + a_ref[...].astype(F32) + b_ref[...].astype(F32) + c_ref[...].astype(F32)
    units = gate_ref.shape[0]
    for index, out_ref in enumerate((gate_ref, up_ref, down_ref)):
        out_ref[...] = total[index * units : (index + 1) * units].astype(BF)


def call(kernel, outs, name, scratch=(), smem=(), out_hbm=(), limit=0):
    def run(*args):
        moved = sum(a.size * a.dtype.itemsize for a in args)
        moved += sum(o.size * o.dtype.itemsize for o in outs)
        return pl.pallas_call(
            kernel,
            out_shape=outs,
            in_specs=[
                pl.BlockSpec(memory_space=pltpu.SMEM if i in smem else pltpu.VMEM)
                for i in range(len(args))
            ],
            out_specs=[
                pl.BlockSpec(memory_space=pltpu.HBM if i in out_hbm else pltpu.VMEM)
                for i in range(len(outs))
            ],
            scratch_shapes=[pltpu.VMEM(*s) if isinstance(s, tuple) else s for s in scratch],
            compiler_params=pltpu.CompilerParams(
                vmem_limit_bytes=limit or min(VMEM_LIMIT, VMEM_BASE + 3 * moved // 2)
            ),
            cost_estimate=pl.CostEstimate(flops=1024, bytes_accessed=1024, transcendentals=0),
            name=name,
        )(*args)

    return run


def local(
    tokens,
    grad_out,
    gate_probs,
    expert_ids,
    route_slots,
    hot_flags,
    owner_slot,
    cold_gate,
    cold_up,
    cold_down,
    hot_gate,
    hot_up,
    hot_down,
):
    count = lax.axis_size("dp")
    z_count = count // 4
    chunk_count = 2 * z_count
    token_count, width = tokens.shape
    lanes = width + TAIL
    units = hot_gate.shape[0]
    base = (count // 2) * CAP
    shape = jax.ShapeDtypeStruct
    half = token_count // 2
    pad = -units % 8

    def swap(value, mask):
        flip_dp, flip_pair = 2 * (mask & 1), mask >> 1
        perm = [
            (2 * i + p, 2 * (i ^ flip_dp) + (p ^ flip_pair)) for i in range(count) for p in range(2)
        ]
        return lax.ppermute(value, ("dp", "pair"), perm)

    def along_z(value, k):
        perm = [(i, 4 * ((i // 4) ^ k) + i % 4) for i in range(count)]
        return lax.ppermute(value, "dp", perm)

    def all_along_z(values):
        order = sorted(range(1, z_count), key=lambda k: (k == 1, k))
        got = {k: along_z(values[k], k) for k in order}
        return [values[0]] + [got[k] for k in range(1, z_count)]

    def other_core(value):
        return lax.ppermute(value, "dp", [(i, i ^ 1) for i in range(count)])

    hot_weights = [jnp.pad(w, ((0, pad), (0, 0))) if pad else w for w in (hot_gate, hot_up, hot_down)]
    units_padded = units + pad
    used = 3 * units_padded
    cold_rows = z_count * COLD_PART
    message = shape((MESSAGE, lanes), BF)
    long_message = shape((MESSAGE + COLD_PART, lanes), BF)
    pos, hot_own, *messages = call(
        functools.partial(dispatch_kernel, base),
        [shape((TOP, token_count), jnp.int32), shape((used, width), BF)]
        + [message, message]
        + [long_message] * (z_count // 2 - 1),
        "dispatch",
        scratch=[((HCAP + cold_rows, lanes), BF)],
        smem=(5, 6),
        limit=VMEM_LIMIT,
    )(
        tokens,
        grad_out,
        gate_probs.T,
        expert_ids.T,
        route_slots.T,
        hot_flags,
        owner_slot,
        *hot_weights,
    )

    chunks = [messages[0], along_z(messages[1], 1)]
    for index in range(2, len(messages)):
        direct = along_z(messages[index], 2 * index - 2)
        (onward,) = call(relay_kernel, [message], "relay_rows")(direct)
        chunks += [direct, along_z(onward, 1)]
    first_out, hot_out, _ = lax.optimization_barrier((messages[0], hot_own, chunks[1]))
    first_out, hot_out = call(
        copy_kernel, [message, shape(hot_own.shape, BF)], "own_rows"
    )(first_out, hot_out)
    chunks[0] = first_out
    weights = [hot_out] + [swap(hot_own, mask) for mask in (1, 2, 3)]
    (away,) = call(away_kernel, [shape((cold_rows // 2, lanes), BF)], "cold_away")(*chunks)
    chunks = chunks + [other_core(chunk) for chunk in chunks]
    cold_mine = swap(away, 1)
    cold_other = other_core(cold_mine)

    cold_units = cold_gate.shape[1]
    cold_shape = shape(cold_gate.shape, BF)
    all_rows = chunk_count * HCAP
    half_rows = chunk_count * HALF // 2
    term = shape((used, width), BF)
    hot_dx, hot_dx_out, own_term, *sent_terms = call(
        functools.partial(hot_kernel, chunk_count, units_padded),
        [
            shape((half_rows, lanes), F32),
            shape((half_rows, lanes), BF),
            shape(term.shape, F32),
            term,
            term,
            term,
        ],
        "hot",
        scratch=[
            ((all_rows, width), BF),
            ((all_rows, TAIL), BF),
            ((4 * UNIT_BLOCK, width), BF),
            ((4, used, width) if chunk_count > CHUNK_BLOCK else (8, 128), F32),
        ],
    )(*chunks, *weights)

    cold_mine, hot_dx = lax.optimization_barrier((cold_mine, hot_dx))
    cold_own, cold_out, grad_cold_gate, grad_cold_up, grad_cold_down = call(
        functools.partial(cold_kernel, chunk_count),
        [shape((cold_rows // 2, lanes), F32), shape((cold_rows // 2, lanes), BF)] + [cold_shape] * 3,
        "cold",
        scratch=[
            ((2 * cold_rows, lanes), BF),
            ((cold_rows, lanes), F32),
            ((3, cold_units, width), BF),
            ((3, cold_units, width) if 2 * cold_rows > COLD_ROWS else (8, 128), F32),
            pltpu.SemaphoreType.DMA((3,)),
        ],
        out_hbm=(2, 3, 4),
    )(*chunks, cold_mine, cold_other, cold_gate, cold_up, cold_down)

    hot_got, cold_got = other_core(hot_dx_out), other_core(cold_out)
    part = (HALF + 2 * CAP, lanes)
    parts = call(
        add_kernel, [shape(part, F32)] + [shape(part, BF)] * (z_count - 1), "add_cores"
    )(hot_dx, hot_got, cold_own, cold_got)
    term_x, _ = lax.optimization_barrier((sent_terms[0], cold_mine))
    got_x, got_y = swap(term_x, 1), swap(sent_terms[1], 2)
    *parts, got_x, got_y, last_term = lax.optimization_barrier((*parts, got_x, got_y, sent_terms[2]))
    parts = all_along_z(parts)
    got_terms = [got_x, got_y, swap(last_term, 3)]

    cold_back = z_count * CAP
    own_rows, send_y, send_x = call(
        combine_kernel,
        [
            shape((HALF + cold_back, lanes), F32),
            shape((HALF + cold_back, lanes), BF),
            shape((cold_back, lanes), BF),
        ],
        "combine",
    )(*parts)
    rows_y, rows_x, rows_xy = swap(send_y, 2), swap(send_x, 1), swap(send_x, 3)
    out_shape = shape((units_padded, width), BF)
    hot_grads = call(sum_kernel, [out_shape] * 3, "hot_sum")(
        own_term, *got_terms
    )
    own_rows, *hot_grads = lax.optimization_barrier((own_rows, *hot_grads))
    dx, prob_t = call(
        functools.partial(finish_kernel, base),
        [shape((half, width), BF), shape((TOP, half), F32)],
        "finish",
    )(own_rows, rows_y, rows_x, rows_xy, pos)

    if pad:
        hot_grads = [value[:units] for value in hot_grads]
    return (dx, prob_t.T, grad_cold_gate, grad_cold_up, grad_cold_down, *hot_grads)


def solution(mesh):
    return jax.shard_map(
        local,
        mesh=mesh,
        in_specs=(
            P("dp", None),
            P("dp", None),
            P("dp", None),
            P("dp", None),
            P("dp", None),
            P(),
            P(),
            P("dp", "pair", None),
            P("dp", "pair", None),
            P("dp", "pair", None),
            P(("dp", "pair"), None),
            P(("dp", "pair"), None),
            P(("dp", "pair"), None),
        ),
        out_specs=(
            P(("dp", "pair"), None),
            P(("dp", "pair"), None),
            P("dp", "pair", None),
            P("dp", "pair", None),
            P("dp", "pair", None),
            P(("dp", "pair"), None),
            P(("dp", "pair"), None),
            P(("dp", "pair"), None),
        ),
        check_vma=False,
    )
```

```python
import functools

import jax
import jax.numpy as jnp
from jax import lax
from jax.experimental import pallas as pl
from jax.experimental.pallas import tpu as pltpu
from jax.sharding import PartitionSpec as P

TOP = 2
CAP = 4
HCAP = 48
HALF = HCAP // 2
TAIL = 128
CHUNK_BLOCK = 8
GATHER_BLOCK = 112
COLD_PART = 4 * CAP
MESSAGE = HCAP + COLD_PART
COLD_ROWS = 128
UNIT_BLOCK = 128
BF = jnp.bfloat16
F32 = jnp.float32
VMEM_LIMIT = 56 * 1024 * 1024
VMEM_BASE = 12 * 1024 * 1024

NT = (((1,), (1,)), ((), ()))
TN = (((0,), (0,)), ((), ()))


def dot(a, b, dims=(((1,), (0,)), ((), ()))):
    return lax.dot_general(a, b, dims, preferred_element_type=F32)


def iota(shape, dim):
    return lax.broadcasted_iota(jnp.int32, shape, dim)


def positions(ids, slots, flags_ref, owner_ref, base):
    hot = jnp.zeros_like(ids)
    own = jnp.zeros_like(ids)
    for e in range(flags_ref.shape[0]):
        named = ids == e
        hot = jnp.where(named, flags_ref[e], hot)
        own = jnp.where(named, owner_ref[e], own)
    cold_pos = jnp.where(slots < CAP, own * CAP + slots, -1)
    hot_pos = jnp.where(slots < HCAP, base + slots, -1)
    return jnp.where(hot == 1, hot_pos, cold_pos)


def tail_lanes(first, second=None):
    lane = iota((first.shape[0], TAIL), 1)
    out = jnp.where(lane == 0, first, 0.0)
    if second is not None:
        out = jnp.where(lane == 1, second, out)
    return out


def split_tail(value):
    high = value.astype(BF).astype(F32)
    return tail_lanes(high, value - high)


def each_block(total, size, body):
    if total == size:
        body(0)
    else:

        def step(block, carry):
            body(pl.multiple_of(block * size, size))
            return carry

        lax.fori_loop(0, total // size, step, 0)


def add_to(ref, value, single):
    if single:
        ref[...] = value.astype(ref.dtype)
    else:
        ref[...] += value


def gather_rows(out_ref, start, target, is_grad, pos, prob, tok_ref, grad_ref):
    first = pos[0:1, :] == target
    second = pos[1:2, :] == target
    chosen = jnp.where((first | second) & ~is_grad, 1.0, 0.0)
    weight = jnp.where(first, prob[0:1, :], 0.0) + jnp.where(second, prob[1:2, :], 0.0)
    weight = jnp.where(is_grad, weight, 0.0)
    rows = dot(chosen.astype(BF), tok_ref[...]) + dot(weight.astype(BF), grad_ref[...])
    out_ref[pl.ds(start, target.shape[0]), :] = rows.astype(BF)


def dispatch_kernel(base, *refs):
    tok_ref, grad_ref, prob_ref, ids_ref, slot_ref, flags_ref, owner_ref = refs[:7]
    gate_ref, up_ref, down_ref, pos_ref, weight_ref, *messages, rows_ref = refs[7:]
    pair = lax.axis_index("pair")
    me = lax.axis_index("dp")
    z, x = me // 4, (me // 2) % 2
    pos = positions(ids_ref[...], slot_ref[...], flags_ref, owner_ref, base)
    pos_ref[...] = pos
    joined = [ref[...].astype(F32) for ref in (gate_ref, up_ref, down_ref)]
    weight_ref[...] = jnp.concatenate(joined, axis=0).astype(BF)
    prob = prob_ref[...].astype(F32)

    def block(start):
        row = start + iota((GATHER_BLOCK, tok_ref.shape[0]), 0)
        hot = row < HCAP
        cold_row = row - HCAP
        chip = 2 * (z ^ (cold_row >> 4)) + (x ^ ((cold_row >> 3) & 1))
        hot_target = base + HALF * pair + jnp.where(row >= HALF, row - HALF, row)
        target = jnp.where(hot, hot_target, chip * CAP + (row & 3))
        is_grad = (hot & (row >= HALF)) | (~hot & ((row & 4) != 0))
        gather_rows(rows_ref, start, target, is_grad, pos, prob, tok_ref, grad_ref)

    each_block(rows_ref.shape[0], GATHER_BLOCK, block)
    for message, k in zip(messages, [0, 1] + list(range(2, 2 * len(messages) - 2, 2))):
        message[:COLD_PART, :] = rows_ref[HCAP + k * COLD_PART : HCAP + (k + 1) * COLD_PART, :]
        message[COLD_PART:MESSAGE, :] = rows_ref[:HCAP, :]
        if k > 1:
            message[MESSAGE:, :] = rows_ref[HCAP + (k + 1) * COLD_PART : HCAP + (k + 2) * COLD_PART, :]


def copy_kernel(*refs):
    half = len(refs) // 2
    for in_ref, out_ref in zip(refs[:half], refs[half:]):
        out_ref[...] = in_ref[...]


def relay_kernel(in_ref, out_ref):
    out_ref[:COLD_PART, :] = in_ref[MESSAGE:, :]
    out_ref[COLD_PART:, :] = in_ref[COLD_PART:MESSAGE, :]


def away_kernel(*refs):
    *messages, out_ref = refs
    rows = [ref[:COLD_PART, :].astype(F32)[2 * CAP :] for ref in messages]
    out_ref[...] = jnp.concatenate(rows, axis=0).astype(BF)


def swiglu_back(pre_gate, pre_up, back):
    sig = 1.0 / (1.0 + jnp.exp(-pre_gate))
    act = pre_gate * sig
    hidden = act * pre_up
    gate_grad = back * pre_up * sig * (1.0 + pre_gate * (1.0 - sig))
    return gate_grad, back * act, hidden, hidden * back


def write_rows(out_ref, rows, prob):
    width = rows.shape[1]
    out_ref[:, :width] = rows.astype(out_ref.dtype)
    tail = tail_lanes(prob) if out_ref.dtype == F32 else split_tail(prob).astype(BF)
    out_ref[:, width:] = tail


def read_rows(value):
    value = value.astype(F32)
    width = value.shape[1] - TAIL
    return value[:, :width], value[:, width : width + 1] + value[:, width + 1 : width + 2]


def hot_kernel(chunk_count, units, *refs):
    chunks = refs[:chunk_count]
    weights = refs[chunk_count : chunk_count + 4]
    own_ref, send_ref, *terms = refs[chunk_count + 4 : chunk_count + 10]
    rows_ref, wide_ref, sum_ref = refs[chunk_count + 10 :]
    width = rows_ref.shape[1]
    for k, chunk in enumerate(chunks):
        rows_ref[k * HCAP : (k + 1) * HCAP, :] = chunk[COLD_PART:MESSAGE, :]
    used = 3 * units
    for j, w_ref in enumerate(weights):
        start = j * UNIT_BLOCK
        clear = used // 16 * 16
        if clear < UNIT_BLOCK:
            wide_ref[start + clear : start + UNIT_BLOCK, :] = jnp.zeros((UNIT_BLOCK - clear, width), BF)
        wide_ref[start : start + used, :] = w_ref[...]
    columns = 4 * UNIT_BLOCK
    block_chunks = min(CHUNK_BLOCK, chunk_count)
    block_rows = block_chunks * HCAP
    half_rows = block_rows // 2
    single = block_chunks == chunk_count

    def block(start):
        at = pl.ds(start, block_rows)
        pre = dot(rows_ref[at, :], wide_ref[...], NT).reshape(block_chunks, HCAP, columns)
        pre_x = pre[:, :HALF].reshape(half_rows, columns)
        pre_g = pre[:, HALF:].reshape(half_rows, columns)
        first = (iota(pre_x.shape, 1) & (UNIT_BLOCK - 1)) < units
        gate_grad, up_grad, weighted, prob_term = swiglu_back(
            pre_x,
            pltpu.roll(pre_x, columns - units, 1),
            pltpu.roll(pre_g, columns - 2 * units, 1),
        )
        gate_grad, up_grad, weighted, prob_term = (
            jnp.where(first, value, 0.0) for value in (gate_grad, up_grad, weighted, prob_term)
        )
        grad_prob = jnp.sum(prob_term, axis=1, keepdims=True)
        x_side = gate_grad + pltpu.roll(up_grad, units, 1)
        g_side = pltpu.roll(weighted, 2 * units, 1)
        both = jnp.concatenate(
            [x_side.reshape(block_chunks, HALF, columns), g_side.reshape(block_chunks, HALF, columns)],
            axis=1,
        )
        both = both.reshape(block_rows, columns).astype(BF)
        dx = dot(x_side.astype(BF), wide_ref[...])
        for j in range(4):
            term = dot(both[:, j * UNIT_BLOCK : (j + 1) * UNIT_BLOCK], rows_ref[at, :], TN)
            add_to(terms[j] if single else sum_ref.at[j], term[:used], single)
        return dx, grad_prob

    if single:
        dx, grad_prob = block(0)
        write_rows(own_ref, dx[: half_rows // 2], grad_prob[: half_rows // 2])
        write_rows(send_ref, dx[half_rows // 2 :], grad_prob[half_rows // 2 :])
    else:
        sum_ref[...] = jnp.zeros_like(sum_ref)
        for out_ref, offset in ((own_ref, 0), (send_ref, chunk_count * HCAP // 2)):

            def step(index, carry, out_ref=out_ref, offset=offset):
                dx, grad_prob = block(pl.multiple_of(offset + index * block_rows, 16))
                at = pl.ds(pl.multiple_of(index * half_rows, 16), half_rows)
                write_rows(out_ref.at[at], dx, grad_prob)
                return carry

            lax.fori_loop(0, chunk_count // block_chunks // 2, step, 0)
        for j, out_ref in enumerate(terms):
            out_ref[...] = sum_ref[j].astype(out_ref.dtype)


def cold_kernel(message_count, *refs):
    messages = refs[:message_count]
    mine_x_ref, other_x_ref, gate_ref, up_ref, down_ref = refs[message_count : message_count + 5]
    own_ref, send_ref, *outs = refs[message_count + 5 : message_count + 10]
    data_ref, dx_ref, grad_ref, sum_ref, out_sem = refs[message_count + 10 :]
    total = data_ref.shape[0]
    rows = COLD_ROWS
    single = rows == total
    stores = [
        pltpu.make_async_copy(grad_ref.at[j], ref.at[0], out_sem.at[j]) for j, ref in enumerate(outs)
    ]
    quarter = total // 4
    z_count = message_count // 2
    for flip, away_ref in enumerate((mine_x_ref, other_x_ref)):
        near = [
            ref[:COLD_PART, :].astype(F32)[: 2 * CAP]
            for ref in messages[flip * z_count :][:z_count]
        ]
        start = 2 * flip * quarter
        data_ref[start : start + quarter, :] = jnp.concatenate(near, axis=0).astype(BF)
        data_ref[start + quarter : start + 2 * quarter, :] = away_ref[...]
    if not single:
        sum_ref[...] = jnp.zeros_like(sum_ref)

    def block(start):
        at = pl.ds(start, rows)
        data = data_ref[at, :]
        pre_gate = dot(gate_ref[0], data, NT)
        pre_up = dot(up_ref[0], data, NT)
        back = pltpu.roll(dot(down_ref[0], data, NT), rows - CAP, 1)
        gate_grad, up_grad, weighted, prob_term = swiglu_back(pre_gate, pre_up, back)
        x_lane = (iota(pre_gate.shape, 1) & 4) == 0
        gate_grad = jnp.where(x_lane, gate_grad, 0.0)
        up_grad = jnp.where(x_lane, up_grad, 0.0)
        weighted = pltpu.roll(jnp.where(x_lane, weighted, 0.0), CAP, 1)
        grad_prob = jnp.sum(jnp.where(x_lane, prob_term, 0.0), axis=0, keepdims=True)
        for j, grad in enumerate((gate_grad, up_grad, weighted)):
            term = dot(grad.astype(BF), data)
            if single:
                grad_ref[j] = term.astype(BF)
                stores[j].start()
            else:
                sum_ref[j] += term
        shape = (rows, rows // 2)
        row, col = iota(shape, 0), iota(shape, 1)
        pick = jnp.where(row == (col >> 2) * 8 + (col & 3), 1.0, 0.0).astype(BF)
        dx = dot(dot(gate_grad.astype(BF), pick).astype(BF), gate_ref[0], TN)
        dx = dx + dot(dot(up_grad.astype(BF), pick).astype(BF), up_ref[0], TN)
        shape = (rows // 2, rows)
        row, col = iota(shape, 0), iota(shape, 1)
        pick = jnp.where(col == (row >> 2) * 8 + (row & 3), 1.0, 0.0).astype(BF)
        high = grad_prob.astype(BF).astype(F32)
        row = iota((8, rows), 0)
        both = jnp.where(row == 0, high, jnp.where(row == 1, grad_prob - high, 0.0))
        both = dot(pick, both.astype(BF), NT)
        grad_prob = both[:, 0:1] + both[:, 1:2]
        half_at = pl.ds(start // 2 if single else pl.multiple_of(start // 2, 16), rows // 2)
        write_rows(dx_ref.at[half_at], dx, grad_prob)

    each_block(total, rows, block)
    own_ref[...] = dx_ref[: total // 4, :]
    dx_rows, dx_prob = read_rows(dx_ref[total // 4 :, :])
    write_rows(send_ref, dx_rows, dx_prob)
    if not single:
        for j in range(3):
            grad_ref[j] = sum_ref[j].astype(BF)
            stores[j].start()
    for store in stores:
        store.wait()


def add_kernel(hot_own_ref, hot_got_ref, cold_own_ref, cold_got_ref, *outs):
    def added(own_ref, got_ref):
        rows, prob = read_rows(own_ref[...])
        got_rows, got_prob = read_rows(got_ref[...])
        return jnp.concatenate([rows + got_rows, tail_lanes(prob + got_prob)], axis=1)

    hot = added(hot_own_ref, hot_got_ref)
    cold = added(cold_own_ref, cold_got_ref)
    half = cold.shape[0] // 2
    width = cold.shape[1] - TAIL
    for k, out_ref in enumerate(outs):
        at = k // 2 * 2 * CAP
        near, far = cold[at : at + 2 * CAP], cold[half + at : half + at + 2 * CAP]
        low = (iota(near.shape, 0) & 4) == 0
        if k % 2:
            part = jnp.where(low, pltpu.roll(near, CAP, 0), far)
        else:
            part = jnp.where(low, near, pltpu.roll(far, CAP, 0))
        rows = jnp.concatenate([hot[k * HALF : (k + 1) * HALF], part], axis=0)
        write_rows(out_ref, rows[:, :width], rows[:, width : width + 1])


def combine_kernel(*refs):
    *parts, own_ref, send_y_ref, send_x_ref = refs
    hot, cold = 0.0, []
    for ref in parts:
        rows, prob = read_rows(ref[...])
        both = jnp.concatenate([rows, tail_lanes(prob)], axis=1)
        hot = hot + both[:HALF]
        cold.append(both[HALF:])
    low = (iota(cold[0].shape, 0) & 4) == 0
    mine, other = [], []
    for even, odd in zip(cold[0::2], cold[1::2]):
        mine.append(jnp.where(low, even, pltpu.roll(odd, CAP, 0)))
        other.append(jnp.where(low, pltpu.roll(even, CAP, 0), odd))
    rows = jnp.concatenate([hot] + mine, axis=0)
    away = jnp.concatenate(other, axis=0)
    width = rows.shape[1] - TAIL
    own_ref[...] = rows
    write_rows(send_y_ref, rows[:, :width], rows[:, width : width + 1])
    write_rows(send_x_ref, away[:, :width], away[:, width : width + 1])


def finish_kernel(
    base, own_ref, y_ref, x_ref, xy_ref, pos_ref, weight_ref, dx_ref, prob_ref
):
    pair = lax.axis_index("pair")
    me = lax.axis_index("dp")
    z, x = me // 4, (me // 2) % 2
    half = dx_ref.shape[0]
    pos = jnp.where(pair == 0, pos_ref[:, :half], pos_ref[:, half:])

    def cold_target(row, side):
        return (2 * (z ^ (row >> 2)) + side) * CAP + (row & 3)

    def with_hot(side):
        row = iota((own_ref.shape[0], half), 0)
        return jnp.where(row < HALF, base + HALF * side + row, cold_target(row - HALF, x))

    away = cold_target(iota((x_ref.shape[0], half), 0), 1 - x)
    total = 0.0
    grad_prob = [0.0] * TOP
    for ref, target in (
        (own_ref, with_hot(pair)),
        (y_ref, with_hot(1 - pair)),
        (x_ref, away),
        (xy_ref, away),
    ):
        routes = [pos[k : k + 1, :] == target for k in range(TOP)]
        onehot = jnp.where(routes[0] | routes[1], 1.0, 0.0).astype(BF)
        rows, prob = read_rows(ref[...])
        high = rows.astype(BF)
        total = total + dot(onehot, high, TN)
        if ref.dtype == F32:
            total = total + dot(onehot, (rows - high.astype(F32)).astype(BF), TN)
        for k in range(TOP):
            terms = jnp.sum(jnp.where(routes[k], prob, 0.0), axis=0, keepdims=True)
            grad_prob[k] = grad_prob[k] + terms
    dx_ref[...] = total.astype(BF)
    weight = weight_ref[...].astype(F32)
    weight = jnp.where(pair == 0, weight[:, :half], weight[:, half:])
    for k in range(TOP):
        prob_ref[k : k + 1, :] = grad_prob[k] / weight[k : k + 1, :]


def sum_kernel(own_ref, a_ref, b_ref, c_ref, gate_ref, up_ref, down_ref):
    total = own_ref[...] + a_ref[...].astype(F32) + b_ref[...].astype(F32) + c_ref[...].astype(F32)
    units = gate_ref.shape[0]
    for index, out_ref in enumerate((gate_ref, up_ref, down_ref)):
        out_ref[...] = total[index * units : (index + 1) * units].astype(BF)


def call(kernel, outs, name, scratch=(), smem=(), out_hbm=(), limit=0):
    def run(*args):
        moved = sum(a.size * a.dtype.itemsize for a in args)
        moved += sum(o.size * o.dtype.itemsize for o in outs)
        return pl.pallas_call(
            kernel,
            out_shape=outs,
            in_specs=[
                pl.BlockSpec(memory_space=pltpu.SMEM if i in smem else pltpu.VMEM)
                for i in range(len(args))
            ],
            out_specs=[
                pl.BlockSpec(memory_space=pltpu.HBM if i in out_hbm else pltpu.VMEM)
                for i in range(len(outs))
            ],
            scratch_shapes=[pltpu.VMEM(*s) if isinstance(s, tuple) else s for s in scratch],
            compiler_params=pltpu.CompilerParams(
                vmem_limit_bytes=limit or min(VMEM_LIMIT, VMEM_BASE + 3 * moved // 2)
            ),
            cost_estimate=pl.CostEstimate(flops=1024, bytes_accessed=1024, transcendentals=0),
            name=name,
        )(*args)

    return run


def local(
    tokens,
    grad_out,
    gate_probs,
    expert_ids,
    route_slots,
    hot_flags,
    owner_slot,
    cold_gate,
    cold_up,
    cold_down,
    hot_gate,
    hot_up,
    hot_down,
):
    count = lax.axis_size("dp")
    z_count = count // 4
    chunk_count = 2 * z_count
    token_count, width = tokens.shape
    lanes = width + TAIL
    units = hot_gate.shape[0]
    base = (count // 2) * CAP
    shape = jax.ShapeDtypeStruct
    half = token_count // 2
    pad = -units % 8

    def swap(value, mask):
        flip_dp, flip_pair = 2 * (mask & 1), mask >> 1
        perm = [
            (2 * i + p, 2 * (i ^ flip_dp) + (p ^ flip_pair)) for i in range(count) for p in range(2)
        ]
        return lax.ppermute(value, ("dp", "pair"), perm)

    def along_z(value, k):
        perm = [(i, 4 * ((i // 4) ^ k) + i % 4) for i in range(count)]
        return lax.ppermute(value, "dp", perm)

    def all_along_z(values):
        order = sorted(range(1, z_count), key=lambda k: (k == 1, k))
        got = {k: along_z(values[k], k) for k in order}
        return [values[0]] + [got[k] for k in range(1, z_count)]

    def other_core(value):
        return lax.ppermute(value, "dp", [(i, i ^ 1) for i in range(count)])

    hot_weights = [jnp.pad(w, ((0, pad), (0, 0))) if pad else w for w in (hot_gate, hot_up, hot_down)]
    units_padded = units + pad
    used = 3 * units_padded
    cold_rows = z_count * COLD_PART
    message = shape((MESSAGE, width), BF)
    long_message = shape((MESSAGE + COLD_PART, width), BF)
    pos, hot_own, *messages = call(
        functools.partial(dispatch_kernel, base),
        [shape((TOP, token_count), jnp.int32), shape((used, width), BF)]
        + [message, message]
        + [long_message] * (z_count // 2 - 1),
        "dispatch",
        scratch=[((HCAP + cold_rows, width), BF)],
        smem=(5, 6),
        limit=VMEM_LIMIT,
    )(
        tokens,
        grad_out,
        gate_probs.T,
        expert_ids.T,
        route_slots.T,
        hot_flags,
        owner_slot,
        *hot_weights,
    )

    chunks = [messages[0], along_z(messages[1], 1)]
    for index in range(2, len(messages)):
        direct = along_z(messages[index], 2 * index - 2)
        (onward,) = call(relay_kernel, [message], "relay_rows")(direct)
        chunks += [direct, along_z(onward, 1)]
    first_out, hot_out, _ = lax.optimization_barrier((messages[0], hot_own, chunks[1]))
    first_out, hot_out = call(
        copy_kernel, [message, shape(hot_own.shape, BF)], "own_rows"
    )(first_out, hot_out)
    chunks[0] = first_out
    weights = [hot_out] + [swap(hot_own, mask) for mask in (1, 2, 3)]
    (away,) = call(away_kernel, [shape((cold_rows // 2, width), BF)], "cold_away")(*chunks)
    chunks = chunks + [other_core(chunk) for chunk in chunks]
    cold_mine = swap(away, 1)
    cold_other = other_core(cold_mine)

    cold_units = cold_gate.shape[1]
    cold_shape = shape(cold_gate.shape, BF)
    all_rows = chunk_count * HCAP
    half_rows = chunk_count * HALF // 2
    term = shape((used, width), BF)
    hot_dx, hot_dx_out, own_term, *sent_terms = call(
        functools.partial(hot_kernel, chunk_count, units_padded),
        [
            shape((half_rows, lanes), F32),
            shape((half_rows, lanes), BF),
            shape(term.shape, F32),
            term,
            term,
            term,
        ],
        "hot",
        scratch=[
            ((all_rows, width), BF),
            ((4 * UNIT_BLOCK, width), BF),
            ((4, used, width) if chunk_count > CHUNK_BLOCK else (8, 128), F32),
        ],
    )(*chunks, *weights)

    cold_mine, hot_dx = lax.optimization_barrier((cold_mine, hot_dx))
    cold_own, cold_out, grad_cold_gate, grad_cold_up, grad_cold_down = call(
        functools.partial(cold_kernel, chunk_count),
        [shape((cold_rows // 2, lanes), F32), shape((cold_rows // 2, lanes), BF)] + [cold_shape] * 3,
        "cold",
        scratch=[
            ((2 * cold_rows, width), BF),
            ((cold_rows, lanes), F32),
            ((3, cold_units, width), BF),
            ((3, cold_units, width) if 2 * cold_rows > COLD_ROWS else (8, 128), F32),
            pltpu.SemaphoreType.DMA((3,)),
        ],
        out_hbm=(2, 3, 4),
    )(*chunks, cold_mine, cold_other, cold_gate, cold_up, cold_down)

    hot_got, cold_got = other_core(hot_dx_out), other_core(cold_out)
    part = (HALF + 2 * CAP, lanes)
    parts = call(
        add_kernel, [shape(part, F32)] + [shape(part, BF)] * (z_count - 1), "add_cores"
    )(hot_dx, hot_got, cold_own, cold_got)
    term_x, _ = lax.optimization_barrier((sent_terms[0], cold_mine))
    got_x, got_y = swap(term_x, 1), swap(sent_terms[1], 2)
    *parts, last_term = lax.optimization_barrier((*parts, sent_terms[2]))
    *parts, got_x, got_y = lax.optimization_barrier((*parts, got_x, got_y))
    parts = all_along_z(parts)
    got_terms = [got_x, got_y, swap(last_term, 3)]

    cold_back = z_count * CAP
    own_rows, send_y, send_x = call(
        combine_kernel,
        [
            shape((HALF + cold_back, lanes), F32),
            shape((HALF + cold_back, lanes), BF),
            shape((cold_back, lanes), BF),
        ],
        "combine",
    )(*parts)
    rows_y, rows_x, rows_xy = swap(send_y, 2), swap(send_x, 1), swap(send_x, 3)
    out_shape = shape((units_padded, width), BF)
    hot_grads = call(sum_kernel, [out_shape] * 3, "hot_sum")(
        own_term, *got_terms
    )
    own_rows, *hot_grads = lax.optimization_barrier((own_rows, *hot_grads))
    dx, prob_t = call(
        functools.partial(finish_kernel, base),
        [shape((half, width), BF), shape((TOP, half), F32)],
        "finish",
    )(own_rows, rows_y, rows_x, rows_xy, pos, gate_probs.T)

    if pad:
        hot_grads = [value[:units] for value in hot_grads]
    return (dx, prob_t.T, grad_cold_gate, grad_cold_up, grad_cold_down, *hot_grads)


def solution(mesh):
    return jax.shard_map(
        local,
        mesh=mesh,
        in_specs=(
            P("dp", None),
            P("dp", None),
            P("dp", None),
            P("dp", None),
            P("dp", None),
            P(),
            P(),
            P("dp", "pair", None),
            P("dp", "pair", None),
            P("dp", "pair", None),
            P(("dp", "pair"), None),
            P(("dp", "pair"), None),
            P(("dp", "pair"), None),
        ),
        out_specs=(
            P(("dp", "pair"), None),
            P(("dp", "pair"), None),
            P("dp", "pair", None),
            P("dp", "pair", None),
            P("dp", "pair", None),
            P(("dp", "pair"), None),
            P(("dp", "pair"), None),
            P(("dp", "pair"), None),
        ),
        check_vma=False,
    )
```

```python
import functools

import jax
import jax.numpy as jnp
from jax import lax
from jax.experimental import pallas as pl
from jax.experimental.pallas import tpu as pltpu
from jax.sharding import PartitionSpec as P

TOP = 2
CAP = 4
HCAP = 48
HALF = HCAP // 2
TAIL = 128
CHUNK_BLOCK = 8
GATHER_BLOCK = 112
COLD_PART = 4 * CAP
MESSAGE = HCAP + COLD_PART
COLD_ROWS = 128
UNIT_BLOCK = 128
BF = jnp.bfloat16
F32 = jnp.float32
VMEM_LIMIT = 56 * 1024 * 1024
VMEM_BASE = 12 * 1024 * 1024

NT = (((1,), (1,)), ((), ()))
TN = (((0,), (0,)), ((), ()))


def dot(a, b, dims=(((1,), (0,)), ((), ()))):
    return lax.dot_general(a, b, dims, preferred_element_type=F32)


def iota(shape, dim):
    return lax.broadcasted_iota(jnp.int32, shape, dim)


def positions(ids, slots, flags_ref, owner_ref, base):
    hot = jnp.zeros_like(ids)
    own = jnp.zeros_like(ids)
    for e in range(flags_ref.shape[0]):
        named = ids == e
        hot = jnp.where(named, flags_ref[e], hot)
        own = jnp.where(named, owner_ref[e], own)
    cold_pos = jnp.where(slots < CAP, own * CAP + slots, -1)
    hot_pos = jnp.where(slots < HCAP, base + slots, -1)
    return jnp.where(hot == 1, hot_pos, cold_pos)


def tail_lanes(first, second=None):
    lane = iota((first.shape[0], TAIL), 1)
    out = jnp.where(lane == 0, first, 0.0)
    if second is not None:
        out = jnp.where(lane == 1, second, out)
    return out


def split_tail(value):
    high = value.astype(BF).astype(F32)
    return tail_lanes(high, value - high)


def each_block(total, size, body):
    if total == size:
        body(0)
    else:

        def step(block, carry):
            body(pl.multiple_of(block * size, size))
            return carry

        lax.fori_loop(0, total // size, step, 0)


def add_to(ref, value, single):
    if single:
        ref[...] = value.astype(ref.dtype)
    else:
        ref[...] += value


def gather_rows(out_ref, start, target, is_grad, pos, prob, tok_ref, grad_ref):
    width = tok_ref.shape[1]
    at = pl.ds(start, target.shape[0])
    first = pos[0:1, :] == target
    second = pos[1:2, :] == target
    chosen = jnp.where(first | second, 1.0, 0.0)
    rows = dot(jnp.where(is_grad, 0.0, chosen).astype(BF), tok_ref[...]) + dot(
        jnp.where(is_grad, chosen, 0.0).astype(BF), grad_ref[...]
    )
    out_ref[at, :width] = rows.astype(BF)
    weight = jnp.where(first, prob[0:1, :], 0.0) + jnp.where(second, prob[1:2, :], 0.0)
    weight = jnp.sum(jnp.where(is_grad, 0.0, weight), axis=1, keepdims=True)
    out_ref[at, width:] = tail_lanes(weight).astype(BF)


def dispatch_kernel(base, *refs):
    tok_ref, grad_ref, prob_ref, ids_ref, slot_ref, flags_ref, owner_ref = refs[:7]
    gate_ref, up_ref, down_ref, pos_ref, weight_ref, *messages, rows_ref = refs[7:]
    pair = lax.axis_index("pair")
    me = lax.axis_index("dp")
    z, x = me // 4, (me // 2) % 2
    pos = positions(ids_ref[...], slot_ref[...], flags_ref, owner_ref, base)
    pos_ref[...] = pos
    joined = [ref[...].astype(F32) for ref in (gate_ref, up_ref, down_ref)]
    weight_ref[...] = jnp.concatenate(joined, axis=0).astype(BF)
    prob = prob_ref[...].astype(F32)

    def block(start):
        row = start + iota((GATHER_BLOCK, tok_ref.shape[0]), 0)
        hot = row < HCAP
        cold_row = row - HCAP
        chip = 2 * (z ^ (cold_row >> 4)) + (x ^ ((cold_row >> 3) & 1))
        hot_target = base + HALF * pair + jnp.where(row >= HALF, row - HALF, row)
        target = jnp.where(hot, hot_target, chip * CAP + (row & 3))
        is_grad = (hot & (row >= HALF)) | (~hot & ((row & 4) != 0))
        gather_rows(rows_ref, start, target, is_grad, pos, prob, tok_ref, grad_ref)

    each_block(rows_ref.shape[0], GATHER_BLOCK, block)
    for message, k in zip(messages, [0, 1] + list(range(2, 2 * len(messages) - 2, 2))):
        message[:COLD_PART, :] = rows_ref[HCAP + k * COLD_PART : HCAP + (k + 1) * COLD_PART, :]
        message[COLD_PART:MESSAGE, :] = rows_ref[:HCAP, :]
        if k > 1:
            message[MESSAGE:, :] = rows_ref[HCAP + (k + 1) * COLD_PART : HCAP + (k + 2) * COLD_PART, :]


def copy_kernel(*refs):
    half = len(refs) // 2
    for in_ref, out_ref in zip(refs[:half], refs[half:]):
        out_ref[...] = in_ref[...]


def relay_kernel(in_ref, out_ref):
    out_ref[:COLD_PART, :] = in_ref[MESSAGE:, :]
    out_ref[COLD_PART:, :] = in_ref[COLD_PART:MESSAGE, :]


def away_kernel(*refs):
    *messages, out_ref = refs
    rows = [ref[:COLD_PART, :].astype(F32)[2 * CAP :] for ref in messages]
    out_ref[...] = jnp.concatenate(rows, axis=0).astype(BF)


def swiglu_back(pre_gate, pre_up, back, prob):
    sig = 1.0 / (1.0 + jnp.exp(-pre_gate))
    act = pre_gate * sig
    hidden = act * pre_up
    scaled = prob * back
    gate_grad = scaled * pre_up * sig * (1.0 + pre_gate * (1.0 - sig))
    return gate_grad, scaled * act, prob * hidden, hidden * back


def write_rows(out_ref, rows, prob):
    width = rows.shape[1]
    out_ref[:, :width] = rows.astype(out_ref.dtype)
    tail = tail_lanes(prob) if out_ref.dtype == F32 else split_tail(prob).astype(BF)
    out_ref[:, width:] = tail


def read_rows(value):
    value = value.astype(F32)
    width = value.shape[1] - TAIL
    return value[:, :width], value[:, width : width + 1] + value[:, width + 1 : width + 2]


def hot_kernel(chunk_count, units, *refs):
    chunks = refs[:chunk_count]
    weights = refs[chunk_count : chunk_count + 4]
    own_ref, send_ref, *terms = refs[chunk_count + 4 : chunk_count + 10]
    rows_ref, tail_ref, wide_ref, sum_ref = refs[chunk_count + 10 :]
    width = rows_ref.shape[1]
    for k, chunk in enumerate(chunks):
        rows_ref[k * HCAP : (k + 1) * HCAP, :] = chunk[COLD_PART:MESSAGE, :width]
        tail_ref[k * HCAP : (k + 1) * HCAP, :] = chunk[COLD_PART:MESSAGE, width:]
    used = 3 * units
    for j, w_ref in enumerate(weights):
        start = j * UNIT_BLOCK
        clear = used // 16 * 16
        if clear < UNIT_BLOCK:
            wide_ref[start + clear : start + UNIT_BLOCK, :] = jnp.zeros((UNIT_BLOCK - clear, width), BF)
        wide_ref[start : start + used, :] = w_ref[...]
    columns = 4 * UNIT_BLOCK
    block_chunks = min(CHUNK_BLOCK, chunk_count)
    block_rows = block_chunks * HCAP
    half_rows = block_rows // 2
    single = block_chunks == chunk_count

    def block(start):
        at = pl.ds(start, block_rows)
        prob = tail_ref[at, :].astype(F32).reshape(block_chunks, HCAP, TAIL)[:, :HALF, 0:1]
        prob = prob.reshape(half_rows, 1)
        pre = dot(rows_ref[at, :], wide_ref[...], NT).reshape(block_chunks, HCAP, columns)
        pre_x = pre[:, :HALF].reshape(half_rows, columns)
        pre_g = pre[:, HALF:].reshape(half_rows, columns)
        first = (iota(pre_x.shape, 1) & (UNIT_BLOCK - 1)) < units
        gate_grad, up_grad, weighted, prob_term = swiglu_back(
            pre_x,
            pltpu.roll(pre_x, columns - units, 1),
            pltpu.roll(pre_g, columns - 2 * units, 1),
            prob,
        )
        gate_grad, up_grad, weighted, prob_term = (
            jnp.where(first, value, 0.0) for value in (gate_grad, up_grad, weighted, prob_term)
        )
        grad_prob = jnp.sum(prob_term, axis=1, keepdims=True)
        x_side = gate_grad + pltpu.roll(up_grad, units, 1)
        g_side = pltpu.roll(weighted, 2 * units, 1)
        both = jnp.concatenate(
            [x_side.reshape(block_chunks, HALF, columns), g_side.reshape(block_chunks, HALF, columns)],
            axis=1,
        )
        both = both.reshape(block_rows, columns).astype(BF)
        dx = dot(x_side.astype(BF), wide_ref[...])
        for j in range(4):
            term = dot(both[:, j * UNIT_BLOCK : (j + 1) * UNIT_BLOCK], rows_ref[at, :], TN)
            add_to(terms[j] if single else sum_ref.at[j], term[:used], single)
        return dx, grad_prob

    if single:
        dx, grad_prob = block(0)
        write_rows(own_ref, dx[: half_rows // 2], grad_prob[: half_rows // 2])
        write_rows(send_ref, dx[half_rows // 2 :], grad_prob[half_rows // 2 :])
    else:
        sum_ref[...] = jnp.zeros_like(sum_ref)
        for out_ref, offset in ((own_ref, 0), (send_ref, chunk_count * HCAP // 2)):

            def step(index, carry, out_ref=out_ref, offset=offset):
                dx, grad_prob = block(pl.multiple_of(offset + index * block_rows, 16))
                at = pl.ds(pl.multiple_of(index * half_rows, 16), half_rows)
                write_rows(out_ref.at[at], dx, grad_prob)
                return carry

            lax.fori_loop(0, chunk_count // block_chunks // 2, step, 0)
        for j, out_ref in enumerate(terms):
            out_ref[...] = sum_ref[j].astype(out_ref.dtype)


def cold_kernel(message_count, *refs):
    messages = refs[:message_count]
    mine_x_ref, other_x_ref, gate_ref, up_ref, down_ref = refs[message_count : message_count + 5]
    own_ref, send_ref, *outs = refs[message_count + 5 : message_count + 10]
    data_ref, dx_ref, grad_ref, sum_ref, out_sem = refs[message_count + 10 :]
    total, width = data_ref.shape[0], gate_ref.shape[2]
    rows = COLD_ROWS
    single = rows == total
    stores = [
        pltpu.make_async_copy(grad_ref.at[j], ref.at[0], out_sem.at[j]) for j, ref in enumerate(outs)
    ]
    quarter = total // 4
    z_count = message_count // 2
    for flip, away_ref in enumerate((mine_x_ref, other_x_ref)):
        near = [
            ref[:COLD_PART, :].astype(F32)[: 2 * CAP]
            for ref in messages[flip * z_count :][:z_count]
        ]
        start = 2 * flip * quarter
        data_ref[start : start + quarter, :] = jnp.concatenate(near, axis=0).astype(BF)
        data_ref[start + quarter : start + 2 * quarter, :] = away_ref[...]
    if not single:
        sum_ref[...] = jnp.zeros_like(sum_ref)

    def block(start):
        at = pl.ds(start, rows)
        data = data_ref[at, :width]
        first = jnp.where((iota((8, TAIL), 0) == 0) & (iota((8, TAIL), 1) == 0), 1.0, 0.0)
        prob = dot(first.astype(BF), data_ref[at, width:], NT)[0:1, :]
        pre_gate = dot(gate_ref[0], data, NT)
        pre_up = dot(up_ref[0], data, NT)
        back = pltpu.roll(dot(down_ref[0], data, NT), rows - CAP, 1)
        gate_grad, up_grad, weighted, prob_term = swiglu_back(pre_gate, pre_up, back, prob)
        x_lane = (iota(pre_gate.shape, 1) & 4) == 0
        gate_grad = jnp.where(x_lane, gate_grad, 0.0)
        up_grad = jnp.where(x_lane, up_grad, 0.0)
        weighted = pltpu.roll(jnp.where(x_lane, weighted, 0.0), CAP, 1)
        grad_prob = jnp.sum(jnp.where(x_lane, prob_term, 0.0), axis=0, keepdims=True)
        for j, grad in enumerate((gate_grad, up_grad, weighted)):
            term = dot(grad.astype(BF), data)
            if single:
                grad_ref[j] = term.astype(BF)
                stores[j].start()
            else:
                sum_ref[j] += term
        shape = (rows, rows // 2)
        row, col = iota(shape, 0), iota(shape, 1)
        pick = jnp.where(row == (col >> 2) * 8 + (col & 3), 1.0, 0.0).astype(BF)
        dx = dot(dot(gate_grad.astype(BF), pick).astype(BF), gate_ref[0], TN)
        dx = dx + dot(dot(up_grad.astype(BF), pick).astype(BF), up_ref[0], TN)
        shape = (rows // 2, rows)
        row, col = iota(shape, 0), iota(shape, 1)
        pick = jnp.where(col == (row >> 2) * 8 + (row & 3), 1.0, 0.0).astype(BF)
        high = grad_prob.astype(BF).astype(F32)
        row = iota((8, rows), 0)
        both = jnp.where(row == 0, high, jnp.where(row == 1, grad_prob - high, 0.0))
        both = dot(pick, both.astype(BF), NT)
        grad_prob = both[:, 0:1] + both[:, 1:2]
        half_at = pl.ds(start // 2 if single else pl.multiple_of(start // 2, 16), rows // 2)
        write_rows(dx_ref.at[half_at], dx, grad_prob)

    each_block(total, rows, block)
    own_ref[...] = dx_ref[: total // 4, :]
    dx_rows, dx_prob = read_rows(dx_ref[total // 4 :, :])
    write_rows(send_ref, dx_rows, dx_prob)
    if not single:
        for j in range(3):
            grad_ref[j] = sum_ref[j].astype(BF)
            stores[j].start()
    for store in stores:
        store.wait()


def add_kernel(hot_own_ref, hot_got_ref, cold_own_ref, cold_got_ref, *outs):
    def added(own_ref, got_ref):
        rows, prob = read_rows(own_ref[...])
        got_rows, got_prob = read_rows(got_ref[...])
        return jnp.concatenate([rows + got_rows, tail_lanes(prob + got_prob)], axis=1)

    hot = added(hot_own_ref, hot_got_ref)
    cold = added(cold_own_ref, cold_got_ref)
    half = cold.shape[0] // 2
    width = cold.shape[1] - TAIL
    for k, out_ref in enumerate(outs):
        at = k // 2 * 2 * CAP
        near, far = cold[at : at + 2 * CAP], cold[half + at : half + at + 2 * CAP]
        low = (iota(near.shape, 0) & 4) == 0
        if k % 2:
            part = jnp.where(low, pltpu.roll(near, CAP, 0), far)
        else:
            part = jnp.where(low, near, pltpu.roll(far, CAP, 0))
        rows = jnp.concatenate([hot[k * HALF : (k + 1) * HALF], part], axis=0)
        write_rows(out_ref, rows[:, :width], rows[:, width : width + 1])


def combine_kernel(*refs):
    *parts, own_ref, send_y_ref, send_x_ref = refs
    hot, cold = 0.0, []
    for ref in parts:
        rows, prob = read_rows(ref[...])
        both = jnp.concatenate([rows, tail_lanes(prob)], axis=1)
        hot = hot + both[:HALF]
        cold.append(both[HALF:])
    low = (iota(cold[0].shape, 0) & 4) == 0
    mine, other = [], []
    for even, odd in zip(cold[0::2], cold[1::2]):
        mine.append(jnp.where(low, even, pltpu.roll(odd, CAP, 0)))
        other.append(jnp.where(low, pltpu.roll(even, CAP, 0), odd))
    rows = jnp.concatenate([hot] + mine, axis=0)
    away = jnp.concatenate(other, axis=0)
    width = rows.shape[1] - TAIL
    own_ref[...] = rows
    write_rows(send_y_ref, rows[:, :width], rows[:, width : width + 1])
    write_rows(send_x_ref, away[:, :width], away[:, width : width + 1])


def finish_kernel(base, own_ref, y_ref, x_ref, xy_ref, pos_ref, dx_ref, prob_ref):
    pair = lax.axis_index("pair")
    me = lax.axis_index("dp")
    z, x = me // 4, (me // 2) % 2
    half = dx_ref.shape[0]
    pos = jnp.where(pair == 0, pos_ref[:, :half], pos_ref[:, half:])

    def cold_target(row, side):
        return (2 * (z ^ (row >> 2)) + side) * CAP + (row & 3)

    def with_hot(side):
        row = iota((own_ref.shape[0], half), 0)
        return jnp.where(row < HALF, base + HALF * side + row, cold_target(row - HALF, x))

    away = cold_target(iota((x_ref.shape[0], half), 0), 1 - x)
    total = 0.0
    grad_prob = [0.0] * TOP
    for ref, target in (
        (own_ref, with_hot(pair)),
        (y_ref, with_hot(1 - pair)),
        (x_ref, away),
        (xy_ref, away),
    ):
        routes = [pos[k : k + 1, :] == target for k in range(TOP)]
        onehot = jnp.where(routes[0] | routes[1], 1.0, 0.0).astype(BF)
        rows, prob = read_rows(ref[...])
        high = rows.astype(BF)
        total = total + dot(onehot, high, TN)
        if ref.dtype == F32:
            total = total + dot(onehot, (rows - high.astype(F32)).astype(BF), TN)
        for k in range(TOP):
            terms = jnp.sum(jnp.where(routes[k], prob, 0.0), axis=0, keepdims=True)
            grad_prob[k] = grad_prob[k] + terms
    dx_ref[...] = total.astype(BF)
    for k in range(TOP):
        prob_ref[k : k + 1, :] = grad_prob[k]


def sum_kernel(own_ref, a_ref, b_ref, c_ref, gate_ref, up_ref, down_ref):
    total = own_ref[...] + a_ref[...].astype(F32) + b_ref[...].astype(F32) + c_ref[...].astype(F32)
    units = gate_ref.shape[0]
    for index, out_ref in enumerate((gate_ref, up_ref, down_ref)):
        out_ref[...] = total[index * units : (index + 1) * units].astype(BF)


def call(kernel, outs, name, scratch=(), smem=(), out_hbm=(), limit=0):
    def run(*args):
        moved = sum(a.size * a.dtype.itemsize for a in args)
        moved += sum(o.size * o.dtype.itemsize for o in outs)
        return pl.pallas_call(
            kernel,
            out_shape=outs,
            in_specs=[
                pl.BlockSpec(memory_space=pltpu.SMEM if i in smem else pltpu.VMEM)
                for i in range(len(args))
            ],
            out_specs=[
                pl.BlockSpec(memory_space=pltpu.HBM if i in out_hbm else pltpu.VMEM)
                for i in range(len(outs))
            ],
            scratch_shapes=[pltpu.VMEM(*s) if isinstance(s, tuple) else s for s in scratch],
            compiler_params=pltpu.CompilerParams(
                vmem_limit_bytes=limit or min(VMEM_LIMIT, VMEM_BASE + 3 * moved // 2)
            ),
            cost_estimate=pl.CostEstimate(flops=1024, bytes_accessed=1024, transcendentals=0),
            name=name,
        )(*args)

    return run


def local(
    tokens,
    grad_out,
    gate_probs,
    expert_ids,
    route_slots,
    hot_flags,
    owner_slot,
    cold_gate,
    cold_up,
    cold_down,
    hot_gate,
    hot_up,
    hot_down,
):
    count = lax.axis_size("dp")
    z_count = count // 4
    chunk_count = 2 * z_count
    token_count, width = tokens.shape
    lanes = width + TAIL
    units = hot_gate.shape[0]
    base = (count // 2) * CAP
    shape = jax.ShapeDtypeStruct
    half = token_count // 2
    pad = -units % 8

    def swap(value, mask):
        flip_dp, flip_pair = 2 * (mask & 1), mask >> 1
        perm = [
            (2 * i + p, 2 * (i ^ flip_dp) + (p ^ flip_pair)) for i in range(count) for p in range(2)
        ]
        return lax.ppermute(value, ("dp", "pair"), perm)

    def along_z(value, k):
        perm = [(i, 4 * ((i // 4) ^ k) + i % 4) for i in range(count)]
        return lax.ppermute(value, "dp", perm)

    def all_along_z(values):
        order = sorted(range(1, z_count), key=lambda k: (k == 1, k))
        got = {k: along_z(values[k], k) for k in order}
        return [values[0]] + [got[k] for k in range(1, z_count)]

    def other_core(value):
        return lax.ppermute(value, "dp", [(i, i ^ 1) for i in range(count)])

    hot_weights = [jnp.pad(w, ((0, pad), (0, 0))) if pad else w for w in (hot_gate, hot_up, hot_down)]
    units_padded = units + pad
    used = 3 * units_padded
    cold_rows = z_count * COLD_PART
    message = shape((MESSAGE, lanes), BF)
    long_message = shape((MESSAGE + COLD_PART, lanes), BF)
    pos, hot_own, *messages = call(
        functools.partial(dispatch_kernel, base),
        [shape((TOP, token_count), jnp.int32), shape((used, width), BF)]
        + [message, message]
        + [long_message] * (z_count // 2 - 1),
        "dispatch",
        scratch=[((HCAP + cold_rows, lanes), BF)],
        smem=(5, 6),
        limit=VMEM_LIMIT,
    )(
        tokens,
        grad_out,
        gate_probs.T,
        expert_ids.T,
        route_slots.T,
        hot_flags,
        owner_slot,
        *hot_weights,
    )

    chunks = [messages[0], along_z(messages[1], 1)]
    for index in range(2, len(messages)):
        direct = along_z(messages[index], 2 * index - 2)
        (onward,) = call(relay_kernel, [message], "relay_rows")(direct)
        chunks += [direct, along_z(onward, 1)]
    first_out, hot_out, _ = lax.optimization_barrier((messages[0], hot_own, chunks[1]))
    first_out, hot_out = call(
        copy_kernel, [message, shape(hot_own.shape, BF)], "own_rows"
    )(first_out, hot_out)
    chunks[0] = first_out
    weights = [hot_out] + [swap(hot_own, mask) for mask in (1, 2, 3)]
    (away,) = call(away_kernel, [shape((cold_rows // 2, lanes), BF)], "cold_away")(*chunks)
    chunks = chunks + [other_core(chunk) for chunk in chunks]
    cold_mine = swap(away, 1)
    cold_other = other_core(cold_mine)

    cold_units = cold_gate.shape[1]
    cold_shape = shape(cold_gate.shape, BF)
    all_rows = chunk_count * HCAP
    half_rows = chunk_count * HALF // 2
    term = shape((used, width), BF)
    hot_dx, hot_dx_out, own_term, *sent_terms = call(
        functools.partial(hot_kernel, chunk_count, units_padded),
        [
            shape((half_rows, lanes), F32),
            shape((half_rows, lanes), BF),
            shape(term.shape, F32),
            term,
            term,
            term,
        ],
        "hot",
        scratch=[
            ((all_rows, width), BF),
            ((all_rows, TAIL), BF),
            ((4 * UNIT_BLOCK, width), BF),
            ((4, used, width) if chunk_count > CHUNK_BLOCK else (8, 128), F32),
        ],
    )(*chunks, *weights)

    cold_mine, hot_dx = lax.optimization_barrier((cold_mine, hot_dx))
    cold_own, cold_out, grad_cold_gate, grad_cold_up, grad_cold_down = call(
        functools.partial(cold_kernel, chunk_count),
        [shape((cold_rows // 2, lanes), F32), shape((cold_rows // 2, lanes), BF)] + [cold_shape] * 3,
        "cold",
        scratch=[
            ((2 * cold_rows, lanes), BF),
            ((cold_rows, lanes), F32),
            ((3, cold_units, width), BF),
            ((3, cold_units, width) if 2 * cold_rows > COLD_ROWS else (8, 128), F32),
            pltpu.SemaphoreType.DMA((3,)),
        ],
        out_hbm=(2, 3, 4),
    )(*chunks, cold_mine, cold_other, cold_gate, cold_up, cold_down)

    hot_got, cold_got = other_core(hot_dx_out), other_core(cold_out)
    part = (HALF + 2 * CAP, lanes)
    parts = call(
        add_kernel, [shape(part, F32)] + [shape(part, BF)] * (z_count - 1), "add_cores"
    )(hot_dx, hot_got, cold_own, cold_got)
    term_x, _ = lax.optimization_barrier((sent_terms[0], cold_mine))
    got_x, got_y = swap(term_x, 1), swap(sent_terms[1], 2)
    *parts, last_term = lax.optimization_barrier((*parts, sent_terms[2]))
    *parts, got_x, got_y = lax.optimization_barrier((*parts, got_x, got_y))
    parts = all_along_z(parts)
    got_terms = [got_x, got_y, swap(last_term, 3)]

    cold_back = z_count * CAP
    own_rows, send_y, send_x = call(
        combine_kernel,
        [
            shape((HALF + cold_back, lanes), F32),
            shape((HALF + cold_back, lanes), BF),
            shape((cold_back, lanes), BF),
        ],
        "combine",
    )(*parts)
    rows_y, rows_x, rows_xy = swap(send_y, 2), swap(send_x, 1), swap(send_x, 3)
    out_shape = shape((units_padded, width), BF)
    hot_grads = call(sum_kernel, [out_shape] * 3, "hot_sum")(
        own_term, *got_terms
    )
    own_rows, *hot_grads = lax.optimization_barrier((own_rows, *hot_grads))
    dx, prob_t = call(
        functools.partial(finish_kernel, base),
        [shape((half, width), BF), shape((TOP, half), F32)],
        "finish",
    )(own_rows, rows_y, rows_x, rows_xy, pos)

    if pad:
        hot_grads = [value[:units] for value in hot_grads]
    return (dx, prob_t.T, grad_cold_gate, grad_cold_up, grad_cold_down, *hot_grads)


def solution(mesh):
    return jax.shard_map(
        local,
        mesh=mesh,
        in_specs=(
            P("dp", None),
            P("dp", None),
            P("dp", None),
            P("dp", None),
            P("dp", None),
            P(),
            P(),
            P("dp", "pair", None),
            P("dp", "pair", None),
            P("dp", "pair", None),
            P(("dp", "pair"), None),
            P(("dp", "pair"), None),
            P(("dp", "pair"), None),
        ),
        out_specs=(
            P(("dp", "pair"), None),
            P(("dp", "pair"), None),
            P("dp", "pair", None),
            P("dp", "pair", None),
            P("dp", "pair", None),
            P(("dp", "pair"), None),
            P(("dp", "pair"), None),
            P(("dp", "pair"), None),
        ),
        check_vma=False,
    )
```

```python
import functools

import jax
import jax.numpy as jnp
from jax import lax
from jax.experimental import pallas as pl
from jax.experimental.pallas import tpu as pltpu
from jax.sharding import PartitionSpec as P

TOP = 2
CAP = 4
HCAP = 48
HALF = HCAP // 2
TAIL = 128
CHUNK_BLOCK = 8
GATHER_BLOCK = 112
COLD_PART = 4 * CAP
MESSAGE = HCAP + COLD_PART
COLD_ROWS = 128
UNIT_BLOCK = 128
BF = jnp.bfloat16
F32 = jnp.float32
VMEM_LIMIT = 56 * 1024 * 1024
VMEM_BASE = 12 * 1024 * 1024

NT = (((1,), (1,)), ((), ()))
TN = (((0,), (0,)), ((), ()))


def dot(a, b, dims=(((1,), (0,)), ((), ()))):
    return lax.dot_general(a, b, dims, preferred_element_type=F32)


def iota(shape, dim):
    return lax.broadcasted_iota(jnp.int32, shape, dim)


def positions(ids, slots, flags_ref, owner_ref, base):
    hot = jnp.zeros_like(ids)
    own = jnp.zeros_like(ids)
    for e in range(flags_ref.shape[0]):
        named = ids == e
        hot = jnp.where(named, flags_ref[e], hot)
        own = jnp.where(named, owner_ref[e], own)
    cold_pos = jnp.where(slots < CAP, own * CAP + slots, -1)
    hot_pos = jnp.where(slots < HCAP, base + slots, -1)
    return jnp.where(hot == 1, hot_pos, cold_pos)


def tail_lanes(first, second=None):
    lane = iota((first.shape[0], TAIL), 1)
    out = jnp.where(lane == 0, first, 0.0)
    if second is not None:
        out = jnp.where(lane == 1, second, out)
    return out


def split_tail(value):
    high = value.astype(BF).astype(F32)
    return tail_lanes(high, value - high)


def each_block(total, size, body):
    if total == size:
        body(0)
    else:

        def step(block, carry):
            body(pl.multiple_of(block * size, size))
            return carry

        lax.fori_loop(0, total // size, step, 0)


def add_to(ref, value, single):
    if single:
        ref[...] = value.astype(ref.dtype)
    else:
        ref[...] += value


def gather_rows(out_ref, start, target, is_grad, pos, prob, tok_ref, grad_ref):
    width = tok_ref.shape[1]
    at = pl.ds(start, target.shape[0])
    first = pos[0:1, :] == target
    second = pos[1:2, :] == target
    chosen = jnp.where(first | second, 1.0, 0.0)
    rows = dot(jnp.where(is_grad, 0.0, chosen).astype(BF), tok_ref[...]) + dot(
        jnp.where(is_grad, chosen, 0.0).astype(BF), grad_ref[...]
    )
    out_ref[at, :width] = rows.astype(BF)
    weight = jnp.where(first, prob[0:1, :], 0.0) + jnp.where(second, prob[1:2, :], 0.0)
    weight = jnp.sum(jnp.where(is_grad, 0.0, weight), axis=1, keepdims=True)
    out_ref[at, width:] = tail_lanes(weight).astype(BF)


def dispatch_kernel(base, *refs):
    tok_ref, grad_ref, prob_ref, ids_ref, slot_ref, flags_ref, owner_ref = refs[:7]
    gate_ref, up_ref, down_ref, pos_ref, weight_ref, *messages, rows_ref = refs[7:]
    pair = lax.axis_index("pair")
    me = lax.axis_index("dp")
    z, x = me // 4, (me // 2) % 2
    pos = positions(ids_ref[...], slot_ref[...], flags_ref, owner_ref, base)
    pos_ref[...] = pos
    joined = [ref[...].astype(F32) for ref in (gate_ref, up_ref, down_ref)]
    weight_ref[...] = jnp.concatenate(joined, axis=0).astype(BF)
    prob = prob_ref[...].astype(F32)

    def block(start):
        row = start + iota((GATHER_BLOCK, tok_ref.shape[0]), 0)
        hot = row < HCAP
        cold_row = row - HCAP
        chip = 2 * (z ^ (cold_row >> 4)) + (x ^ ((cold_row >> 3) & 1))
        hot_target = base + HALF * pair + jnp.where(row >= HALF, row - HALF, row)
        target = jnp.where(hot, hot_target, chip * CAP + (row & 3))
        is_grad = (hot & (row >= HALF)) | (~hot & ((row & 4) != 0))
        gather_rows(rows_ref, start, target, is_grad, pos, prob, tok_ref, grad_ref)

    each_block(rows_ref.shape[0], GATHER_BLOCK, block)
    for message, k in zip(messages, [0, 1] + list(range(2, 2 * len(messages) - 2, 2))):
        message[:COLD_PART, :] = rows_ref[HCAP + k * COLD_PART : HCAP + (k + 1) * COLD_PART, :]
        message[COLD_PART:MESSAGE, :] = rows_ref[:HCAP, :]
        if k > 1:
            message[MESSAGE:, :] = rows_ref[HCAP + (k + 1) * COLD_PART : HCAP + (k + 2) * COLD_PART, :]


def copy_kernel(*refs):
    half = len(refs) // 2
    for in_ref, out_ref in zip(refs[:half], refs[half:]):
        out_ref[...] = in_ref[...]


def relay_kernel(in_ref, out_ref):
    out_ref[:COLD_PART, :] = in_ref[MESSAGE:, :]
    out_ref[COLD_PART:, :] = in_ref[COLD_PART:MESSAGE, :]


def away_kernel(*refs):
    *messages, out_ref = refs
    rows = [ref[:COLD_PART, :].astype(F32)[2 * CAP :] for ref in messages]
    out_ref[...] = jnp.concatenate(rows, axis=0).astype(BF)


def swiglu_back(pre_gate, pre_up, back, prob):
    sig = 1.0 / (1.0 + jnp.exp(-pre_gate))
    act = pre_gate * sig
    hidden = act * pre_up
    scaled = prob * back
    gate_grad = scaled * pre_up * sig * (1.0 + pre_gate * (1.0 - sig))
    return gate_grad, scaled * act, prob * hidden, hidden * back


def write_rows(out_ref, rows, prob):
    width = rows.shape[1]
    out_ref[:, :width] = rows.astype(out_ref.dtype)
    tail = tail_lanes(prob) if out_ref.dtype == F32 else split_tail(prob).astype(BF)
    out_ref[:, width:] = tail


def read_rows(value):
    value = value.astype(F32)
    width = value.shape[1] - TAIL
    return value[:, :width], value[:, width : width + 1] + value[:, width + 1 : width + 2]


def hot_kernel(chunk_count, units, *refs):
    chunks = refs[:chunk_count]
    weights = refs[chunk_count : chunk_count + 4]
    own_ref, send_ref, *terms = refs[chunk_count + 4 : chunk_count + 10]
    rows_ref, tail_ref, wide_ref, sum_ref = refs[chunk_count + 10 :]
    width = rows_ref.shape[1]
    for k, chunk in enumerate(chunks):
        rows_ref[k * HCAP : (k + 1) * HCAP, :] = chunk[COLD_PART:MESSAGE, :width]
        tail_ref[k * HCAP : (k + 1) * HCAP, :] = chunk[COLD_PART:MESSAGE, width:]
    used = 3 * units
    for j, w_ref in enumerate(weights):
        start = j * UNIT_BLOCK
        clear = used // 16 * 16
        if clear < UNIT_BLOCK:
            wide_ref[start + clear : start + UNIT_BLOCK, :] = jnp.zeros((UNIT_BLOCK - clear, width), BF)
        wide_ref[start : start + used, :] = w_ref[...]
    columns = 4 * UNIT_BLOCK
    block_chunks = min(CHUNK_BLOCK, chunk_count)
    block_rows = block_chunks * HCAP
    half_rows = block_rows // 2
    single = block_chunks == chunk_count

    def block(start):
        at = pl.ds(start, block_rows)
        prob = tail_ref[at, :].astype(F32).reshape(block_chunks, HCAP, TAIL)[:, :HALF, 0:1]
        prob = prob.reshape(half_rows, 1)
        pre = dot(rows_ref[at, :], wide_ref[...], NT).reshape(block_chunks, HCAP, columns)
        pre_x = pre[:, :HALF].reshape(half_rows, columns)
        pre_g = pre[:, HALF:].reshape(half_rows, columns)
        first = (iota(pre_x.shape, 1) & (UNIT_BLOCK - 1)) < units
        gate_grad, up_grad, weighted, prob_term = swiglu_back(
            pre_x,
            pltpu.roll(pre_x, columns - units, 1),
            pltpu.roll(pre_g, columns - 2 * units, 1),
            prob,
        )
        gate_grad, up_grad, weighted, prob_term = (
            jnp.where(first, value, 0.0) for value in (gate_grad, up_grad, weighted, prob_term)
        )
        grad_prob = jnp.sum(prob_term, axis=1, keepdims=True)
        x_side = gate_grad + pltpu.roll(up_grad, units, 1)
        g_side = pltpu.roll(weighted, 2 * units, 1)
        both = jnp.concatenate(
            [x_side.reshape(block_chunks, HALF, columns), g_side.reshape(block_chunks, HALF, columns)],
            axis=1,
        )
        both = both.reshape(block_rows, columns).astype(BF)
        dx = dot(x_side.astype(BF), wide_ref[...])
        for j in range(4):
            term = dot(both[:, j * UNIT_BLOCK : (j + 1) * UNIT_BLOCK], rows_ref[at, :], TN)
            add_to(terms[j] if single else sum_ref.at[j], term[:used], single)
        return dx, grad_prob

    if single:
        dx, grad_prob = block(0)
        write_rows(own_ref, dx[: half_rows // 2], grad_prob[: half_rows // 2])
        write_rows(send_ref, dx[half_rows // 2 :], grad_prob[half_rows // 2 :])
    else:
        sum_ref[...] = jnp.zeros_like(sum_ref)
        for out_ref, offset in ((own_ref, 0), (send_ref, chunk_count * HCAP // 2)):

            def step(index, carry, out_ref=out_ref, offset=offset):
                dx, grad_prob = block(pl.multiple_of(offset + index * block_rows, 16))
                at = pl.ds(pl.multiple_of(index * half_rows, 16), half_rows)
                write_rows(out_ref.at[at], dx, grad_prob)
                return carry

            lax.fori_loop(0, chunk_count // block_chunks // 2, step, 0)
        for j, out_ref in enumerate(terms):
            out_ref[...] = sum_ref[j].astype(out_ref.dtype)


def cold_kernel(message_count, *refs):
    messages = refs[:message_count]
    mine_x_ref, other_x_ref, gate_ref, up_ref, down_ref = refs[message_count : message_count + 5]
    own_ref, send_ref, *outs = refs[message_count + 5 : message_count + 10]
    data_ref, dx_ref, grad_ref, sum_ref, out_sem = refs[message_count + 10 :]
    total, width = data_ref.shape[0], gate_ref.shape[2]
    rows = COLD_ROWS
    single = rows == total
    stores = [
        pltpu.make_async_copy(grad_ref.at[j], ref.at[0], out_sem.at[j]) for j, ref in enumerate(outs)
    ]
    quarter = total // 4
    z_count = message_count // 2
    for flip, away_ref in enumerate((mine_x_ref, other_x_ref)):
        near = [
            ref[:COLD_PART, :].astype(F32)[: 2 * CAP]
            for ref in messages[flip * z_count :][:z_count]
        ]
        start = 2 * flip * quarter
        data_ref[start : start + quarter, :] = jnp.concatenate(near, axis=0).astype(BF)
        data_ref[start + quarter : start + 2 * quarter, :] = away_ref[...]
    if not single:
        sum_ref[...] = jnp.zeros_like(sum_ref)

    def block(start):
        at = pl.ds(start, rows)
        data = data_ref[at, :width]
        first = jnp.where((iota((8, TAIL), 0) == 0) & (iota((8, TAIL), 1) == 0), 1.0, 0.0)
        prob = dot(first.astype(BF), data_ref[at, width:], NT)[0:1, :]
        pre_gate = dot(gate_ref[0], data, NT)
        pre_up = dot(up_ref[0], data, NT)
        back = pltpu.roll(dot(down_ref[0], data, NT), rows - CAP, 1)
        gate_grad, up_grad, weighted, prob_term = swiglu_back(pre_gate, pre_up, back, prob)
        x_lane = (iota(pre_gate.shape, 1) & 4) == 0
        gate_grad = jnp.where(x_lane, gate_grad, 0.0)
        up_grad = jnp.where(x_lane, up_grad, 0.0)
        weighted = pltpu.roll(jnp.where(x_lane, weighted, 0.0), CAP, 1)
        grad_prob = jnp.sum(jnp.where(x_lane, prob_term, 0.0), axis=0, keepdims=True)
        for j, grad in enumerate((gate_grad, up_grad, weighted)):
            term = dot(grad.astype(BF), data)
            if single:
                grad_ref[j] = term.astype(BF)
                stores[j].start()
            else:
                sum_ref[j] += term
        shape = (rows, rows // 2)
        row, col = iota(shape, 0), iota(shape, 1)
        pick = jnp.where(row == (col >> 2) * 8 + (col & 3), 1.0, 0.0).astype(BF)
        dx = dot(dot(gate_grad.astype(BF), pick).astype(BF), gate_ref[0], TN)
        dx = dx + dot(dot(up_grad.astype(BF), pick).astype(BF), up_ref[0], TN)
        shape = (rows // 2, rows)
        row, col = iota(shape, 0), iota(shape, 1)
        pick = jnp.where(col == (row >> 2) * 8 + (row & 3), 1.0, 0.0).astype(BF)
        high = grad_prob.astype(BF).astype(F32)
        row = iota((8, rows), 0)
        both = jnp.where(row == 0, high, jnp.where(row == 1, grad_prob - high, 0.0))
        both = dot(pick, both.astype(BF), NT)
        grad_prob = both[:, 0:1] + both[:, 1:2]
        half_at = pl.ds(start // 2 if single else pl.multiple_of(start // 2, 16), rows // 2)
        write_rows(dx_ref.at[half_at], dx, grad_prob)

    each_block(total, rows, block)
    own_ref[...] = dx_ref[: total // 4, :]
    dx_rows, dx_prob = read_rows(dx_ref[total // 4 :, :])
    write_rows(send_ref, dx_rows, dx_prob)
    if not single:
        for j in range(3):
            grad_ref[j] = sum_ref[j].astype(BF)
            stores[j].start()
    for store in stores:
        store.wait()


def add_kernel(hot_own_ref, hot_got_ref, cold_own_ref, cold_got_ref, *outs):
    def added(own_ref, got_ref):
        rows, prob = read_rows(own_ref[...])
        got_rows, got_prob = read_rows(got_ref[...])
        return jnp.concatenate([rows + got_rows, tail_lanes(prob + got_prob)], axis=1)

    hot = added(hot_own_ref, hot_got_ref)
    cold = added(cold_own_ref, cold_got_ref)
    half = cold.shape[0] // 2
    width = cold.shape[1] - TAIL
    for k, out_ref in enumerate(outs):
        at = k // 2 * 2 * CAP
        near, far = cold[at : at + 2 * CAP], cold[half + at : half + at + 2 * CAP]
        low = (iota(near.shape, 0) & 4) == 0
        if k % 2:
            part = jnp.where(low, pltpu.roll(near, CAP, 0), far)
        else:
            part = jnp.where(low, near, pltpu.roll(far, CAP, 0))
        rows = jnp.concatenate([hot[k * HALF : (k + 1) * HALF], part], axis=0)
        write_rows(out_ref, rows[:, :width], rows[:, width : width + 1])


def combine_kernel(*refs):
    *parts, own_ref, send_y_ref, send_x_ref = refs
    hot, cold = 0.0, []
    for ref in parts:
        rows, prob = read_rows(ref[...])
        both = jnp.concatenate([rows, tail_lanes(prob)], axis=1)
        hot = hot + both[:HALF]
        cold.append(both[HALF:])
    low = (iota(cold[0].shape, 0) & 4) == 0
    mine, other = [], []
    for even, odd in zip(cold[0::2], cold[1::2]):
        mine.append(jnp.where(low, even, pltpu.roll(odd, CAP, 0)))
        other.append(jnp.where(low, pltpu.roll(even, CAP, 0), odd))
    rows = jnp.concatenate([hot] + mine, axis=0)
    away = jnp.concatenate(other, axis=0)
    width = rows.shape[1] - TAIL
    own_ref[...] = rows
    write_rows(send_y_ref, rows[:, :width], rows[:, width : width + 1])
    write_rows(send_x_ref, away[:, :width], away[:, width : width + 1])


def finish_kernel(base, own_ref, y_ref, x_ref, xy_ref, pos_ref, dx_ref, prob_ref):
    pair = lax.axis_index("pair")
    me = lax.axis_index("dp")
    z, x = me // 4, (me // 2) % 2
    half = dx_ref.shape[0]
    pos = jnp.where(pair == 0, pos_ref[:, :half], pos_ref[:, half:])

    def cold_target(row, side):
        return (2 * (z ^ (row >> 2)) + side) * CAP + (row & 3)

    def with_hot(side):
        row = iota((own_ref.shape[0], half), 0)
        return jnp.where(row < HALF, base + HALF * side + row, cold_target(row - HALF, x))

    away = cold_target(iota((x_ref.shape[0], half), 0), 1 - x)
    total = 0.0
    grad_prob = [0.0] * TOP
    for ref, target in (
        (own_ref, with_hot(pair)),
        (y_ref, with_hot(1 - pair)),
        (x_ref, away),
        (xy_ref, away),
    ):
        routes = [pos[k : k + 1, :] == target for k in range(TOP)]
        onehot = jnp.where(routes[0] | routes[1], 1.0, 0.0).astype(BF)
        rows, prob = read_rows(ref[...])
        high = rows.astype(BF)
        total = total + dot(onehot, high, TN)
        if ref.dtype == F32:
            total = total + dot(onehot, (rows - high.astype(F32)).astype(BF), TN)
        for k in range(TOP):
            terms = jnp.sum(jnp.where(routes[k], prob, 0.0), axis=0, keepdims=True)
            grad_prob[k] = grad_prob[k] + terms
    dx_ref[...] = total.astype(BF)
    for k in range(TOP):
        prob_ref[k : k + 1, :] = grad_prob[k]


def sum_kernel(own_ref, a_ref, b_ref, c_ref, gate_ref, up_ref, down_ref):
    total = own_ref[...] + a_ref[...].astype(F32) + b_ref[...].astype(F32) + c_ref[...].astype(F32)
    units = gate_ref.shape[0]
    for index, out_ref in enumerate((gate_ref, up_ref, down_ref)):
        out_ref[...] = total[index * units : (index + 1) * units].astype(BF)


def call(kernel, outs, name, scratch=(), smem=(), out_hbm=(), limit=0):
    def run(*args):
        moved = sum(a.size * a.dtype.itemsize for a in args)
        moved += sum(o.size * o.dtype.itemsize for o in outs)
        return pl.pallas_call(
            kernel,
            out_shape=outs,
            in_specs=[
                pl.BlockSpec(memory_space=pltpu.SMEM if i in smem else pltpu.VMEM)
                for i in range(len(args))
            ],
            out_specs=[
                pl.BlockSpec(memory_space=pltpu.HBM if i in out_hbm else pltpu.VMEM)
                for i in range(len(outs))
            ],
            scratch_shapes=[pltpu.VMEM(*s) if isinstance(s, tuple) else s for s in scratch],
            compiler_params=pltpu.CompilerParams(
                vmem_limit_bytes=limit or min(VMEM_LIMIT, VMEM_BASE + 3 * moved // 2)
            ),
            cost_estimate=pl.CostEstimate(flops=1024, bytes_accessed=1024, transcendentals=0),
            name=name,
        )(*args)

    return run


def local(
    tokens,
    grad_out,
    gate_probs,
    expert_ids,
    route_slots,
    hot_flags,
    owner_slot,
    cold_gate,
    cold_up,
    cold_down,
    hot_gate,
    hot_up,
    hot_down,
):
    count = lax.axis_size("dp")
    z_count = count // 4
    chunk_count = 2 * z_count
    token_count, width = tokens.shape
    lanes = width + TAIL
    units = hot_gate.shape[0]
    base = (count // 2) * CAP
    shape = jax.ShapeDtypeStruct
    half = token_count // 2
    pad = -units % 8

    def swap(value, mask):
        flip_dp, flip_pair = 2 * (mask & 1), mask >> 1
        perm = [
            (2 * i + p, 2 * (i ^ flip_dp) + (p ^ flip_pair)) for i in range(count) for p in range(2)
        ]
        return lax.ppermute(value, ("dp", "pair"), perm)

    def along_z(value, k):
        perm = [(i, 4 * ((i // 4) ^ k) + i % 4) for i in range(count)]
        return lax.ppermute(value, "dp", perm)

    def all_along_z(values):
        order = sorted(range(1, z_count), key=lambda k: (k == 1, k))
        got = {k: along_z(values[k], k) for k in order}
        return [values[0]] + [got[k] for k in range(1, z_count)]

    def other_core(value):
        return lax.ppermute(value, "dp", [(i, i ^ 1) for i in range(count)])

    hot_weights = [jnp.pad(w, ((0, pad), (0, 0))) if pad else w for w in (hot_gate, hot_up, hot_down)]
    units_padded = units + pad
    used = 3 * units_padded
    cold_rows = z_count * COLD_PART
    message = shape((MESSAGE, lanes), BF)
    long_message = shape((MESSAGE + COLD_PART, lanes), BF)
    pos, hot_own, *messages = call(
        functools.partial(dispatch_kernel, base),
        [shape((TOP, token_count), jnp.int32), shape((used, width), BF)]
        + [message, message]
        + [long_message] * (z_count // 2 - 1),
        "dispatch",
        scratch=[((HCAP + cold_rows, lanes), BF)],
        smem=(5, 6),
        limit=VMEM_LIMIT,
    )(
        tokens,
        grad_out,
        gate_probs.T,
        expert_ids.T,
        route_slots.T,
        hot_flags,
        owner_slot,
        *hot_weights,
    )

    chunks = [messages[0], along_z(messages[1], 1)]
    for index in range(2, len(messages)):
        direct = along_z(messages[index], 2 * index - 2)
        (onward,) = call(relay_kernel, [message], "relay_rows")(direct)
        chunks += [direct, along_z(onward, 1)]
    first_out, hot_out, _ = lax.optimization_barrier((messages[0], hot_own, chunks[1]))
    first_out, hot_out = call(
        copy_kernel, [message, shape(hot_own.shape, BF)], "own_rows"
    )(first_out, hot_out)
    chunks[0] = first_out
    weights = [hot_out] + [swap(hot_own, mask) for mask in (1, 2, 3)]
    (away,) = call(away_kernel, [shape((cold_rows // 2, lanes), BF)], "cold_away")(*chunks)
    chunks = chunks + [other_core(chunk) for chunk in chunks]
    cold_mine = swap(away, 1)
    cold_other = other_core(cold_mine)

    cold_units = cold_gate.shape[1]
    cold_shape = shape(cold_gate.shape, BF)
    all_rows = chunk_count * HCAP
    half_rows = chunk_count * HALF // 2
    term = shape((used, width), BF)
    hot_dx, hot_dx_out, own_term, *sent_terms = call(
        functools.partial(hot_kernel, chunk_count, units_padded),
        [
            shape((half_rows, lanes), F32),
            shape((half_rows, lanes), BF),
            shape(term.shape, F32),
            term,
            term,
            term,
        ],
        "hot",
        scratch=[
            ((all_rows, width), BF),
            ((all_rows, TAIL), BF),
            ((4 * UNIT_BLOCK, width), BF),
            ((4, used, width) if chunk_count > CHUNK_BLOCK else (8, 128), F32),
        ],
    )(*chunks, *weights)

    cold_mine, hot_dx = lax.optimization_barrier((cold_mine, hot_dx))
    cold_own, cold_out, grad_cold_gate, grad_cold_up, grad_cold_down = call(
        functools.partial(cold_kernel, chunk_count),
        [shape((cold_rows // 2, lanes), F32), shape((cold_rows // 2, lanes), BF)] + [cold_shape] * 3,
        "cold",
        scratch=[
            ((2 * cold_rows, lanes), BF),
            ((cold_rows, lanes), F32),
            ((3, cold_units, width), BF),
            ((3, cold_units, width) if 2 * cold_rows > COLD_ROWS else (8, 128), F32),
            pltpu.SemaphoreType.DMA((3,)),
        ],
        out_hbm=(2, 3, 4),
    )(*chunks, cold_mine, cold_other, cold_gate, cold_up, cold_down)

    hot_got, cold_got = other_core(hot_dx_out), other_core(cold_out)
    part = (HALF + 2 * CAP, lanes)
    parts = call(
        add_kernel, [shape(part, F32)] + [shape(part, BF)] * (z_count - 1), "add_cores"
    )(hot_dx, hot_got, cold_own, cold_got)
    term_x, _ = lax.optimization_barrier((sent_terms[0], cold_mine))
    got_x, got_y = swap(term_x, 1), swap(sent_terms[1], 2)
    last_term, cold_out = lax.optimization_barrier((sent_terms[2], cold_out))
    *parts, got_x, got_y = lax.optimization_barrier((*parts, got_x, got_y))
    parts = all_along_z(parts)
    got_terms = [got_x, got_y, swap(last_term, 3)]

    cold_back = z_count * CAP
    own_rows, send_y, send_x = call(
        combine_kernel,
        [
            shape((HALF + cold_back, lanes), F32),
            shape((HALF + cold_back, lanes), BF),
            shape((cold_back, lanes), BF),
        ],
        "combine",
    )(*parts)
    rows_y, rows_x, rows_xy = swap(send_y, 2), swap(send_x, 1), swap(send_x, 3)
    out_shape = shape((units_padded, width), BF)
    hot_grads = call(sum_kernel, [out_shape] * 3, "hot_sum")(
        own_term, *got_terms
    )
    own_rows, *hot_grads = lax.optimization_barrier((own_rows, *hot_grads))
    dx, prob_t = call(
        functools.partial(finish_kernel, base),
        [shape((half, width), BF), shape((TOP, half), F32)],
        "finish",
    )(own_rows, rows_y, rows_x, rows_xy, pos)

    if pad:
        hot_grads = [value[:units] for value in hot_grads]
    return (dx, prob_t.T, grad_cold_gate, grad_cold_up, grad_cold_down, *hot_grads)


def solution(mesh):
    return jax.shard_map(
        local,
        mesh=mesh,
        in_specs=(
            P("dp", None),
            P("dp", None),
            P("dp", None),
            P("dp", None),
            P("dp", None),
            P(),
            P(),
            P("dp", "pair", None),
            P("dp", "pair", None),
            P("dp", "pair", None),
            P(("dp", "pair"), None),
            P(("dp", "pair"), None),
            P(("dp", "pair"), None),
        ),
        out_specs=(
            P(("dp", "pair"), None),
            P(("dp", "pair"), None),
            P("dp", "pair", None),
            P("dp", "pair", None),
            P("dp", "pair", None),
            P(("dp", "pair"), None),
            P(("dp", "pair"), None),
            P(("dp", "pair"), None),
        ),
        check_vma=False,
    )
```

```python
import functools

import jax
import jax.numpy as jnp
from jax import lax
from jax.experimental import pallas as pl
from jax.experimental.pallas import tpu as pltpu
from jax.sharding import PartitionSpec as P

TOP = 2
CAP = 4
HCAP = 48
HALF = HCAP // 2
TAIL = 128
CHUNK_BLOCK = 8
GATHER_BLOCK = 112
COLD_PART = 4 * CAP
MESSAGE = HCAP + COLD_PART
COLD_ROWS = 128
UNIT_BLOCK = 128
BF = jnp.bfloat16
F32 = jnp.float32
VMEM_LIMIT = 56 * 1024 * 1024
VMEM_BASE = 12 * 1024 * 1024

NT = (((1,), (1,)), ((), ()))
TN = (((0,), (0,)), ((), ()))


def dot(a, b, dims=(((1,), (0,)), ((), ()))):
    return lax.dot_general(a, b, dims, preferred_element_type=F32)


def iota(shape, dim):
    return lax.broadcasted_iota(jnp.int32, shape, dim)


def positions(ids, slots, flags_ref, owner_ref, base):
    hot = jnp.zeros_like(ids)
    own = jnp.zeros_like(ids)
    for e in range(flags_ref.shape[0]):
        named = ids == e
        hot = jnp.where(named, flags_ref[e], hot)
        own = jnp.where(named, owner_ref[e], own)
    cold_pos = jnp.where(slots < CAP, own * CAP + slots, -1)
    hot_pos = jnp.where(slots < HCAP, base + slots, -1)
    return jnp.where(hot == 1, hot_pos, cold_pos)


def tail_lanes(first, second=None):
    lane = iota((first.shape[0], TAIL), 1)
    out = jnp.where(lane == 0, first, 0.0)
    if second is not None:
        out = jnp.where(lane == 1, second, out)
    return out


def split_tail(value):
    high = value.astype(BF).astype(F32)
    return tail_lanes(high, value - high)


def each_block(total, size, body):
    if total == size:
        body(0)
    else:

        def step(block, carry):
            body(pl.multiple_of(block * size, size))
            return carry

        lax.fori_loop(0, total // size, step, 0)


def add_to(ref, value, single):
    if single:
        ref[...] = value.astype(ref.dtype)
    else:
        ref[...] += value


def gather_rows(out_ref, start, target, is_grad, pos, prob, tok_ref, grad_ref):
    width = tok_ref.shape[1]
    at = pl.ds(start, target.shape[0])
    first = pos[0:1, :] == target
    second = pos[1:2, :] == target
    chosen = jnp.where(first | second, 1.0, 0.0)
    rows = dot(jnp.where(is_grad, 0.0, chosen).astype(BF), tok_ref[...]) + dot(
        jnp.where(is_grad, chosen, 0.0).astype(BF), grad_ref[...]
    )
    out_ref[at, :width] = rows.astype(BF)
    weight = jnp.where(first, prob[0:1, :], 0.0) + jnp.where(second, prob[1:2, :], 0.0)
    weight = jnp.sum(jnp.where(is_grad, 0.0, weight), axis=1, keepdims=True)
    out_ref[at, width:] = tail_lanes(weight).astype(BF)


def dispatch_kernel(base, *refs):
    tok_ref, grad_ref, prob_ref, ids_ref, slot_ref, flags_ref, owner_ref = refs[:7]
    gate_ref, up_ref, down_ref, pos_ref, weight_ref, *messages, rows_ref = refs[7:]
    pair = lax.axis_index("pair")
    me = lax.axis_index("dp")
    z, x = me // 4, (me // 2) % 2
    pos = positions(ids_ref[...], slot_ref[...], flags_ref, owner_ref, base)
    pos_ref[...] = pos
    joined = [ref[...].astype(F32) for ref in (gate_ref, up_ref, down_ref)]
    weight_ref[...] = jnp.concatenate(joined, axis=0).astype(BF)
    prob = prob_ref[...].astype(F32)

    def block(start):
        row = start + iota((GATHER_BLOCK, tok_ref.shape[0]), 0)
        hot = row < HCAP
        cold_row = row - HCAP
        chip = 2 * (z ^ (cold_row >> 4)) + (x ^ ((cold_row >> 3) & 1))
        hot_target = base + HALF * pair + jnp.where(row >= HALF, row - HALF, row)
        target = jnp.where(hot, hot_target, chip * CAP + (row & 3))
        is_grad = (hot & (row >= HALF)) | (~hot & ((row & 4) != 0))
        gather_rows(rows_ref, start, target, is_grad, pos, prob, tok_ref, grad_ref)

    each_block(rows_ref.shape[0], GATHER_BLOCK, block)
    for message, k in zip(messages, [0, 1] + list(range(2, 2 * len(messages) - 2, 2))):
        message[:COLD_PART, :] = rows_ref[HCAP + k * COLD_PART : HCAP + (k + 1) * COLD_PART, :]
        message[COLD_PART:MESSAGE, :] = rows_ref[:HCAP, :]
        if k > 1:
            message[MESSAGE:, :] = rows_ref[HCAP + (k + 1) * COLD_PART : HCAP + (k + 2) * COLD_PART, :]


def copy_kernel(*refs):
    half = len(refs) // 2
    for in_ref, out_ref in zip(refs[:half], refs[half:]):
        out_ref[...] = in_ref[...]


def relay_kernel(in_ref, out_ref):
    out_ref[:COLD_PART, :] = in_ref[MESSAGE:, :]
    out_ref[COLD_PART:, :] = in_ref[COLD_PART:MESSAGE, :]


def away_kernel(*refs):
    *messages, out_ref = refs
    rows = [ref[:COLD_PART, :].astype(F32)[2 * CAP :] for ref in messages]
    out_ref[...] = jnp.concatenate(rows, axis=0).astype(BF)


def swiglu_back(pre_gate, pre_up, back, prob):
    sig = 1.0 / (1.0 + jnp.exp(-pre_gate))
    act = pre_gate * sig
    hidden = act * pre_up
    scaled = prob * back
    gate_grad = scaled * pre_up * sig * (1.0 + pre_gate * (1.0 - sig))
    return gate_grad, scaled * act, prob * hidden, hidden * back


def write_rows(out_ref, rows, prob):
    width = rows.shape[1]
    out_ref[:, :width] = rows.astype(out_ref.dtype)
    tail = tail_lanes(prob) if out_ref.dtype == F32 else split_tail(prob).astype(BF)
    out_ref[:, width:] = tail


def read_rows(value):
    value = value.astype(F32)
    width = value.shape[1] - TAIL
    return value[:, :width], value[:, width : width + 1] + value[:, width + 1 : width + 2]


def hot_kernel(chunk_count, units, *refs):
    chunks = refs[:chunk_count]
    weights = refs[chunk_count : chunk_count + 4]
    own_ref, send_ref, *terms = refs[chunk_count + 4 : chunk_count + 10]
    rows_ref, tail_ref, wide_ref, sum_ref = refs[chunk_count + 10 :]
    width = rows_ref.shape[1]
    for k, chunk in enumerate(chunks):
        rows_ref[k * HCAP : (k + 1) * HCAP, :] = chunk[COLD_PART:MESSAGE, :width]
        tail_ref[k * HCAP : (k + 1) * HCAP, :] = chunk[COLD_PART:MESSAGE, width:]
    used = 3 * units
    for j, w_ref in enumerate(weights):
        start = j * UNIT_BLOCK
        clear = used // 16 * 16
        if clear < UNIT_BLOCK:
            wide_ref[start + clear : start + UNIT_BLOCK, :] = jnp.zeros((UNIT_BLOCK - clear, width), BF)
        wide_ref[start : start + used, :] = w_ref[...]
    columns = 4 * UNIT_BLOCK
    block_chunks = min(CHUNK_BLOCK, chunk_count)
    block_rows = block_chunks * HCAP
    half_rows = block_rows // 2
    single = block_chunks == chunk_count

    def block(start):
        at = pl.ds(start, block_rows)
        prob = tail_ref[at, :].astype(F32).reshape(block_chunks, HCAP, TAIL)[:, :HALF, 0:1]
        prob = prob.reshape(half_rows, 1)
        pre = dot(rows_ref[at, :], wide_ref[...], NT).reshape(block_chunks, HCAP, columns)
        pre_x = pre[:, :HALF].reshape(half_rows, columns)
        pre_g = pre[:, HALF:].reshape(half_rows, columns)
        first = (iota(pre_x.shape, 1) & (UNIT_BLOCK - 1)) < units
        gate_grad, up_grad, weighted, prob_term = swiglu_back(
            pre_x,
            pltpu.roll(pre_x, columns - units, 1),
            pltpu.roll(pre_g, columns - 2 * units, 1),
            prob,
        )
        gate_grad, up_grad, weighted, prob_term = (
            jnp.where(first, value, 0.0) for value in (gate_grad, up_grad, weighted, prob_term)
        )
        grad_prob = jnp.sum(prob_term, axis=1, keepdims=True)
        x_side = gate_grad + pltpu.roll(up_grad, units, 1)
        g_side = pltpu.roll(weighted, 2 * units, 1)
        both = jnp.concatenate(
            [x_side.reshape(block_chunks, HALF, columns), g_side.reshape(block_chunks, HALF, columns)],
            axis=1,
        )
        both = both.reshape(block_rows, columns).astype(BF)
        dx = dot(x_side.astype(BF), wide_ref[...])
        for j in range(4):
            term = dot(both[:, j * UNIT_BLOCK : (j + 1) * UNIT_BLOCK], rows_ref[at, :], TN)
            add_to(terms[j] if single else sum_ref.at[j], term[:used], single)
        return dx, grad_prob

    if single:
        dx, grad_prob = block(0)
        write_rows(own_ref, dx[: half_rows // 2], grad_prob[: half_rows // 2])
        write_rows(send_ref, dx[half_rows // 2 :], grad_prob[half_rows // 2 :])
    else:
        sum_ref[...] = jnp.zeros_like(sum_ref)
        for out_ref, offset in ((own_ref, 0), (send_ref, chunk_count * HCAP // 2)):

            def step(index, carry, out_ref=out_ref, offset=offset):
                dx, grad_prob = block(pl.multiple_of(offset + index * block_rows, 16))
                at = pl.ds(pl.multiple_of(index * half_rows, 16), half_rows)
                write_rows(out_ref.at[at], dx, grad_prob)
                return carry

            lax.fori_loop(0, chunk_count // block_chunks // 2, step, 0)
        for j, out_ref in enumerate(terms):
            out_ref[...] = sum_ref[j].astype(out_ref.dtype)


def cold_kernel(message_count, *refs):
    messages = refs[:message_count]
    mine_x_ref, other_x_ref, gate_ref, up_ref, down_ref = refs[message_count : message_count + 5]
    own_ref, send_ref, *outs = refs[message_count + 5 : message_count + 10]
    data_ref, dx_ref, grad_ref, sum_ref, out_sem = refs[message_count + 10 :]
    total, width = data_ref.shape[0], gate_ref.shape[2]
    rows = COLD_ROWS
    single = rows == total
    stores = [
        pltpu.make_async_copy(grad_ref.at[j], ref.at[0], out_sem.at[j]) for j, ref in enumerate(outs)
    ]
    quarter = total // 4
    z_count = message_count // 2
    for flip, away_ref in enumerate((mine_x_ref, other_x_ref)):
        near = [
            ref[:COLD_PART, :].astype(F32)[: 2 * CAP]
            for ref in messages[flip * z_count :][:z_count]
        ]
        start = 2 * flip * quarter
        data_ref[start : start + quarter, :] = jnp.concatenate(near, axis=0).astype(BF)
        data_ref[start + quarter : start + 2 * quarter, :] = away_ref[...]
    if not single:
        sum_ref[...] = jnp.zeros_like(sum_ref)

    def block(start):
        at = pl.ds(start, rows)
        data = data_ref[at, :width]
        first = jnp.where((iota((8, TAIL), 0) == 0) & (iota((8, TAIL), 1) == 0), 1.0, 0.0)
        prob = dot(first.astype(BF), data_ref[at, width:], NT)[0:1, :]
        pre_gate = dot(gate_ref[0], data, NT)
        pre_up = dot(up_ref[0], data, NT)
        back = pltpu.roll(dot(down_ref[0], data, NT), rows - CAP, 1)
        gate_grad, up_grad, weighted, prob_term = swiglu_back(pre_gate, pre_up, back, prob)
        x_lane = (iota(pre_gate.shape, 1) & 4) == 0
        gate_grad = jnp.where(x_lane, gate_grad, 0.0)
        up_grad = jnp.where(x_lane, up_grad, 0.0)
        weighted = pltpu.roll(jnp.where(x_lane, weighted, 0.0), CAP, 1)
        grad_prob = jnp.sum(jnp.where(x_lane, prob_term, 0.0), axis=0, keepdims=True)
        for j, grad in enumerate((gate_grad, up_grad, weighted)):
            term = dot(grad.astype(BF), data)
            if single:
                grad_ref[j] = term.astype(BF)
                stores[j].start()
            else:
                sum_ref[j] += term
        shape = (rows, rows // 2)
        row, col = iota(shape, 0), iota(shape, 1)
        pick = jnp.where(row == (col >> 2) * 8 + (col & 3), 1.0, 0.0).astype(BF)
        dx = dot(dot(gate_grad.astype(BF), pick).astype(BF), gate_ref[0], TN)
        dx = dx + dot(dot(up_grad.astype(BF), pick).astype(BF), up_ref[0], TN)
        shape = (rows // 2, rows)
        row, col = iota(shape, 0), iota(shape, 1)
        pick = jnp.where(col == (row >> 2) * 8 + (row & 3), 1.0, 0.0).astype(BF)
        high = grad_prob.astype(BF).astype(F32)
        row = iota((8, rows), 0)
        both = jnp.where(row == 0, high, jnp.where(row == 1, grad_prob - high, 0.0))
        both = dot(pick, both.astype(BF), NT)
        grad_prob = both[:, 0:1] + both[:, 1:2]
        half_at = pl.ds(start // 2 if single else pl.multiple_of(start // 2, 16), rows // 2)
        write_rows(dx_ref.at[half_at], dx, grad_prob)

    each_block(total, rows, block)
    own_ref[...] = dx_ref[: total // 4, :]
    dx_rows, dx_prob = read_rows(dx_ref[total // 4 :, :])
    write_rows(send_ref, dx_rows, dx_prob)
    if not single:
        for j in range(3):
            grad_ref[j] = sum_ref[j].astype(BF)
            stores[j].start()
    for store in stores:
        store.wait()


def add_kernel(hot_own_ref, hot_got_ref, cold_own_ref, cold_got_ref, *outs):
    def added(own_ref, got_ref):
        rows, prob = read_rows(own_ref[...])
        got_rows, got_prob = read_rows(got_ref[...])
        return jnp.concatenate([rows + got_rows, tail_lanes(prob + got_prob)], axis=1)

    hot = added(hot_own_ref, hot_got_ref)
    cold = added(cold_own_ref, cold_got_ref)
    half = cold.shape[0] // 2
    width = cold.shape[1] - TAIL
    for k, out_ref in enumerate(outs):
        at = k // 2 * 2 * CAP
        near, far = cold[at : at + 2 * CAP], cold[half + at : half + at + 2 * CAP]
        low = (iota(near.shape, 0) & 4) == 0
        if k % 2:
            part = jnp.where(low, pltpu.roll(near, CAP, 0), far)
        else:
            part = jnp.where(low, near, pltpu.roll(far, CAP, 0))
        rows = jnp.concatenate([hot[k * HALF : (k + 1) * HALF], part], axis=0)
        write_rows(out_ref, rows[:, :width], rows[:, width : width + 1])


def combine_kernel(*refs):
    *parts, own_ref, send_y_ref, send_x_ref = refs
    hot, cold = 0.0, []
    for ref in parts:
        rows, prob = read_rows(ref[...])
        both = jnp.concatenate([rows, tail_lanes(prob)], axis=1)
        hot = hot + both[:HALF]
        cold.append(both[HALF:])
    low = (iota(cold[0].shape, 0) & 4) == 0
    mine, other = [], []
    for even, odd in zip(cold[0::2], cold[1::2]):
        mine.append(jnp.where(low, even, pltpu.roll(odd, CAP, 0)))
        other.append(jnp.where(low, pltpu.roll(even, CAP, 0), odd))
    rows = jnp.concatenate([hot] + mine, axis=0)
    away = jnp.concatenate(other, axis=0)
    width = rows.shape[1] - TAIL
    own_ref[...] = rows
    write_rows(send_y_ref, rows[:, :width], rows[:, width : width + 1])
    write_rows(send_x_ref, away[:, :width], away[:, width : width + 1])


def finish_kernel(base, own_ref, y_ref, x_ref, xy_ref, pos_ref, dx_ref, prob_ref):
    pair = lax.axis_index("pair")
    me = lax.axis_index("dp")
    z, x = me // 4, (me // 2) % 2
    half = dx_ref.shape[0]
    pos = jnp.where(pair == 0, pos_ref[:, :half], pos_ref[:, half:])

    def cold_target(row, side):
        return (2 * (z ^ (row >> 2)) + side) * CAP + (row & 3)

    def with_hot(side):
        row = iota((own_ref.shape[0], half), 0)
        return jnp.where(row < HALF, base + HALF * side + row, cold_target(row - HALF, x))

    away = cold_target(iota((x_ref.shape[0], half), 0), 1 - x)
    total = 0.0
    grad_prob = [0.0] * TOP
    for ref, target in (
        (own_ref, with_hot(pair)),
        (y_ref, with_hot(1 - pair)),
        (x_ref, away),
        (xy_ref, away),
    ):
        routes = [pos[k : k + 1, :] == target for k in range(TOP)]
        onehot = jnp.where(routes[0] | routes[1], 1.0, 0.0).astype(BF)
        rows, prob = read_rows(ref[...])
        high = rows.astype(BF)
        total = total + dot(onehot, high, TN)
        if ref.dtype == F32:
            total = total + dot(onehot, (rows - high.astype(F32)).astype(BF), TN)
        for k in range(TOP):
            terms = jnp.sum(jnp.where(routes[k], prob, 0.0), axis=0, keepdims=True)
            grad_prob[k] = grad_prob[k] + terms
    dx_ref[...] = total.astype(BF)
    for k in range(TOP):
        prob_ref[k : k + 1, :] = grad_prob[k]


def sum_kernel(own_ref, a_ref, b_ref, c_ref, gate_ref, up_ref, down_ref):
    total = own_ref[...] + a_ref[...].astype(F32) + b_ref[...].astype(F32) + c_ref[...].astype(F32)
    units = gate_ref.shape[0]
    for index, out_ref in enumerate((gate_ref, up_ref, down_ref)):
        out_ref[...] = total[index * units : (index + 1) * units].astype(BF)


def call(kernel, outs, name, scratch=(), smem=(), out_hbm=(), limit=0):
    def run(*args):
        moved = sum(a.size * a.dtype.itemsize for a in args)
        moved += sum(o.size * o.dtype.itemsize for o in outs)
        return pl.pallas_call(
            kernel,
            out_shape=outs,
            in_specs=[
                pl.BlockSpec(memory_space=pltpu.SMEM if i in smem else pltpu.VMEM)
                for i in range(len(args))
            ],
            out_specs=[
                pl.BlockSpec(memory_space=pltpu.HBM if i in out_hbm else pltpu.VMEM)
                for i in range(len(outs))
            ],
            scratch_shapes=[pltpu.VMEM(*s) if isinstance(s, tuple) else s for s in scratch],
            compiler_params=pltpu.CompilerParams(
                vmem_limit_bytes=limit or min(VMEM_LIMIT, VMEM_BASE + 3 * moved // 2)
            ),
            cost_estimate=pl.CostEstimate(flops=1024, bytes_accessed=1024, transcendentals=0),
            name=name,
        )(*args)

    return run


def local(
    tokens,
    grad_out,
    gate_probs,
    expert_ids,
    route_slots,
    hot_flags,
    owner_slot,
    cold_gate,
    cold_up,
    cold_down,
    hot_gate,
    hot_up,
    hot_down,
):
    count = lax.axis_size("dp")
    z_count = count // 4
    chunk_count = 2 * z_count
    token_count, width = tokens.shape
    lanes = width + TAIL
    units = hot_gate.shape[0]
    base = (count // 2) * CAP
    shape = jax.ShapeDtypeStruct
    half = token_count // 2
    pad = -units % 8

    def swap(value, mask):
        flip_dp, flip_pair = 2 * (mask & 1), mask >> 1
        perm = [
            (2 * i + p, 2 * (i ^ flip_dp) + (p ^ flip_pair)) for i in range(count) for p in range(2)
        ]
        return lax.ppermute(value, ("dp", "pair"), perm)

    def along_z(value, k):
        perm = [(i, 4 * ((i // 4) ^ k) + i % 4) for i in range(count)]
        return lax.ppermute(value, "dp", perm)

    def all_along_z(values):
        order = sorted(range(1, z_count), key=lambda k: (k == 1, k))
        got = {k: along_z(values[k], k) for k in order}
        return [values[0]] + [got[k] for k in range(1, z_count)]

    def other_core(value):
        return lax.ppermute(value, "dp", [(i, i ^ 1) for i in range(count)])

    hot_weights = [jnp.pad(w, ((0, pad), (0, 0))) if pad else w for w in (hot_gate, hot_up, hot_down)]
    units_padded = units + pad
    used = 3 * units_padded
    cold_rows = z_count * COLD_PART
    message = shape((MESSAGE, lanes), BF)
    long_message = shape((MESSAGE + COLD_PART, lanes), BF)
    pos, hot_own, *messages = call(
        functools.partial(dispatch_kernel, base),
        [shape((TOP, token_count), jnp.int32), shape((used, width), BF)]
        + [message, message]
        + [long_message] * (z_count // 2 - 1),
        "dispatch",
        scratch=[((HCAP + cold_rows, lanes), BF)],
        smem=(5, 6),
        limit=VMEM_LIMIT,
    )(
        tokens,
        grad_out,
        gate_probs.T,
        expert_ids.T,
        route_slots.T,
        hot_flags,
        owner_slot,
        *hot_weights,
    )

    chunks = [messages[0], along_z(messages[1], 1)]
    for index in range(2, len(messages)):
        direct = along_z(messages[index], 2 * index - 2)
        (onward,) = call(relay_kernel, [message], "relay_rows")(direct)
        chunks += [direct, along_z(onward, 1)]
    first_out, hot_out, _ = lax.optimization_barrier((messages[0], hot_own, chunks[1]))
    first_out, hot_out = call(
        copy_kernel, [message, shape(hot_own.shape, BF)], "own_rows"
    )(first_out, hot_out)
    chunks[0] = first_out
    weights = [hot_out] + [swap(hot_own, mask) for mask in (1, 2, 3)]
    (away,) = call(away_kernel, [shape((cold_rows // 2, lanes), BF)], "cold_away")(*chunks)
    chunks = chunks + [other_core(chunk) for chunk in chunks]
    cold_mine = swap(away, 1)
    cold_other = other_core(cold_mine)

    cold_units = cold_gate.shape[1]
    cold_shape = shape(cold_gate.shape, BF)
    all_rows = chunk_count * HCAP
    half_rows = chunk_count * HALF // 2
    term = shape((used, width), BF)
    hot_dx, hot_dx_out, own_term, *sent_terms = call(
        functools.partial(hot_kernel, chunk_count, units_padded),
        [
            shape((half_rows, lanes), F32),
            shape((half_rows, lanes), BF),
            shape(term.shape, F32),
            term,
            term,
            term,
        ],
        "hot",
        scratch=[
            ((all_rows, width), BF),
            ((all_rows, TAIL), BF),
            ((4 * UNIT_BLOCK, width), BF),
            ((4, used, width) if chunk_count > CHUNK_BLOCK else (8, 128), F32),
        ],
    )(*chunks, *weights)

    cold_mine, hot_dx = lax.optimization_barrier((cold_mine, hot_dx))
    cold_own, cold_out, grad_cold_gate, grad_cold_up, grad_cold_down = call(
        functools.partial(cold_kernel, chunk_count),
        [shape((cold_rows // 2, lanes), F32), shape((cold_rows // 2, lanes), BF)] + [cold_shape] * 3,
        "cold",
        scratch=[
            ((2 * cold_rows, lanes), BF),
            ((cold_rows, lanes), F32),
            ((3, cold_units, width), BF),
            ((3, cold_units, width) if 2 * cold_rows > COLD_ROWS else (8, 128), F32),
            pltpu.SemaphoreType.DMA((3,)),
        ],
        out_hbm=(2, 3, 4),
    )(*chunks, cold_mine, cold_other, cold_gate, cold_up, cold_down)

    hot_got, cold_got = other_core(hot_dx_out), other_core(cold_out)
    part = (HALF + 2 * CAP, lanes)
    parts = call(
        add_kernel, [shape(part, F32)] + [shape(part, BF)] * (z_count - 1), "add_cores"
    )(hot_dx, hot_got, cold_own, cold_got)
    term_x, _ = lax.optimization_barrier((sent_terms[0], cold_mine))
    got_x, got_y = swap(term_x, 1), swap(sent_terms[1], 2)
    *parts, got_x, last_term = lax.optimization_barrier((*parts, got_x, sent_terms[2]))
    parts = all_along_z(parts)
    got_terms = [got_x, got_y, swap(last_term, 3)]

    cold_back = z_count * CAP
    own_rows, send_y, send_x = call(
        combine_kernel,
        [
            shape((HALF + cold_back, lanes), F32),
            shape((HALF + cold_back, lanes), BF),
            shape((cold_back, lanes), BF),
        ],
        "combine",
    )(*parts)
    rows_y, rows_x, rows_xy = swap(send_y, 2), swap(send_x, 1), swap(send_x, 3)
    out_shape = shape((units_padded, width), BF)
    hot_grads = call(sum_kernel, [out_shape] * 3, "hot_sum")(
        own_term, *got_terms
    )
    own_rows, *hot_grads = lax.optimization_barrier((own_rows, *hot_grads))
    dx, prob_t = call(
        functools.partial(finish_kernel, base),
        [shape((half, width), BF), shape((TOP, half), F32)],
        "finish",
    )(own_rows, rows_y, rows_x, rows_xy, pos)

    if pad:
        hot_grads = [value[:units] for value in hot_grads]
    return (dx, prob_t.T, grad_cold_gate, grad_cold_up, grad_cold_down, *hot_grads)


def solution(mesh):
    return jax.shard_map(
        local,
        mesh=mesh,
        in_specs=(
            P("dp", None),
            P("dp", None),
            P("dp", None),
            P("dp", None),
            P("dp", None),
            P(),
            P(),
            P("dp", "pair", None),
            P("dp", "pair", None),
            P("dp", "pair", None),
            P(("dp", "pair"), None),
            P(("dp", "pair"), None),
            P(("dp", "pair"), None),
        ),
        out_specs=(
            P(("dp", "pair"), None),
            P(("dp", "pair"), None),
            P("dp", "pair", None),
            P("dp", "pair", None),
            P("dp", "pair", None),
            P(("dp", "pair"), None),
            P(("dp", "pair"), None),
            P(("dp", "pair"), None),
        ),
        check_vma=False,
    )
```
